32 devices in a mesh: dp: 8 (over z, x), tensor: 4 (over y, core).
Axes of the slice: x: 2, y: 2, z: 4, core: 2. Of those that a mesh axis runs over, the one named last changes fastest.
Arguments:
- block_input: bfloat16 [16, 1024, 1536], P('dp', 'tensor'), may hold values from -6 to 6
- out_grad: bfloat16 [16, 1024, 1536], P('dp', 'tensor'), may hold values from -6 to 6
- seg_lengths: int32 [16, 4], P('dp'), may hold values from 1 to 1020, as said below
- norm1_gain: bfloat16 [1536], replicated, may hold values from 0.5 to 1.5
- norm2_gain: bfloat16 [1536], replicated, may hold values from 0.5 to 1.5
- rel_bias: bfloat16 [32, 12], replicated, may hold values from -3 to 3
- w_query: bfloat16 [1536, 768], P(None, 'tensor'), may hold values from -0.078125 to 0.078125
- w_key: bfloat16 [1536, 768], P(None, 'tensor'), may hold values from -0.078125 to 0.078125
- w_value: bfloat16 [1536, 768], P(None, 'tensor'), may hold values from -0.15625 to 0.15625
- w_out: bfloat16 [768, 1536], P('tensor'), may hold values from -0.75 to 0.75
- w_gate: bfloat16 [1536, 3968], P(None, 'tensor'), may hold values from -0.15625 to 0.15625
- w_up: bfloat16 [1536, 3968], P(None, 'tensor'), may hold values from -0.15625 to 0.15625
- w_down: bfloat16 [3968, 1536], P('tensor'), may hold values from -0.09375 to 0.09375
Outputs:
- block_out: float32 [16, 1024, 1536], P('dp', 'tensor')
- input_grad: float32 [16, 1024, 1536], P('dp', 'tensor')
- norm1_grad: float32 [1536], replicated
- norm2_grad: float32 [1536], replicated
- bias_grad: float32 [32, 12], replicated
- query_grad: float32 [1536, 768], P('dp', 'tensor')
- key_grad: float32 [1536, 768], P('dp', 'tensor')
- value_grad: float32 [1536, 768], P('dp', 'tensor')
- outproj_grad: float32 [768, 1536], P('tensor', 'dp')
- gate_grad: float32 [1536, 3968], P('dp', 'tensor')
- up_grad: float32 [1536, 3968], P('dp', 'tensor')
- down_grad: float32 [3968, 1536], P('tensor', 'dp')
The draws below stay inside these ranges and needn't reach their ends.
Inputs may be any that keep to these rules, and one draw needn't show every extreme that they name: `seg_lengths`: each row's 4 lengths add up to less than 1024; the remaining positions of the row are padding. In every row one segment covers more than three quarters of the row. In some row of every draw the longest segment has exactly 1020 positions.
All inputs are finite; a program needn't handle non-finite values.
Results may differ from the reference program's by a relative error of at most 0.014.
The reference program's roundings to bfloat16 on the way count: a program that leaves them out, or rounds other values in their place, can miss the bound.
Values may be sent and summed in bfloat16 or wider, within the bound.
No kernel may reach another device: no remote copies, remote signals or barrier semaphores. Data moves between devices by JAX's collectives and lax.ppermute only.
A program may use at most 256 MiB of HBM per device.

```python
import jax
import jax.numpy as jnp
from jax import lax

D = 1536
H = 12
DK = 64
FF = 3968
BUCKETS = 32
LEN = 1024
SEGS = 4
ROWS = 16
BLOCK = 512


def draw_seg_lengths(key, part):
    key = jax.random.fold_in(key, 7)
    key_short, key_padding, key_choice, key_fullrow = jax.random.split(key, 4)
    shorter = jax.random.randint(key_short, (ROWS, SEGS), 1, LEN // 32 + 1)
    shorter = shorter - jnp.min(shorter) + 1
    padding = jax.random.randint(key_padding, (ROWS, 1), 1, LEN // 16 + 1)
    fullest = jax.random.randint(key_fullrow, (), 0, ROWS)
    fullest_row = jnp.arange(ROWS, dtype=jnp.int32)[:, None] == fullest
    shorter = jnp.where(fullest_row, 1, shorter)
    padding = jnp.where(fullest_row, 1, padding)
    chosen = jax.random.randint(key_choice, (ROWS, 1), 0, SEGS)
    chosen_slot = jnp.arange(SEGS, dtype=jnp.int32)[None, :] == chosen
    others = jnp.sum(jnp.where(chosen_slot, 0, shorter), axis=1, keepdims=True)
    longest = LEN - padding - others
    return jnp.where(chosen_slot, longest, shorter).astype(jnp.int32)


def with_spikes(values, stream_key, source, target, blocks, factor):
    owner, partner = [(jnp.arange(values.shape[axis_at]) // (values.shape[axis_at] // blocks)).reshape([-1 if axis == axis_at else 1 for axis in range(values.ndim)]) for axis_at in (source, target)]
    chosen = jax.random.permutation(stream_key, blocks)[partner]
    strong = (owner == chosen) | (owner == (partner + blocks // 2) % blocks)
    return jnp.where(strong, factor * values, values)


def block_levels(key, dims, shards, smallest, top_value):
    def one(dim, shards_of):
        draws = jax.random.uniform(jax.random.fold_in(jax.random.fold_in(key, 6), dim), (shards_of,), jnp.float32, smallest / len(shards), top_value / len(shards))
        return jnp.repeat(jnp.exp(draws), dims[dim] // shards_of).reshape((-1,) + (1,) * (len(dims) - dim - 1))

    level = one(*shards[0])
    for cut in shards[1:]:
        level = level * one(*cut)
    return level


def noise(own_key, dims, width, bound, shards=(), kind=jnp.bfloat16):
    values = jax.random.normal(own_key, dims, jnp.float32) * width
    if len(shards) > 0:
        values = block_levels(own_key, dims, shards, -0.22, 0.18) * values
    return jnp.clip(values, min=-bound, max=bound).astype(kind)


def heavy_noise(stream_key, shape, spread, most, cuts, heavy, kind=jnp.bfloat16):
    values = spread * jax.random.normal(stream_key, shape, jnp.float32)
    if cuts:
        values = values * block_levels(stream_key, shape, cuts, -0.22, 0.18)
    return jnp.clip(with_spikes(values, jax.random.fold_in(stream_key, 3), *heavy), -most, most).astype(kind)


def setup_inputs(seed: int = 0) -> dict:
    key_list = jax.random.split(jax.random.key(seed), 14)
    block_input = heavy_noise(key_list[0], (ROWS, LEN, D), 1.0, 6.0, ((0, 8), (1, 4)), (0, 2, 8, 2.0))
    out_grad = heavy_noise(key_list[1], (ROWS, LEN, D), 1.0, 6.0, ((0, 8), (1, 4)), (0, 2, 8, 2.0))
    seg_lengths = draw_seg_lengths(jax.random.fold_in(key_list[13], 71), 0)
    norm1_gain = jnp.clip(1.0 + 0.1 * jax.random.normal(key_list[3], (D,), jnp.float32), 0.5, 1.5).astype(jnp.bfloat16)
    norm2_gain = jnp.clip(1.0 + 0.1 * jax.random.normal(key_list[4], (D,), jnp.float32), 0.5, 1.5).astype(jnp.bfloat16)
    rel_bias = noise(key_list[5], (BUCKETS, H), 0.5, 3.0)
    w_query = noise(key_list[6], (D, H * DK), (4 * D) ** -0.5, 0.078125, ((1, 4),))
    w_key = noise(key_list[7], (D, H * DK), (4 * D) ** -0.5, 0.078125, ((1, 4),))
    w_value = noise(key_list[8], (D, H * DK), D ** -0.5, 0.15625, ((1, 4),))
    w_out = noise(key_list[9], (H * DK, D), DK ** -0.5, 0.75, ((0, 4),))
    w_gate = noise(key_list[10], (D, FF), D ** -0.5, 0.15625, ((1, 4),))
    w_up = noise(key_list[11], (D, FF), D ** -0.5, 0.15625, ((1, 4),))
    w_down = noise(key_list[12], (FF, D), FF ** -0.5, 0.09375, ((0, 4),))
    return {"block_input": block_input, "out_grad": out_grad, "seg_lengths": seg_lengths, "norm1_gain": norm1_gain, "norm2_gain": norm2_gain, "rel_bias": rel_bias, "w_query": w_query, "w_key": w_key, "w_value": w_value, "w_out": w_out, "w_gate": w_gate, "w_up": w_up, "w_down": w_down}


@jax.custom_vjp
def low(v):
    return lax.optimization_barrier(v.astype(jnp.bfloat16)).astype(jnp.float32)

@jax.custom_vjp
def low_back(v):
    return v

def low_keep(v):
    return (low(v), None)

def low_pass(kept, grad):
    return (grad,)

def back_keep(v):
    return (v, None)

def back_low(kept, grad):
    return (low(grad),)
low.defvjp(low_keep, low_pass)
low_back.defvjp(back_keep, back_low)
bucket_edges = (12, 16, 23, 32, 46, 64, 91)
masked_score = -1000000000.0
epsilon = 1e-06
highest_precision = lax.Precision.HIGHEST

def norm_rows(rows, gain):
    factor = lax.rsqrt(lax.optimization_barrier(jnp.mean(rows * rows, axis=-1, keepdims=True)) + epsilon)
    return rows * factor * gain

def gated_unit(gate_rows, up_rows):
    return jax.nn.gelu(gate_rows, approximate=True) * up_rows

def bucket_table(start, count, length, buckets):
    query_pos = start + jnp.arange(count, dtype=jnp.int32)
    key_pos = jnp.arange(length, dtype=jnp.int32)
    offset = key_pos[None, :] - query_pos[:, None]
    magnitude = jnp.abs(offset)
    larger = sum(((magnitude >= edge).astype(jnp.int32) for edge in bucket_edges))
    exact = buckets // 4
    inside = jnp.where(magnitude < exact, magnitude, exact + larger)
    return (inside + jnp.where(offset > 0, buckets // 2, 0)).astype(jnp.int32)

def segment_ids(lengths, length):
    ends = jnp.cumsum(lengths.astype(jnp.int32))
    positions = jnp.arange(length, dtype=jnp.int32)
    return lax.optimization_barrier(jnp.sum((positions[:, None] >= ends[None, :]).astype(jnp.int32), axis=1))

def product(left, right):
    return jnp.dot(left, right, precision=highest_precision, preferred_element_type=jnp.float32)

def layer_row(row_inputs, row_lengths, params):
    gain_one, gain_two, bias_table, w_query, w_key, w_value, w_out, w_gate, w_up, w_down = params
    normed_one = low(norm_rows(row_inputs, gain_one))
    queries = low_back(low(product(normed_one, w_query))).reshape(LEN, H, DK)
    key_rows = low_back(low(product(normed_one, w_key))).reshape(LEN, H, DK)
    value_rows = low_back(low(product(normed_one, w_value))).reshape(LEN, H, DK)
    segids = segment_ids(row_lengths, LEN)

    def attend(start):
        query_block = lax.dynamic_slice_in_dim(queries, start, BLOCK, 0)
        seg_block = lax.dynamic_slice_in_dim(segids, start, BLOCK, 0)
        bucket_rows = bucket_table(start, BLOCK, LEN, BUCKETS)
        bias_block = jnp.transpose(bias_table[bucket_rows], (2, 0, 1))
        raw = jnp.einsum('qhd,khd->hqk', query_block, key_rows, precision=highest_precision) + bias_block
        scores = low_back(raw)
        same = (seg_block[:, None] == segids[None, :])[None]
        probs = low(jax.nn.softmax(jnp.where(same, scores, masked_score), axis=-1))
        return jnp.einsum('hqk,khd->qhd', probs, value_rows, precision=highest_precision)
    starts = jnp.arange(LEN // BLOCK, dtype=jnp.int32) * BLOCK
    attended = lax.map(jax.checkpoint(attend), starts).reshape(LEN, H * DK)
    attended = low_back(low(attended))
    branch = low_back(product(attended, w_out))
    middle = row_inputs + branch
    normed_two = low(norm_rows(middle, gain_two))
    gate_rows = low_back(product(normed_two, w_gate))
    up_rows = low_back(product(normed_two, w_up))
    hidden = low(gated_unit(gate_rows, up_rows))
    feed_out = low_back(product(hidden, w_down))
    return middle + feed_out

def reference(block_input, out_grad, seg_lengths, norm1_gain, norm2_gain, rel_bias, w_query, w_key, w_value, w_out, w_gate, w_up, w_down):
    params = tuple((item.astype(jnp.float32) for item in (norm1_gain, norm2_gain, rel_bias, w_query, w_key, w_value, w_out, w_gate, w_up, w_down)))
    inputs = block_input.astype(jnp.float32)

    def forward(rows_in, *weights):
        return lax.map(lambda pair: layer_row(pair[0], pair[1], weights), (rows_in, seg_lengths))
    result, pullback = jax.vjp(forward, inputs, *params)
    grads = pullback(out_grad.astype(jnp.float32))
    return (result, grads[0], grads[1], grads[2], grads[3], grads[4], grads[5], grads[6], grads[7], grads[8], grads[9], grads[10])
```

```python
import functools

import jax
import jax.numpy as jnp
import numpy as np
from jax import lax
from jax.experimental import pallas as pl
from jax.experimental.pallas import tpu as pltpu
from jax.sharding import PartitionSpec as P

DK = 64
QUERY_BLOCK = 256
REACH = 128
LANES = 64
MIB = 2**20

bucket_edges = (12, 16, 23, 32, 46, 64, 91)
masked_score = -1000000000.0
epsilon = 1e-06
gelu_scale = float(np.sqrt(2 / np.pi))
gelu_cubic = 0.044715
bf16 = jnp.bfloat16
f32 = jnp.float32

across_y = ((0, 2), (2, 0), (1, 3), (3, 1))
across_core = ((0, 1), (1, 0), (2, 3), (3, 2))
across_both = ((0, 3), (3, 0), (1, 2), (2, 1))


def dot_nn(left, right):
    return lax.dot_general(left, right, (((1,), (0,)), ((), ())), preferred_element_type=f32)


def dot_nt(left, right):
    return lax.dot_general(left, right, (((1,), (1,)), ((), ())), preferred_element_type=f32)


def dot_tn(left, right):
    return lax.dot_general(left, right, (((0,), (0,)), ((), ())), preferred_element_type=f32)


def over_y(array):
    return lax.ppermute(array, "tensor", across_y)


def over_core(array):
    return lax.ppermute(array, "tensor", across_core)


def over_both(array):
    return lax.ppermute(array, "tensor", across_both)


smem = pl.BlockSpec(memory_space=pltpu.SMEM)
vmem = pl.BlockSpec(memory_space=pltpu.VMEM)
anywhere = pl.BlockSpec(memory_space=pl.ANY)


def row_of(row, shape):
    return pl.BlockSpec((1,) + shape[1:], lambda *_: (row, 0, 0))


class Order:
    def __init__(self):
        self.last = []

    def after(self, *arrays):
        self.last = self.last + list(arrays)

    def call(self, kernel, name, inputs, in_specs, outputs, room, scratch=(), out_specs=None, grid=(1,), aliases=None):
        count, extra = len(inputs), len(self.last)

        def body(*refs):
            kernel(*refs[:count], *refs[count + extra :])

        results = pl.pallas_call(
            body,
            grid=grid,
            in_specs=list(in_specs) + [anywhere] * extra,
            out_specs=out_specs or [vmem] * len(outputs),
            out_shape=[jax.ShapeDtypeStruct(shape, kind) for shape, kind in outputs],
            scratch_shapes=scratch,
            input_output_aliases=aliases or {},
            compiler_params=pltpu.CompilerParams(vmem_limit_bytes=room * MIB),
            cost_estimate=pl.CostEstimate(flops=10**13, bytes_accessed=1024, transcendentals=0),
            name=name,
        )(*inputs, *self.last)
        self.last = [results[0]]
        return results


def norm_factor(rows):
    return lax.rsqrt(jnp.mean(rows * rows, axis=-1, keepdims=True) + epsilon)


def norm_backward(dnormed, rows, gain):
    factor = norm_factor(rows)
    scaled = dnormed * gain
    return factor * (scaled - rows * factor * factor * jnp.mean(scaled * rows, axis=-1, keepdims=True))


def project_kernel(own, other_y, other_core, other_both, gain, weight_t, normed, qkv):
    count = own.shape[1]
    for index, piece in enumerate((own[0], other_y[...], other_core[0], other_both[...])):
        rows = piece.astype(f32)
        result = (rows * norm_factor(rows) * gain[...]).astype(bf16)
        at = slice(index * count, (index + 1) * count)
        normed[at, :] = result
        qkv[at, :] = dot_nt(result, weight_t[...]).astype(bf16)


def project(order, row, pieces, gain, weight_t):
    own, other_y, other_core, other_both = pieces
    count, width = other_y.shape
    return order.call(
        project_kernel,
        "normed_projections",
        (own, other_y, other_core, other_both, gain, weight_t),
        [row_of(row, own.shape), vmem, row_of(row, other_core.shape), vmem, vmem, vmem],
        [((4 * count, width), bf16), ((4 * count, weight_t.shape[0]), bf16)],
        28,
    )


def bucket_of(offset, buckets):
    magnitude = jnp.abs(offset)
    larger = sum(((magnitude >= edge).astype(jnp.int32) for edge in bucket_edges))
    exact = buckets // 4
    inside = jnp.where(magnitude < exact, magnitude, exact + larger)
    return inside + jnp.where(offset > 0, buckets // 2, 0)


def band_buckets(buckets):
    key = jnp.arange(QUERY_BLOCK + 2 * REACH, dtype=jnp.int32) - REACH
    query = jnp.arange(QUERY_BLOCK, dtype=jnp.int32)
    return bucket_of(key[:, None] - query[None, :], buckets)


def bias_parts(bias, length):
    buckets = bias.shape[0]
    index = band_buckets(buckets)
    wide = bias.astype(f32)
    band = jnp.zeros((bias.shape[1],) + index.shape, f32)
    for bucket in range(buckets):
        band = jnp.where((index == bucket)[None], wide[bucket][:, None, None], band)
    key = jnp.arange(length, dtype=jnp.int32)[:, None]
    block = jnp.arange(LANES, dtype=jnp.int32)[None]
    used = block < length // QUERY_BLOCK
    before = (key < block * QUERY_BLOCK - REACH) & used
    after = (key >= (block + 1) * QUERY_BLOCK + REACH) & used
    far_before = bias[buckets // 2 - 1][:, None, None]
    far_after = bias[buckets - 1][:, None, None]
    far = jnp.where(before[None], far_before, jnp.where(after[None], far_after, jnp.zeros((), bias.dtype)))
    return band, far


def near_keys(block, length):
    low = max(0, block * QUERY_BLOCK - REACH)
    high = min(length, (block + 1) * QUERY_BLOCK + REACH)
    return low, high, low - (block * QUERY_BLOCK - REACH)


def segment_of(position, lengths, row):
    end = jnp.int32(0)
    segment = jnp.zeros(position.shape, jnp.int32)
    for part in range(lengths.shape[1]):
        end = end + lengths[row, part]
        segment = segment + (position >= end).astype(jnp.int32)
    return segment


def fill_masks(lengths, row, masks):
    blocks, length, width = masks.shape
    key_segment = segment_of(lax.broadcasted_iota(jnp.int32, (length, width), 0), lengths, row)
    for block in range(blocks):
        at = lax.broadcasted_iota(jnp.int32, (1, width), 1) + block * width
        masks[block] = jnp.where(key_segment == segment_of(at, lengths, row), 0.0, masked_score)


def relative_block(place, block):
    along_y = jnp.bitwise_xor(place[0], block // 2)
    along_core = jnp.bitwise_xor(place[1], block % 2)
    return along_y + 2 * along_core


def rows_at(index):
    return pl.ds(pl.multiple_of(index * QUERY_BLOCK, QUERY_BLOCK), QUERY_BLOCK)


def block_scores(key_wide, query_wide, mask, band, head, block):
    length = key_wide.shape[0]
    scores = dot_nt(key_wide, query_wide) + mask
    low, high, start = near_keys(block, length)
    parts = []
    if low > 0:
        parts.append(scores[:low])
    parts.append(scores[low:high] + band[head, start : start + high - low])
    if high < length:
        parts.append(scores[high:])
    return jnp.concatenate(parts, axis=0)


def block_indicator(block):
    lane = lax.broadcasted_iota(jnp.int32, (QUERY_BLOCK, LANES), 1)
    return jnp.where(lane == block, 1.0, 0.0).astype(bf16)


def attention_forward_kernel(
    row, place, lengths, qkv, band, far, attended_keep, attended_send, logsum, masks, keys, values, attended
):
    length = qkv.shape[0]
    width = qkv.shape[1] // 3
    fill_masks(lengths, row, masks)
    blocks = length // QUERY_BLOCK
    order = [relative_block(place, block) for block in range(blocks)]
    for block in range(blocks):
        at = slice(block * QUERY_BLOCK, (block + 1) * QUERY_BLOCK)
        keys[at, :] = qkv[rows_at(order[block]), width : 2 * width]
        values[at, :] = qkv[rows_at(order[block]), 2 * width :]
    for head in range(width // DK):
        cols = slice(head * DK, (head + 1) * DK)
        key_wide = jnp.concatenate([keys[:, cols], far[head]], axis=1)
        values_t = values[:, cols].T
        for block in range(blocks):
            query_wide = jnp.concatenate([qkv[rows_at(order[block]), cols], block_indicator(block)], axis=1)
            scores = block_scores(key_wide, query_wide, masks[block], band, head, block)
            peak = jnp.max(scores, axis=0, keepdims=True)
            expo = jnp.exp(scores - peak)
            total = jnp.sum(expo, axis=0, keepdims=True)
            probs_low = (expo * (1.0 / total)).astype(bf16)
            logsum[head : head + 1, block * QUERY_BLOCK : (block + 1) * QUERY_BLOCK] = peak + jnp.log(total)
            result = dot_nn(values_t, probs_low).T.astype(bf16)
            attended[rows_at(order[block]), cols] = result
    attended_keep[...] = attended[: length // 2, :]
    attended_send[...] = attended[length // 2 :, :]


def attention_forward(order, row, place, lengths, qkv, band, far):
    length, width = qkv.shape[0], qkv.shape[1] // 3
    return order.call(
        functools.partial(attention_forward_kernel, row),
        "attention_forward",
        (place, lengths, qkv, band, far),
        [smem, smem, vmem, vmem, vmem],
        [((length // 2, width), bf16), ((length // 2, width), bf16), ((8, length), f32)],
        36,
        scratch=[
            pltpu.VMEM((length // QUERY_BLOCK, length, QUERY_BLOCK), f32),
            pltpu.VMEM((length, width), bf16),
            pltpu.VMEM((length, width), bf16),
            pltpu.VMEM((length, width), bf16),
        ],
    )


def attention_backward_kernel(
    row, place, lengths, qkv, dout_own, dout_y, dout_core, logsum, band, far, weight_t, normed,
    band_before, far_before, dqkv, dnormed_keep, dnormed_send, band_grad, far_grad, gain_sum,
    masks, keys, values, douts,
):
    length = qkv.shape[0]
    width = qkv.shape[1] // 3
    fill_masks(lengths, row, masks)
    blocks = length // QUERY_BLOCK
    order = [relative_block(place, block) for block in range(blocks)]
    for block, piece in enumerate((dout_own[...], dout_y[0], dout_core[0], dout_core[1])):
        at = slice(block * QUERY_BLOCK, (block + 1) * QUERY_BLOCK)
        keys[at, :] = qkv[rows_at(order[block]), width : 2 * width]
        values[at, :] = qkv[rows_at(order[block]), 2 * width :]
        douts[at, :] = piece
    band_grad[...] = band_before[...]
    far_grad[...] = far_before[...]
    key_at = lax.broadcasted_iota(jnp.int32, (length, LANES), 0)
    block_at = lax.broadcasted_iota(jnp.int32, (length, LANES), 1)
    before = key_at < block_at * QUERY_BLOCK - REACH
    after = key_at >= (block_at + 1) * QUERY_BLOCK + REACH
    for head in range(width // DK):
        cols = slice(head * DK, (head + 1) * DK)
        key_head = keys[:, cols]
        key_wide = jnp.concatenate([key_head, far[head]], axis=1)
        key_t = key_head.T
        value_head = values[:, cols]
        dkey_wide = None
        dvalue = None
        for block in range(blocks):
            query_wide = jnp.concatenate([qkv[rows_at(order[block]), cols], block_indicator(block)], axis=1)
            dout = douts[rows_at(order[block]), cols]
            scores = block_scores(key_wide, query_wide, masks[block], band, head, block)
            probs = jnp.exp(scores - logsum[head : head + 1, block * QUERY_BLOCK : (block + 1) * QUERY_BLOCK])
            weighted = probs * dot_nt(value_head, dout)
            inner = jnp.sum(weighted, axis=0, keepdims=True)
            dscores = (weighted - probs * inner).astype(bf16)
            dvalue_part = dot_nn(probs.astype(bf16), dout)
            dkey_part = dot_nn(dscores, query_wide)
            dvalue = dvalue_part if dvalue is None else dvalue + dvalue_part
            dkey_wide = dkey_part if dkey_wide is None else dkey_wide + dkey_part
            dqkv[rows_at(order[block]), cols] = dot_nn(key_t, dscores).T.astype(bf16)
            low, high, start = near_keys(block, length)
            band_grad[head, start : start + high - low] += dscores[low:high].astype(f32)
        for block in range(blocks):
            at = slice(block * QUERY_BLOCK, (block + 1) * QUERY_BLOCK)
            key_cols = slice(width + head * DK, width + (head + 1) * DK)
            value_cols = slice(2 * width + head * DK, 2 * width + (head + 1) * DK)
            dqkv[rows_at(order[block]), key_cols] = dkey_wide[at, :DK].astype(bf16)
            dqkv[rows_at(order[block]), value_cols] = dvalue[at].astype(bf16)
        sums = dkey_wide[:, DK:]
        far_grad[head : head + 1, :] += jnp.concatenate(
            [
                jnp.sum(jnp.where(before, sums, 0.0), axis=0, keepdims=True),
                jnp.sum(jnp.where(after, sums, 0.0), axis=0, keepdims=True),
            ],
            axis=1,
        )
    total = jnp.zeros((1, normed.shape[1]), f32)
    for half, target in enumerate((dnormed_keep, dnormed_send)):
        for part in range(2):
            at = slice((2 * half + part) * QUERY_BLOCK, (2 * half + part + 1) * QUERY_BLOCK)
            dnormed = dot_nn(dqkv[at, :], weight_t[...])
            target[part * QUERY_BLOCK : (part + 1) * QUERY_BLOCK, :] = dnormed.astype(bf16)
            total = total + jnp.sum(dnormed * normed[at, :].astype(f32), axis=0, keepdims=True)
    gain_sum[...] = total


def attention_backward(order, row, place, lengths, qkv, douts, logsum, band, far, weight_t, normed, band_before, far_before):
    length, width = qkv.shape[0], qkv.shape[1] // 3
    half = ((length // 2, normed.shape[1]), bf16)
    return order.call(
        functools.partial(attention_backward_kernel, row),
        "attention_backward",
        (place, lengths, qkv, *douts, logsum, band, far, weight_t, normed, band_before, far_before),
        [smem, smem] + [vmem] * 11,
        [(qkv.shape, bf16), half, half, (band.shape, f32), ((8, 2 * LANES), f32), ((1, normed.shape[1]), f32)],
        48,
        scratch=[
            pltpu.VMEM((length // QUERY_BLOCK, length, QUERY_BLOCK), f32),
            pltpu.VMEM((length, width), bf16),
            pltpu.VMEM((length, width), bf16),
            pltpu.VMEM((length, width), bf16),
        ],
    )


def branch_kernel(heads_0, heads_1, heads_2, heads_3, out_0, out_1, out_2, out_3, own, other_y, gain, middle, normed):
    count = own.shape[1]
    for index, piece in enumerate((own[0], other_y[...])):
        here = slice(index * count, (index + 1) * count)
        there = slice((1 - index) * count, (2 - index) * count)
        branch = (
            dot_nn(heads_0[here, :], out_0[...])
            + dot_nn(heads_1[here, :], out_1[...])
            + dot_nn(heads_2[there, :], out_2[...])
            + dot_nn(heads_3[there, :], out_3[...])
        )
        rows = piece.astype(f32) + branch
        if index == 0:
            middle[...] = rows
        normed[here, :] = (rows * norm_factor(rows) * gain[...]).astype(bf16)


def attention_branch(order, row, heads, out_parts, own, other_y, gain):
    count, width = other_y.shape
    return order.call(
        branch_kernel,
        "attention_branch",
        (*heads, *out_parts, own, other_y, gain),
        [vmem] * 8 + [row_of(row, own.shape), vmem, vmem],
        [((count, width), f32), ((2 * count, width), bf16)],
        28,
    )


def branch_backward_kernel(
    keep, received, from_y, middle, out_grad, gain, out_0, out_1, out_2, out_3,
    dmiddle, dbranch, gain_sum, douts_own, douts_core, douts_y,
):
    dnormed = summed(keep, received, from_y)
    rows = middle[...]
    result = out_grad[0].astype(f32) + norm_backward(dnormed, rows, gain[...])
    dmiddle[...] = result
    low = result.astype(bf16)
    dbranch[...] = low
    gain_sum[...] = jnp.sum(dnormed * rows * norm_factor(rows), axis=0, keepdims=True)
    douts_own[...] = dot_nt(low, out_0[...]).astype(bf16)
    douts_core[...] = dot_nt(low, out_1[...]).astype(bf16)
    douts_y[0] = dot_nt(low, out_2[...]).astype(bf16)
    douts_y[1] = dot_nt(low, out_3[...]).astype(bf16)


def branch_backward(order, row, keep, received, from_y, middle, out_grad, gain, out_parts):
    count, width = middle.shape
    first = pl.BlockSpec((count, width), lambda *_: (0, 0))
    return order.call(
        branch_backward_kernel,
        "branch_backward",
        (keep, received, from_y, middle, out_grad, gain, *out_parts),
        [first, pl.BlockSpec((1, count, width), lambda *_: (0, 0, 0)), vmem, vmem, row_of(row, out_grad.shape)]
        + [vmem] * 5,
        [((count, width), f32), ((count, width), bf16), ((1, width), f32)]
        + [((count, out_parts[0].shape[0]), bf16)] * 2
        + [((2, count, out_parts[0].shape[0]), bf16)],
        24,
    )


def outproj_grad_kernel(rows, *refs):
    heads, branches, (keep, send) = refs[: 4 * rows], refs[4 * rows : 5 * rows], refs[5 * rows :]
    count = branches[0].shape[0]
    for index in range(4):
        total = None
        for row in range(rows):
            at = slice((index // 2) * count, (index // 2 + 1) * count)
            part = dot_tn(heads[4 * row + index][at, :], branches[row][...])
            total = part if total is None else total + part
        target = keep if index % 2 == 0 else send
        target[index // 2] = total.astype(bf16)


def outproj_grad(order, heads, branches):
    rows, width, cols = len(branches), branches[0].shape[1], heads[0].shape[1]
    return order.call(
        functools.partial(outproj_grad_kernel, rows),
        "outproj_gradient",
        (*heads, *branches),
        [vmem] * (5 * rows),
        [((2, cols, width), bf16)] * 2,
        24,
    )


def load_once(sources, targets, sem):
    @pl.when(pl.program_id(0) == 0)
    def _():
        copies = [
            pltpu.make_async_copy(source, target, sem.at[index])
            for index, (source, target) in enumerate(zip(sources, targets))
        ]
        for copy in copies:
            copy.start()
        for copy in copies:
            copy.wait()


def feed_kernel(
    chunk, normed_keep, normed_recv, grad_0, grad_1, grad_2, grad_3, gate_hbm, up_hbm, down_hbm,
    hidden_ref, dgate_ref, dup_ref, dnormed_keep, feed_keep, sends, gate_t, up_t, down, sem,
):
    step = pl.program_id(0)
    load_once((gate_hbm, up_hbm, down_hbm), (gate_t, up_t, down), sem)
    normed = jnp.where(step < 2, normed_keep[...], normed_recv[...])
    grad = jnp.where(
        step < 2,
        jnp.where(step == 0, grad_0[0], grad_1[...]),
        jnp.where(step == 2, grad_2[0], grad_3[...]),
    )
    units = down.shape[0]
    for start in range(0, units, chunk):
        at = slice(start, min(units, start + chunk))
        gate = dot_nt(normed, gate_t[at, :])
        up = dot_nt(normed, up_t[at, :])
        dhidden = dot_nt(grad, down[at, :])
        square = gate * gate
        bend = jnp.tanh(gelu_scale * gate * (1.0 + gelu_cubic * square))
        half = 0.5 * (1.0 + bend)
        active = gate * half
        slope = half + (0.5 * gelu_scale) * gate * (1.0 - bend * bend) * (1.0 + (3 * gelu_cubic) * square)
        hidden_ref[:, at] = (active * up).astype(bf16)
        dup_ref[:, at] = (dhidden * active).astype(bf16)
        dgate_ref[:, at] = (dhidden * up * slope).astype(bf16)
    dnormed = (dot_nn(dgate_ref[...], gate_t[...]) + dot_nn(dup_ref[...], up_t[...])).astype(bf16)
    feed = dot_nn(hidden_ref[...], down[...]).astype(bf16)

    @pl.when(step < 2)
    def _():
        dnormed_keep[...] = dnormed
        feed_keep[...] = feed

    @pl.when(step >= 2)
    def _():
        sends[0] = dnormed
        sends[1] = feed


def feed_forward(order, row, normed_keep, normed_recv, grads, gate_t, up_t, down):
    units, width = down.shape
    length = 2 * normed_keep.shape[0]
    count = length // 4
    first = pl.BlockSpec((count, width), lambda step: (jnp.minimum(step, 1), 0))
    last = pl.BlockSpec((count, width), lambda step: (jnp.maximum(step - 2, 0), 0))
    pair = pl.BlockSpec((2, count, width), lambda step: (0, jnp.maximum(step - 2, 0), 0))
    each = pl.BlockSpec((count, units), lambda step: (step, 0))
    half = ((length // 2, width), bf16)
    return order.call(
        functools.partial(feed_kernel, 256),
        "feed_forward",
        (normed_keep, normed_recv, *grads, gate_t, up_t, down),
        [first, last, row_of(row, grads[0].shape), vmem, row_of(row, grads[2].shape), vmem] + [anywhere] * 3,
        [((length, units), bf16)] * 3 + [half, half, ((2, length // 2, width), bf16)],
        44,
        out_specs=[each] * 3 + [first, first, pair],
        grid=(4,),
        scratch=[pltpu.VMEM((units, width), bf16)] * 3 + [pltpu.SemaphoreType.DMA((3,))],
    )


def halves(parts, stride, bit):
    count, rows, width = parts.shape
    pairs = parts.reshape(count // (2 * stride), 2, stride, rows, width)
    low, high = pairs[:, 0], pairs[:, 1]
    shape = (count // 2, rows, width)
    return jnp.where(bit == 0, low, high).reshape(shape), jnp.where(bit == 0, high, low).reshape(shape)


def gradient_kernel(groups, bit, extra, place, *refs):
    rows = len(groups)
    extras, refs = refs[:extra], refs[extra:]
    lefts, refs = refs[: sum(map(len, groups))], refs[sum(map(len, groups)) :]
    rights_hbm, (kept_ref, sent_ref, left, right, left_sem, right_sem) = refs[:rows], refs[rows:]
    step, steps = pl.program_id(0), pl.num_programs(0)
    length, tile = left.shape[2], left.shape[3]

    def left_copies(row, at_step):
        taken = sum(map(len, groups[:row]))
        copies = []
        at = 0
        for index, lead in enumerate(groups[row]):
            source = lefts[taken + index]
            source = source if lead is None else source.at[lead]
            count = source.shape[0]
            cols = pl.ds(pl.multiple_of(at_step * tile, tile), tile)
            slot = lax.rem(at_step, 2)
            copies.append(
                pltpu.make_async_copy(
                    source.at[:, cols], left.at[slot, row, pl.ds(at, count)], left_sem.at[slot, taken + index]
                )
            )
            at += count
        return copies

    def right_copy(row):
        return pltpu.make_async_copy(rights_hbm[row], right.at[row], right_sem.at[row])

    @pl.when(step == 0)
    def _():
        for row in range(rows):
            for copy in left_copies(row, 0):
                copy.start()
            right_copy(row).start()

    @pl.when(step + 1 < steps)
    def _():
        for row in range(rows):
            for copy in left_copies(row, step + 1):
                copy.start()

    total = None
    for row in range(rows):
        for copy in left_copies(row, step):
            copy.wait()
        pl.when(step == 0)(right_copy(row).wait)
        part = dot_tn(left[lax.rem(step, 2), row], right[row])
        total = part if total is None else total + part
    if extra:
        added = sum(ref[0].astype(f32) for ref in extras)
        total = jnp.concatenate([total, added.T], axis=1)
    parts = total.reshape(-1, kept_ref.shape[1], kept_ref.shape[2])
    kept, sent = halves(parts, 1 << bit, place[2 + bit])
    kept_ref[...] = kept.astype(bf16)
    sent_ref[...] = sent.astype(bf16)


def gradient(order, name, place, lefts, rights, bit, extras=()):
    size = lax.axis_size("dp")
    length, cols = rights[0].shape
    width = lefts[0][0][0].shape[-1]
    tile = width // 2
    chunk_rows = width // size
    pieces = [piece for group in lefts for piece in group]
    rows = len(rights)
    all_cols = cols + (extras[0].shape[1] if extras else 0)
    return order.call(
        functools.partial(gradient_kernel, [[lead for _, lead in group] for group in lefts], bit, len(extras)),
        name,
        (place, *extras, *[array for array, _ in pieces], *rights),
        [smem]
        + [pl.BlockSpec((1, extra.shape[1], tile), lambda step: (0, 0, step)) for extra in extras]
        + [anywhere] * (len(pieces) + rows),
        [((size // 2, chunk_rows, all_cols), bf16)] * 2,
        40,
        out_specs=[pl.BlockSpec((size // 4, chunk_rows, all_cols), lambda step: (step, 0, 0))] * 2,
        grid=(2,),
        scratch=[
            pltpu.VMEM((2, rows, length, tile), bf16),
            pltpu.VMEM((rows, length, cols), bf16),
            pltpu.SemaphoreType.DMA((2, len(pieces))),
            pltpu.SemaphoreType.DMA((rows,)),
        ],
    )


def exchange(sent, bit):
    return lax.ppermute(sent, "dp", [(i, i ^ (1 << bit)) for i in range(lax.axis_size("dp"))])


def halve_kernel(stride, bit, place, kept, received, keep_ref, send_ref):
    parts = kept[...].astype(f32) + received[...].astype(f32)
    keep, send = halves(parts, stride, place[2 + bit])
    keep_ref[...] = keep.astype(bf16)
    send_ref[...] = send.astype(bf16)


class Scatter:
    def __init__(self, order, place, first, parts, finish):
        self.order, self.place, self.finish = order, place, finish
        count = lax.axis_size("dp").bit_length() - 1
        self.bits = list(range(first, count)) + list(range(first))
        self.left = sorted(self.bits)
        self.send(*parts)

    def send(self, kept, sent):
        bit = self.bits.pop(0)
        self.left.remove(bit)
        self.parts = kept, exchange(sent, bit)

    def step(self):
        kept, received = self.parts
        if not self.bits:
            return self.finish(self.order, kept, received)
        bit = self.bits[0]
        stride = 1 << self.left.index(bit)
        shape = (kept.shape[0] // 2,) + kept.shape[1:]
        self.send(
            *self.order.call(
                functools.partial(halve_kernel, stride, bit),
                "halve",
                (self.place, kept, received),
                [smem] + [vmem] * 2,
                [(shape, bf16)] * 2,
                12,
            )
        )

    def run(self):
        result = None
        while result is None:
            result = self.step()
        return result


def joined_kernel(kept, received, out):
    out[...] = kept[0].astype(f32) + received[0].astype(f32)


def finish_joined(order, kept, received):
    return order.call(joined_kernel, "gradient_output", (kept, received), [vmem] * 2, [(kept.shape[1:], f32)], 8)[0]


def projections_kernel(kept, received, query, key, value, out):
    total = kept[0].astype(f32) + received[0].astype(f32)
    cols = total.shape[1] // 4
    for index, target in enumerate((query, key, value)):
        target[...] = total[:, index * cols : (index + 1) * cols]
    out[...] = total[:, 3 * cols :].T


def finish_projections(order, kept, received):
    rows, cols = kept.shape[1], kept.shape[2] // 4
    return order.call(
        projections_kernel,
        "projection_outputs",
        (kept, received),
        [vmem] * 2,
        [((rows, cols), f32)] * 3 + [((cols, rows), f32)],
        8,
    )


def pass_kernel(*refs):
    for keep, received, out in zip(refs[0::2], refs[1::2], refs[-(len(refs) // 3) :]):
        out[...] = (keep[...].reshape(out.shape).astype(f32) + received[...].reshape(out.shape).astype(f32)).astype(bf16)


def pass_on(order, keep, received, lead=None):
    count, width = keep.shape[0] // 2, keep.shape[1]
    second = pl.BlockSpec((count, width), lambda *_: (1, 0))
    other = second if lead is None else pl.BlockSpec((1, count, width), lambda *_: (lead, 1, 0))
    return over_y(
        order.call(pass_kernel, "pass_on", (keep, received), [second, other], [((count, width), bf16)], 8)[0]
    )


def pass_rows_kernel(*refs):
    out = refs[-1]
    for row in range(out.shape[0]):
        out[row] = (refs[2 * row][...].astype(f32) + refs[2 * row + 1][0].astype(f32)).astype(bf16)


def pass_rows(order, parts, lead):
    count, width = parts[0][0].shape[0] // 2, parts[0][0].shape[1]
    second = pl.BlockSpec((count, width), lambda *_: (1, 0))
    other = pl.BlockSpec((1, count, width), lambda *_: (lead, 1, 0))
    return over_y(
        order.call(
            pass_rows_kernel,
            "pass_on",
            [array for pair in parts for array in pair],
            [second, other] * len(parts),
            [((len(parts), count, width), bf16)],
            12,
        )[0]
    )


def outproj_pass(order, keep, received):
    shape = keep.shape[1:]
    second = pl.BlockSpec((1,) + shape, lambda *_: (1, 0, 0))
    return over_y(order.call(pass_kernel, "pass_on", (keep, received), [second] * 2, [((1,) + shape, bf16)], 8)[0])


def relay_kernel(source, target):
    target[...] = source[0] if len(source.shape) == 3 else source[...]


def relay(order, array, row=None):
    shape = array.shape if row is None else array.shape[1:]
    spec = vmem if row is None else row_of(row, array.shape)
    return order.call(relay_kernel, "relay", (array,), [spec], [(shape, array.dtype)], 8)[0]


def summed(keep, received, from_y):
    shape = keep.shape
    return sum(ref[...].reshape(shape).astype(f32) for ref in (keep, received, from_y))


def block_out_kernel(middle, keep, received, from_y, _, out):
    out[0] = middle[...] + summed(keep, received, from_y)


def input_grad_kernel(dmiddle, keep, received, from_y, inputs, gain, _, out):
    dnormed = summed(keep, received, from_y)
    out[0] = dmiddle[...] + norm_backward(dnormed, inputs[0].astype(f32), gain[...])


def place_row(order, kernel, name, row, before, summed, inputs, in_specs, lead=None):
    keep, received, from_y = summed
    count, width = from_y.shape[-2:]
    first = pl.BlockSpec((count, width), lambda *_: (0, 0))
    pair = first if len(received.shape) == 2 else pl.BlockSpec((1, count, width), lambda *_: (lead, 0, 0))
    arrived = vmem if len(from_y.shape) == 2 else row_of(row, from_y.shape)
    specs = [vmem, first, pair, arrived] + in_specs + [anywhere]
    return order.call(
        kernel,
        name,
        (inputs[0], keep, received, from_y, *inputs[1:], before),
        specs,
        [(before.shape, f32)],
        16,
        out_specs=[row_of(row, before.shape)],
        aliases={len(specs) - 1: 0},
    )[0]


def add_kernel(*refs):
    refs[-1][...] = sum(ref[...] for ref in refs[:-1])


def add_all(order, arrays):
    return order.call(add_kernel, "small_sum", arrays, [vmem] * len(arrays), [(arrays[0].shape, f32)], 4)[0]


def small_rounds(order, vector):
    count = lax.axis_size("dp").bit_length() - 1
    moved = [over_core(vector), over_y(vector), over_both(vector)]
    yield None
    vector = add_all(order, [vector, *moved])
    for low in range(0, count, 2):
        masks = [mask << low for mask in (1, 2, 3) if mask << low < 1 << count]
        moved = [lax.ppermute(vector, "dp", [(i, i ^ mask) for i in range(1 << count)]) for mask in masks]
        yield None
        vector = add_all(order, [vector, *moved])
    yield vector


def per_device(
    block_input,
    out_grad,
    seg_lengths,
    norm1_gain,
    norm2_gain,
    rel_bias,
    w_query,
    w_key,
    w_value,
    w_out,
    w_gate,
    w_up,
    w_down,
):
    rows, count, width = block_input.shape
    length = 4 * count
    here = lax.axis_index("tensor")
    dp_bits = lax.axis_size("dp").bit_length() - 1
    dp_at = lax.axis_index("dp")
    place = jnp.stack([here // 2, here % 2] + [(dp_at >> bit) & 1 for bit in range(dp_bits)]).astype(jnp.int32)
    head_width = w_query.shape[1]
    heads = head_width // DK
    buckets = rel_bias.shape[0]
    gain_one = norm1_gain.astype(f32)[None]
    gain_two = norm2_gain.astype(f32)[None]
    first_head = here * heads
    weight_t = jnp.concatenate([w_query.T, w_key.T, w_value.T], axis=0)
    gate_t, up_t = w_gate.T, w_up.T

    order = Order()
    every_row = range(rows)
    last_row = rows - 1

    band, far = bias_parts(lax.dynamic_slice_in_dim(rel_bias, first_head, heads, 1), length)
    order.after(band, far, weight_t)
    input_y = [over_y(block_input[0])]
    input_core = over_core(block_input)
    grad_core = over_core(out_grad)
    out_core = over_core(w_out)
    order.after(grad_core, out_core)
    for row in range(1, rows):
        order.after(input_y[-1])
        input_y.append(over_y(relay(order, block_input, row)))

    normed_one, qkvs, logsums, attended, middles = [], [], [], [], []
    grad_y, grad_both = [], []
    normed_keeps, normed_recvs = [], []

    def second_norm(row):
        middle, normed_keep = attention_branch(
            order, row, attended[row], out_parts, block_input, input_y[row], gain_two
        )
        middles.append(middle)
        normed_keeps.append(normed_keep)
        normed_recvs.append(over_core(normed_keep))

    for row in every_row:
        normed, qkv = project(
            order, row, (block_input, input_y[row], input_core, over_core(input_y[row])), gain_one, weight_t
        )
        if row == 0:
            out_y = over_y(relay(order, w_out))
        keep, send, logsum = attention_forward(order, row, place, seg_lengths, qkv, band, far)
        other = over_core(send)
        normed_one.append(normed)
        qkvs.append(qkv)
        logsums.append(logsum)
        attended.append([keep, other, over_y(keep), over_y(other)])
        if row == 0:
            order.after(out_y)
            out_both = over_core(out_y)
            out_parts = [w_out, out_core, out_y, out_both]
        else:
            second_norm(row - 1)
        if row < last_row:
            order.after(input_y[row + 1])
        order.after(other)
        if grad_y:
            order.after(grad_y[-1])
        grad_y.append(over_y(relay(order, out_grad, row)))
        if row > 0:
            grad_both.append(over_core(grad_y[row - 1]))

    hiddens, dgates, dups, dnormed, feeds = [], [], [], [], []

    def feed(row):
        hidden, dgate, dup, dn_keep, ff_keep, sends = feed_forward(
            order,
            row,
            normed_keeps[row],
            normed_recvs[row],
            (out_grad, grad_y[row], grad_core, grad_both[row]),
            gate_t,
            up_t,
            w_down,
        )
        hiddens.append(hidden)
        dgates.append(dgate)
        dups.append(dup)
        received = over_core(sends)
        dnormed.append([dn_keep, received])
        feeds.append([ff_keep, received])

    feed(0)
    second_norm(last_row)
    grad_both.append(over_core(relay(order, grad_y[last_row])))
    dnormed[0].append(pass_on(order, *dnormed[0], lead=0))
    for row in range(1, rows):
        feed(row)
    grad_pieces = [[(out_grad, r), (grad_y[r], None), (grad_core, r), (grad_both[r], None)] for r in every_row]
    normed_pieces = [[(normed_keeps[r], None), (normed_recvs[r], None)] for r in every_row]
    down_scatter = Scatter(
        order, place, 0, gradient(order, "down_gradient", place, grad_pieces, hiddens, 0), finish_joined
    )
    for row in range(1, rows):
        dnormed[row].append(pass_on(order, *dnormed[row], lead=0))

    band_grad = jnp.zeros(band.shape, f32)
    far_grad = jnp.zeros((8, 2 * LANES), f32)
    dmiddles, dbranches, dqkvs, norm1_sums, norm2_sums, inner = [], [], [], [], [], []
    for row in every_row:
        if row > 0:
            order.after(feeds_y)
        dmiddle, dbranch, norm2_sum, dout_own, dout_core, dout_y = branch_backward(
            order, row, *dnormed[row], middles[row], out_grad, gain_two, out_parts
        )
        dmiddles.append(dmiddle)
        dbranches.append(dbranch)
        norm2_sums.append(norm2_sum)
        dout_y = over_y(dout_y)
        if row == 0:
            gate_scatter = Scatter(
                order, place, 1, gradient(order, "gate_gradient", place, normed_pieces, dgates, 1), finish_joined
            )
        else:
            down_scatter.step()
            gate_scatter.step()
        order.after(dout_y)
        dout_core = over_core(jnp.stack([dout_core, dout_y[1]]))
        if row == 0:
            up_scatter = Scatter(
                order, place, 0, gradient(order, "up_gradient", place, normed_pieces, dups, 0), finish_joined
            )
            down_scatter.step()
            feeds_y = pass_rows(order, feeds, 1)
        else:
            inner[0].append(pass_on(order, *inner[0]))
            out_keep, out_send = outproj_grad(order, [part for group in attended for part in group], dbranches)
            out_recv = over_core(out_send)
        dqkv, dn_keep, dn_send, band_grad, far_grad, norm1_sum = attention_backward(
            order, row, place, seg_lengths, qkvs[row], (dout_own, dout_y, dout_core), logsums[row], band, far,
            weight_t, normed_one[row], band_grad, far_grad,
        )
        norm1_sums.append(norm1_sum)
        dqkvs.append(dqkv)
        inner.append([dn_keep, over_core(dn_send)])
    out_from_y = outproj_pass(order, out_keep, out_recv)
    up_scatter.step()
    for row in range(1, rows):
        inner[row].append(pass_on(order, *inner[row]))
    qkv_scatter = Scatter(
        order,
        place,
        0,
        gradient(
            order,
            "projection_gradient",
            place,
            [[(normed_one[r], None)] for r in every_row],
            dqkvs,
            0,
            (out_keep, out_recv, out_from_y),
        ),
        finish_projections,
    )
    down_out = down_scatter.run()
    block_out = jnp.zeros((rows, count, width), f32)
    input_grad = jnp.zeros((rows, count, width), f32)
    for row in every_row:
        block_out = place_row(
            order, block_out_kernel, "block_output", row, block_out, (*feeds[row], feeds_y), (middles[row],), [], 1
        )
    gate_out = gate_scatter.run()
    up_scatter.step()

    norm1_sum = sum(norm1_sums)[0] / gain_one[0]
    norm2_sum = sum(norm2_sums)[0]
    index = band_buckets(buckets)
    bucket_sum = jnp.einsum(
        "bkp,hkp->bh",
        (index[None] == jnp.arange(buckets, dtype=jnp.int32)[:, None, None]).astype(bf16),
        band_grad.astype(bf16),
        preferred_element_type=f32,
    )
    far_sums = jnp.sum(far_grad[:heads].reshape(heads, 2, LANES), axis=2)
    bucket_sum = bucket_sum.at[buckets // 2 - 1].add(far_sums[:, 0]).at[buckets - 1].add(far_sums[:, 1])
    bias_sum = lax.dynamic_update_slice(jnp.zeros(rel_bias.shape, f32), bucket_sum, (0, first_head))
    small = jnp.concatenate([norm1_sum, norm2_sum, bias_sum.reshape(-1)])[None]
    small = relay(order, small)
    rounds = small_rounds(order, small)
    small = next(rounds)
    qkv_scatter.step()
    small = next(rounds)
    for row in range(rows):
        input_grad = place_row(
            order,
            input_grad_kernel,
            "input_gradient",
            row,
            input_grad,
            inner[row],
            (dmiddles[row], block_input, gain_one),
            [row_of(row, block_input.shape), vmem],
        )
    up_out = up_scatter.run()
    qkv_scatter.step()
    while small is None:
        small = next(rounds)
    small = small[0]
    query_out, key_out, value_out, outproj_out = qkv_scatter.run()

    return (
        block_out,
        input_grad,
        small[:width],
        small[width : 2 * width],
        small[2 * width :].reshape(rel_bias.shape),
        query_out,
        key_out,
        value_out,
        outproj_out,
        gate_out,
        up_out,
        down_out.T,
    )


def solution(mesh):
    in_specs = (
        P("dp", "tensor", None),
        P("dp", "tensor", None),
        P("dp", None),
        P(),
        P(),
        P(),
        P(None, "tensor"),
        P(None, "tensor"),
        P(None, "tensor"),
        P("tensor", None),
        P(None, "tensor"),
        P(None, "tensor"),
        P("tensor", None),
    )
    out_specs = (
        P("dp", "tensor", None),
        P("dp", "tensor", None),
        P(),
        P(),
        P(),
        P("dp", "tensor"),
        P("dp", "tensor"),
        P("dp", "tensor"),
        P("tensor", "dp"),
        P("dp", "tensor"),
        P("dp", "tensor"),
        P("tensor", "dp"),
    )
    return jax.shard_map(
        per_device, mesh=mesh, in_specs=in_specs, out_specs=out_specs, check_vma=False
    )
```

```python
import functools

import jax
import jax.numpy as jnp
import numpy as np
from jax import lax
from jax.experimental import pallas as pl
from jax.experimental.pallas import tpu as pltpu
from jax.sharding import PartitionSpec as P

DK = 64
QUERY_BLOCK = 256
REACH = 128
LANES = 64
MIB = 2**20

bucket_edges = (12, 16, 23, 32, 46, 64, 91)
masked_score = -1000000000.0
epsilon = 1e-06
gelu_scale = float(np.sqrt(2 / np.pi))
gelu_cubic = 0.044715
bf16 = jnp.bfloat16
f32 = jnp.float32

across_y = ((0, 2), (2, 0), (1, 3), (3, 1))
across_core = ((0, 1), (1, 0), (2, 3), (3, 2))
across_both = ((0, 3), (3, 0), (1, 2), (2, 1))


def dot_nn(left, right):
    return lax.dot_general(left, right, (((1,), (0,)), ((), ())), preferred_element_type=f32)


def dot_nt(left, right):
    return lax.dot_general(left, right, (((1,), (1,)), ((), ())), preferred_element_type=f32)


def dot_tn(left, right):
    return lax.dot_general(left, right, (((0,), (0,)), ((), ())), preferred_element_type=f32)


def over_y(array):
    return lax.ppermute(array, "tensor", across_y)


def over_core(array):
    return lax.ppermute(array, "tensor", across_core)


def over_both(array):
    return lax.ppermute(array, "tensor", across_both)


smem = pl.BlockSpec(memory_space=pltpu.SMEM)
vmem = pl.BlockSpec(memory_space=pltpu.VMEM)
anywhere = pl.BlockSpec(memory_space=pl.ANY)


def piece_of(array, lead):
    return vmem if lead is None else row_of(lead, array.shape)


def row_of(row, shape):
    return pl.BlockSpec((1,) + shape[1:], lambda *_: (row, 0, 0))


def placed(shape, kind, space=None):
    return jax.ShapeDtypeStruct(shape, kind) if space is None else space(shape, kind)


class Order:
    def __init__(self):
        self.last = []

    def after(self, *arrays):
        self.last = self.last + list(arrays)

    def call(self, kernel, name, inputs, in_specs, outputs, room, scratch=(), out_specs=None, grid=(1,), aliases=None):
        count, extra = len(inputs), len(self.last)

        def body(*refs):
            kernel(*refs[:count], *refs[count + extra :])

        results = pl.pallas_call(
            body,
            grid=grid,
            in_specs=list(in_specs) + [anywhere] * extra,
            out_specs=out_specs or [vmem] * len(outputs),
            out_shape=[placed(*output) for output in outputs],
            scratch_shapes=scratch,
            input_output_aliases=aliases or {},
            compiler_params=pltpu.CompilerParams(vmem_limit_bytes=room * MIB),
            cost_estimate=pl.CostEstimate(flops=10**13, bytes_accessed=1024, transcendentals=0),
            name=name,
        )(*inputs, *self.last)
        self.last = [results[0]]
        return results


def norm_factor(rows):
    return lax.rsqrt(jnp.mean(rows * rows, axis=-1, keepdims=True) + epsilon)


def norm_backward(dnormed, rows, gain):
    factor = norm_factor(rows)
    scaled = dnormed * gain
    return factor * (scaled - rows * factor * factor * jnp.mean(scaled * rows, axis=-1, keepdims=True))


def project_kernel(own, other_y, other_core, other_both, gain, weight_t, normed, qkv, normed_t):
    count = own.shape[1]
    for index, piece in enumerate((own, other_y, other_core, other_both)):
        rows = piece[...].reshape(own.shape[1:]).astype(f32)
        result = (rows * norm_factor(rows) * gain[...]).astype(bf16)
        at = slice(index * count, (index + 1) * count)
        normed[at, :] = result
        qkv[at, :] = dot_nt(result, weight_t[...]).astype(bf16)
        normed_t[:, at] = result.T


def project(order, pieces, gain, weight_t):
    count, width = pieces[0][0].shape[1:]
    return order.call(
        project_kernel,
        "normed_projections",
        (*[array for array, _ in pieces], gain, weight_t),
        [piece_of(*piece) for piece in pieces] + [vmem, vmem],
        [((4 * count, width), bf16), ((4 * count, weight_t.shape[0]), bf16), ((width, 4 * count), bf16)],
        36,
    )


def bucket_of(offset, buckets):
    magnitude = jnp.abs(offset)
    larger = sum(((magnitude >= edge).astype(jnp.int32) for edge in bucket_edges))
    exact = buckets // 4
    inside = jnp.where(magnitude < exact, magnitude, exact + larger)
    return inside + jnp.where(offset > 0, buckets // 2, 0)


def band_buckets(buckets):
    key = jnp.arange(QUERY_BLOCK + 2 * REACH, dtype=jnp.int32) - REACH
    query = jnp.arange(QUERY_BLOCK, dtype=jnp.int32)
    return bucket_of(key[:, None] - query[None, :], buckets)


def bias_parts(bias, length):
    buckets = bias.shape[0]
    index = band_buckets(buckets)
    wide = bias.astype(f32)
    band = jnp.zeros((bias.shape[1],) + index.shape, f32)
    for bucket in range(buckets):
        band = jnp.where((index == bucket)[None], wide[bucket][:, None, None], band)
    key = jnp.arange(length, dtype=jnp.int32)[:, None]
    block = jnp.arange(LANES, dtype=jnp.int32)[None]
    used = block < length // QUERY_BLOCK
    before = (key < block * QUERY_BLOCK - REACH) & used
    after = (key >= (block + 1) * QUERY_BLOCK + REACH) & used
    far_before = bias[buckets // 2 - 1][:, None, None]
    far_after = bias[buckets - 1][:, None, None]
    far = jnp.where(before[None], far_before, jnp.where(after[None], far_after, jnp.zeros((), bias.dtype)))
    return band, far


def near_keys(block, length):
    low = max(0, block * QUERY_BLOCK - REACH)
    high = min(length, (block + 1) * QUERY_BLOCK + REACH)
    return low, high, low - (block * QUERY_BLOCK - REACH)


def segment_of(position, lengths, row):
    end = jnp.int32(0)
    segment = jnp.zeros(position.shape, jnp.int32)
    for part in range(lengths.shape[1]):
        end = end + lengths[row, part]
        segment = segment + (position >= end).astype(jnp.int32)
    return segment


def fill_masks(lengths, row, masks):
    blocks, length, width = masks.shape
    key_segment = segment_of(lax.broadcasted_iota(jnp.int32, (length, width), 0), lengths, row)
    for block in range(blocks):
        at = lax.broadcasted_iota(jnp.int32, (1, width), 1) + block * width
        masks[block] = jnp.where(key_segment == segment_of(at, lengths, row), 0.0, masked_score)


def relative_block(place, block):
    along_y = jnp.bitwise_xor(place[0], block // 2)
    along_core = jnp.bitwise_xor(place[1], block % 2)
    return along_y + 2 * along_core


def rows_at(index):
    return pl.ds(pl.multiple_of(index * QUERY_BLOCK, QUERY_BLOCK), QUERY_BLOCK)


def block_scores(key_wide, query_wide, mask, band, head, block):
    length = key_wide.shape[0]
    scores = dot_nt(key_wide, query_wide) + mask
    low, high, start = near_keys(block, length)
    parts = []
    if low > 0:
        parts.append(scores[:low])
    parts.append(scores[low:high] + band[head, start : start + high - low])
    if high < length:
        parts.append(scores[high:])
    return jnp.concatenate(parts, axis=0)


def block_indicator(block):
    lane = lax.broadcasted_iota(jnp.int32, (QUERY_BLOCK, LANES), 1)
    return jnp.where(lane == block, 1.0, 0.0).astype(bf16)


def attention_forward_kernel(
    row, place, lengths, qkv, band, far, attended_keep, attended_send, logsum, masks, keys, values, attended
):
    length = qkv.shape[0]
    width = qkv.shape[1] // 3
    fill_masks(lengths, row, masks)
    blocks = length // QUERY_BLOCK
    order = [relative_block(place, block) for block in range(blocks)]
    for block in range(blocks):
        at = slice(block * QUERY_BLOCK, (block + 1) * QUERY_BLOCK)
        keys[at, :] = qkv[rows_at(order[block]), width : 2 * width]
        values[at, :] = qkv[rows_at(order[block]), 2 * width :]
    for head in range(width // DK):
        cols = slice(head * DK, (head + 1) * DK)
        key_wide = jnp.concatenate([keys[:, cols], far[head]], axis=1)
        for block in range(blocks):
            query_wide = jnp.concatenate([qkv[rows_at(order[block]), cols], block_indicator(block)], axis=1)
            scores = block_scores(key_wide, query_wide, masks[block], band, head, block)
            peak = jnp.max(scores, axis=0, keepdims=True)
            expo = jnp.exp(scores - peak)
            total = jnp.sum(expo, axis=0, keepdims=True)
            probs_low = (expo * (1.0 / total)).astype(bf16)
            logsum[head : head + 1, block * QUERY_BLOCK : (block + 1) * QUERY_BLOCK] = peak + jnp.log(total)
            result = dot_tn(probs_low, values[:, cols]).astype(bf16)
            attended[rows_at(order[block]), cols] = result
    attended_keep[...] = attended[: length // 2, :]
    attended_send[...] = attended[length // 2 :, :]


def attention_forward(order, row, place, lengths, qkv, band, far):
    length, width = qkv.shape[0], qkv.shape[1] // 3
    return order.call(
        functools.partial(attention_forward_kernel, row),
        "attention_forward",
        (place, lengths, qkv, band, far),
        [smem, smem, vmem, vmem, vmem],
        [((length // 2, width), bf16), ((length // 2, width), bf16), ((8, length), f32)],
        36,
        scratch=[
            pltpu.VMEM((length // QUERY_BLOCK, length, QUERY_BLOCK), f32),
            pltpu.VMEM((length, width), bf16),
            pltpu.VMEM((length, width), bf16),
            pltpu.VMEM((length, width), bf16),
        ],
    )


def attention_backward_kernel(
    row, place, lengths, qkv, dout_own, dout_y, dout_core, logsum, band, far, weight_t, normed,
    dqkv, dnormed_keep, dnormed_send, band_grad, far_grad, gain_sum,
    masks, keys, values, douts, queries_wide, probs_low, dscores,
):
    length = qkv.shape[0]
    width = qkv.shape[1] // 3
    fill_masks(lengths, row, masks)
    blocks = length // QUERY_BLOCK
    order = [relative_block(place, block) for block in range(blocks)]
    for block, piece in enumerate((dout_own[...], dout_y[0], dout_core[0], dout_core[1])):
        at = slice(block * QUERY_BLOCK, (block + 1) * QUERY_BLOCK)
        keys[at, :] = qkv[rows_at(order[block]), width : 2 * width]
        values[at, :] = qkv[rows_at(order[block]), 2 * width :]
        true_block = 2 * jnp.bitwise_xor(place[0], block % 2) + jnp.bitwise_xor(place[1], block // 2)
        douts[rows_at(true_block), :] = piece
    band_grad[...] = jnp.zeros_like(band_grad)
    far_grad[...] = jnp.zeros_like(far_grad)
    key_at = lax.broadcasted_iota(jnp.int32, (length, LANES), 0)
    block_at = lax.broadcasted_iota(jnp.int32, (length, LANES), 1)
    before = key_at < block_at * QUERY_BLOCK - REACH
    after = key_at >= (block_at + 1) * QUERY_BLOCK + REACH
    for head in range(width // DK):
        cols = slice(head * DK, (head + 1) * DK)
        slot = head % 2
        key_head = keys[:, cols]
        key_wide = jnp.concatenate([key_head, far[head]], axis=1)
        value_head = values[:, cols]
        for block in range(blocks):
            at = slice(block * QUERY_BLOCK, (block + 1) * QUERY_BLOCK)
            query_wide = jnp.concatenate([qkv[rows_at(order[block]), cols], block_indicator(block)], axis=1)
            queries_wide[slot, at, :] = query_wide
            scores = block_scores(key_wide, query_wide, masks[block], band, head, block)
            probs = jnp.exp(scores - logsum[head : head + 1, at])
            weighted = probs * dot_nt(value_head, douts[at, cols])
            inner = jnp.sum(weighted, axis=0, keepdims=True)
            low_dscores = (weighted - probs * inner).astype(bf16)
            probs_low[slot, :, at] = probs.astype(bf16)
            dscores[slot, :, at] = low_dscores
            low, high, start = near_keys(block, length)
            band_grad[head, start : start + high - low] += low_dscores[low:high].astype(f32)
        dvalue = dot_nn(probs_low[slot], douts[:, cols])
        dkey_wide = dot_nn(dscores[slot], queries_wide[slot])
        dquery = dot_nn(key_head.T, dscores[slot]).T
        for block in range(blocks):
            at = slice(block * QUERY_BLOCK, (block + 1) * QUERY_BLOCK)
            for index, part in enumerate((dquery, dkey_wide[:, :DK], dvalue)):
                part_cols = slice(index * width + head * DK, index * width + (head + 1) * DK)
                dqkv[rows_at(order[block]), part_cols] = part[at].astype(bf16)
        sums = dkey_wide[:, DK:]
        far_grad[head : head + 1, :] += jnp.concatenate(
            [
                jnp.sum(jnp.where(before, sums, 0.0), axis=0, keepdims=True),
                jnp.sum(jnp.where(after, sums, 0.0), axis=0, keepdims=True),
            ],
            axis=1,
        )
    total = jnp.zeros((1, normed.shape[1]), f32)
    for half, target in enumerate((dnormed_keep, dnormed_send)):
        for part in range(2):
            at = slice((2 * half + part) * QUERY_BLOCK, (2 * half + part + 1) * QUERY_BLOCK)
            dnormed = dot_nn(dqkv[at, :], weight_t[...])
            target[part * QUERY_BLOCK : (part + 1) * QUERY_BLOCK, :] = dnormed.astype(bf16)
            total = total + jnp.sum(dnormed * normed[at, :].astype(f32), axis=0, keepdims=True)
    gain_sum[...] = total


def attention_backward(order, row, place, lengths, qkv, douts, logsum, band, far, weight_t, normed):
    length, width = qkv.shape[0], qkv.shape[1] // 3
    half = ((length // 2, normed.shape[1]), bf16)
    return order.call(
        functools.partial(attention_backward_kernel, row),
        "attention_backward",
        (place, lengths, qkv, *douts, logsum, band, far, weight_t, normed),
        [smem, smem] + [vmem] * 9,
        [(qkv.shape, bf16, pltpu.HBM), half, half, (band.shape, f32), ((8, 2 * LANES), f32)]
        + [((1, normed.shape[1]), f32)],
        52,
        scratch=[pltpu.VMEM((length // QUERY_BLOCK, length, QUERY_BLOCK), f32)]
        + [pltpu.VMEM((length, width), bf16)] * 3
        + [pltpu.VMEM((2, length, DK + LANES), bf16)]
        + [pltpu.VMEM((2, length, length), bf16)] * 2,
    )


def branch_kernel(heads_0, heads_1, heads_2, heads_3, out_0, out_1, out_2, out_3, own, other_y, gain, middle, normed):
    count = own.shape[1]
    for index, piece in enumerate((own, other_y)):
        here = slice(index * count, (index + 1) * count)
        there = slice((1 - index) * count, (2 - index) * count)
        branch = (
            dot_nn(heads_0[here, :], out_0[...])
            + dot_nn(heads_1[here, :], out_1[...])
            + dot_nn(heads_2[there, :], out_2[...])
            + dot_nn(heads_3[there, :], out_3[...])
        )
        rows = piece[...].reshape(branch.shape).astype(f32) + branch
        if index == 0:
            middle[...] = rows
        normed[here, :] = (rows * norm_factor(rows) * gain[...]).astype(bf16)


def attention_branch(order, heads, out_parts, own, other_y, gain):
    count, width = own[0].shape[1:]
    return order.call(
        branch_kernel,
        "attention_branch",
        (*heads, *out_parts, own[0], other_y[0], gain),
        [vmem] * 8 + [piece_of(*own), piece_of(*other_y), vmem],
        [((count, width), f32), ((2 * count, width), bf16)],
        28,
    )


def branch_backward_kernel(
    keep, received, from_y, middle, out_grad, gain, out_0, out_1, out_2, out_3,
    dmiddle, dbranch, gain_sum, douts_own, douts_core, douts_y,
):
    dnormed = summed(keep, received, from_y)
    rows = middle[...]
    result = out_grad[0].astype(f32) + norm_backward(dnormed, rows, gain[...])
    dmiddle[...] = result
    low = result.astype(bf16)
    dbranch[...] = low
    gain_sum[...] = jnp.sum(dnormed * rows * norm_factor(rows), axis=0, keepdims=True)
    douts_own[...] = dot_nt(low, out_0[...]).astype(bf16)
    douts_core[...] = dot_nt(low, out_1[...]).astype(bf16)
    douts_y[0] = dot_nt(low, out_2[...]).astype(bf16)
    douts_y[1] = dot_nt(low, out_3[...]).astype(bf16)


def branch_backward(order, row, keep, received, from_y, middle, out_grad, gain, out_parts):
    count, width = middle.shape
    first = pl.BlockSpec((count, width), lambda *_: (0, 0))
    return order.call(
        branch_backward_kernel,
        "branch_backward",
        (keep, received, from_y, middle, out_grad, gain, *out_parts),
        [first, pl.BlockSpec((1, count, width), lambda *_: (0, 0, 0)), vmem, vmem, row_of(row, out_grad.shape)]
        + [vmem] * 5,
        [((count, width), f32), ((count, width), bf16), ((1, width), f32)]
        + [((count, out_parts[0].shape[0]), bf16)] * 2
        + [((2, count, out_parts[0].shape[0]), bf16)],
        24,
    )


def outproj_grad_kernel(rows, *refs):
    heads, branches, (keep, send) = refs[: 4 * rows], refs[4 * rows : 5 * rows], refs[5 * rows :]
    count = branches[0].shape[0]
    for index in range(4):
        total = None
        for row in range(rows):
            at = slice((index // 2) * count, (index // 2 + 1) * count)
            part = dot_tn(heads[4 * row + index][at, :], branches[row][...])
            total = part if total is None else total + part
        target = keep if index % 2 == 0 else send
        target[index // 2] = total.astype(bf16)


def outproj_grad(order, heads, branches):
    rows, width, cols = len(branches), branches[0].shape[1], heads[0].shape[1]
    return order.call(
        functools.partial(outproj_grad_kernel, rows),
        "outproj_gradient",
        (*heads, *branches),
        [vmem] * (5 * rows),
        [((2, cols, width), bf16)] * 2,
        24,
    )


def feed_kernel(chunk, blocks, leads, normed_keep, normed_recv, *refs):
    count = len(blocks)
    grads_hbm, (gate_hbm, up_hbm, down_hbm), refs = refs[:count], refs[count : count + 3], refs[count + 3 :]
    refs = refs[-12:]
    hidden_ref, dgate_ref, dup_ref, dnormed_keep, feed_keep, sends = refs[:6]
    gate_t, up_t, down, grads, weight_sem, grad_sem = refs[6:]
    step = pl.program_id(0)
    units = down.shape[0]
    chunks = [slice(start, min(units, start + chunk)) for start in range(0, units, chunk)]
    kept = sum(block < 2 for block in blocks)

    def weight_copies(index):
        at = pl.ds(chunks[index].start, chunks[index].stop - chunks[index].start)
        pairs = ((gate_hbm, gate_t), (up_hbm, up_t), (down_hbm, down))
        return [
            pltpu.make_async_copy(source.at[at], target.at[at], weight_sem.at[index, which])
            for which, (source, target) in enumerate(pairs)
        ]

    def grad_copy(index):
        source = grads_hbm[index] if leads[index] is None else grads_hbm[index].at[leads[index]]
        return pltpu.make_async_copy(source, grads.at[index], grad_sem.at[index])

    def work(first):
        normed = jnp.where(step < kept, normed_keep[...], normed_recv[...])
        grad = grads[step]
        for index, at in enumerate(chunks):
            if first:
                for copy in weight_copies(index):
                    copy.wait()
            values = gated_products(normed, grad, gate_t[at, :], up_t[at, :], down[at, :])
            hidden_ref[:, at], dgate_ref[:, at], dup_ref[:, at] = values
        for ref in (dgate_ref, dup_ref):
            ref[:, units:] = jnp.zeros((ref.shape[0], ref.shape[1] - units), bf16)
        dnormed = dot_nn(dgate_ref[:, :units], gate_t[...]) + dot_nn(dup_ref[:, :units], up_t[...])
        dnormed = dnormed.astype(bf16)
        feed = dot_nn(hidden_ref[...], down[...]).astype(bf16)

        @pl.when(step < kept)
        def _():
            dnormed_keep[...] = dnormed
            feed_keep[...] = feed

        @pl.when(step >= kept)
        def _():
            sends[0] = dnormed
            sends[1] = feed

    @pl.when(step == 0)
    def _():
        for index in range(len(chunks)):
            for copy in weight_copies(index):
                copy.start()
            if index == 0:
                grad_copy(0).start()
        for index in range(1, count):
            grad_copy(index).start()
        grad_copy(0).wait()
        work(True)

    @pl.when(step > 0)
    def _():
        for index in range(1, count):
            pl.when(step == index)(grad_copy(index).wait)
        work(False)


def feed_forward(order, normed_keep, normed_recv, blocks, grads, gate_t, up_t, down, before=()):
    units, width = down.shape
    length = 2 * normed_keep.shape[0]
    count = length // 4
    if len(blocks) == 4:
        kept_at, sent_at, at = (lambda s: jnp.minimum(s, 1)), (lambda s: jnp.maximum(s - 2, 0)), (lambda s: s)
    else:
        low, high = blocks
        kept_at = sent_at = lambda s: low
        at = lambda s: low + s * (high - low)
    first = pl.BlockSpec((count, width), lambda step: (kept_at(step), 0))
    last = pl.BlockSpec((count, width), lambda step: (sent_at(step), 0))
    pair = pl.BlockSpec((2, count, width), lambda step: (0, sent_at(step), 0))
    each = pl.BlockSpec((count, units), lambda step: (at(step), 0))
    wide = -(-units // 128) * 128
    padded = pl.BlockSpec((count, wide), lambda step: (at(step), 0))
    half = ((length // 2, width), bf16)
    chunk = 256
    inputs = 5 + len(grads)
    return order.call(
        functools.partial(feed_kernel, chunk, blocks, [lead for _, lead in grads]),
        "feed_forward",
        (normed_keep, normed_recv, *[array for array, _ in grads], gate_t, up_t, down, *before),
        [first, last] + [anywhere] * (inputs - 2 + len(before)),
        [((length, units), bf16, pltpu.HBM)]
        + [((length, wide), bf16, pltpu.HBM)] * 2
        + [half, half, ((2, length // 2, width), bf16)],
        44,
        out_specs=[each, padded, padded, first, first, pair],
        grid=(len(blocks),),
        scratch=[pltpu.VMEM((units, width), bf16)] * 3
        + [
            pltpu.VMEM((len(blocks), count, width), bf16),
            pltpu.SemaphoreType.DMA((-(-units // chunk), 3)),
            pltpu.SemaphoreType.DMA((len(blocks),)),
        ],
        aliases={inputs + index: index for index in range(len(before))},
    )


def gated_products(normed, grad, gate, up, down):
    gate = dot_nt(normed, gate)
    up = dot_nt(normed, up)
    dhidden = dot_nt(grad, down)
    square = gate * gate
    bend = jnp.tanh(gelu_scale * gate * (1.0 + gelu_cubic * square))
    half = 0.5 * (1.0 + bend)
    active = gate * half
    slope = half + (0.5 * gelu_scale) * gate * (1.0 - bend * bend) * (1.0 + (3 * gelu_cubic) * square)
    return (active * up).astype(bf16), (dhidden * up * slope).astype(bf16), (dhidden * active).astype(bf16)


def feed_last_kernel(chunk, pieces, rows, bits, place, *refs):
    count = sum(map(len, pieces))
    arrays, refs = refs[:count], refs[count:]
    earlier, refs = refs[: 3 * (rows - 1)], refs[3 * (rows - 1) :]
    (gate_hbm, up_hbm, down_hbm), refs = refs[:3], refs[3:]
    (dnormed_keep, feed_keep, sends), outs, refs = refs[:3], refs[3:9], refs[9:]
    gate_t, up_t, down, normed, grads, hidden, dgate, dup, stage = refs[:9]
    weight_sem, left_sem, right_sem, out_sem = refs[9:]
    step = pl.program_id(0)
    units = down.shape[0]
    chunks = [slice(start, min(units, start + chunk)) for start in range(0, units, chunk)]
    length = normed.shape[0] // rows
    block = length // 4
    base = (rows - 1) * length

    def weight_copies(index):
        at = pl.ds(chunks[index].start, chunks[index].stop - chunks[index].start)
        pairs = ((gate_hbm, gate_t), (up_hbm, up_t), (down_hbm, down))
        return [
            pltpu.make_async_copy(source.at[at], target.at[at], weight_sem.at[index, which])
            for which, (source, target) in enumerate(pairs)
        ]

    def left_copies(side):
        copies = []
        taken = sum(map(len, pieces[:side]))
        at = 0
        for index, lead in enumerate(pieces[side]):
            source = arrays[taken + index]
            source = source if lead is None else source.at[lead]
            copies.append(
                (
                    at,
                    pltpu.make_async_copy(
                        source, (normed, grads)[side].at[pl.ds(at, source.shape[0])], left_sem.at[side, index]
                    ),
                )
            )
            at += source.shape[0]
        return copies

    def right_copies():
        return [
            pltpu.make_async_copy(
                earlier[3 * row + which], target.at[pl.ds(row * length, length)], right_sem.at[row, which]
            )
            for row in range(rows - 1)
            for which, target in enumerate((hidden, dgate, dup))
        ]

    def work(first):
        at = pl.ds(pl.multiple_of(base + step * block, block), block)
        rows_normed, rows_grad = normed[at, :], grads[at, :]
        for index, part in enumerate(chunks):
            if first:
                for copy in weight_copies(index):
                    copy.wait()
            values = gated_products(rows_normed, rows_grad, gate_t[part, :], up_t[part, :], down[part, :])
            for target, value in zip((hidden, dgate, dup), values):
                target[at, part] = value
        dnormed = dot_nn(dgate[at, :units], gate_t[...]) + dot_nn(dup[at, :units], up_t[...])
        dnormed = dnormed.astype(bf16)
        feed = dot_nn(hidden[at, :], down[...]).astype(bf16)

        @pl.when(step < 2)
        def _():
            dnormed_keep[...] = dnormed
            feed_keep[...] = feed

        @pl.when(step >= 2)
        def _():
            sends[0] = dnormed
            sends[1] = feed

    def gradients():
        width = normed.shape[1]
        chunk_rows = outs[0].shape[1]
        tile = width // 2
        half_rows = tile // 2
        half_chunks = half_rows // chunk_rows
        sending = {}
        turn = 0
        for product, (left, right) in enumerate(((grads, hidden), (normed, dgate), (normed, dup))):
            bit = bits[product]
            for part in range(2):
                slot = turn % 2
                turn += 1
                for copy in sending.get(slot, ()):
                    copy.wait()
                for half in range(2):
                    cols = slice(part * tile + half * half_rows, part * tile + (half + 1) * half_rows)
                    value = dot_tn(left[:, cols], right[:, :units]).reshape(half_chunks, chunk_rows, units)
                    stage[slot, half * half_chunks : (half + 1) * half_chunks] = value.astype(bf16)
                sending[slot] = []
                for index in range(half_chunks):
                    low = index % (1 << bit)
                    first_chunk = (index - low) * 2 + low
                    for side, which in enumerate((place[2 + bit], 1 - place[2 + bit])):
                        copy = pltpu.make_async_copy(
                            stage.at[slot, first_chunk + which * (1 << bit)],
                            outs[2 * product + side].at[part * half_chunks + index],
                            out_sem.at[product, side, part * half_chunks + index],
                        )
                        copy.start()
                        sending[slot].append(copy)
        for copies in sending.values():
            for copy in copies:
                copy.wait()

    @pl.when(step == 0)
    def _():
        mine = [[copy for at, copy in left_copies(side) if at >= base] for side in range(2)]
        for index in range(len(chunks)):
            for copy in weight_copies(index):
                copy.start()
            if index == 0:
                mine[0][0].start()
                mine[1][0].start()
        for copies in mine:
            for copy in copies[1:]:
                copy.start()
        mine[0][0].wait()
        mine[1][0].wait()
        work(True)

    @pl.when(step == 1)
    def _():
        for side in range(2):
            for at, copy in left_copies(side):
                if at < base:
                    copy.start()
                elif at > base:
                    copy.wait()
        for copy in right_copies():
            copy.start()

    pl.when(step > 0)(lambda: work(False))

    @pl.when(step == 3)
    def _():
        for side in range(2):
            for at, copy in left_copies(side):
                if at < base:
                    copy.wait()
        for copy in right_copies():
            copy.wait()
        gradients()


def feed_last(order, place, lefts, earlier, gate_t, up_t, down, bits):
    units, width = down.shape
    size = lax.axis_size("dp")
    rows = len(earlier) + 1
    length = 4 * lefts[1][-1][0].shape[-2]
    count = length // 4
    first = pl.BlockSpec((count, width), lambda step: (jnp.minimum(step, 1), 0))
    pair = pl.BlockSpec((2, count, width), lambda step: (0, jnp.maximum(step - 2, 0), 0))
    half = ((length // 2, width), bf16)
    chunk = 256
    chunk_rows = width // size
    wide = -(-units // 128) * 128
    plan = [[lead for _, lead in side] for side in lefts]
    inputs = [array for side in lefts for array, _ in side] + [array for row in earlier for array in row]
    return order.call(
        functools.partial(feed_last_kernel, chunk, plan, rows, bits),
        "feed_forward_and_gradients",
        (place, *inputs, gate_t, up_t, down),
        [smem] + [anywhere] * (len(inputs) + 3),
        [half, half, ((2, length // 2, width), bf16)] + [((size // 2, chunk_rows, units), bf16)] * 6,
        58,
        out_specs=[first, first, pair] + [anywhere] * 6,
        grid=(4,),
        scratch=[pltpu.VMEM((units, width), bf16)] * 3
        + [pltpu.VMEM((rows * length, width), bf16)] * 2
        + [pltpu.VMEM((rows * length, units), bf16)]
        + [pltpu.VMEM((rows * length, wide), bf16)] * 2
        + [pltpu.VMEM((2, size // 2, chunk_rows, units), bf16)]
        + [
            pltpu.SemaphoreType.DMA((-(-units // chunk), 3)),
            pltpu.SemaphoreType.DMA((2, max(map(len, lefts)))),
            pltpu.SemaphoreType.DMA((max(rows - 1, 1), 3)),
            pltpu.SemaphoreType.DMA((3, 2, size // 2)),
        ],
    )


def halves(parts, stride, bit):
    count, rows, width = parts.shape
    pairs = parts.reshape(count // (2 * stride), 2, stride, rows, width)
    low, high = pairs[:, 0], pairs[:, 1]
    shape = (count // 2, rows, width)
    return jnp.where(bit == 0, low, high).reshape(shape), jnp.where(bit == 0, high, low).reshape(shape)


def gradient_kernel(groups, products, turned, extra, cuts, place, *refs):
    rows = len(groups)
    extras, refs = refs[:extra], refs[extra:]
    pieces = sum(map(len, groups))
    lefts, refs = refs[:pieces], refs[pieces:]
    rights_hbm, refs = refs[: products * rows], refs[products * rows :]
    outs, refs = refs[: 2 * len(cuts)], refs[2 * len(cuts) :]
    stages, (left, right, left_sem, right_sem, out_sem) = refs[: len(cuts)], refs[len(cuts) :]
    steps = left.shape[0]
    tile = left.shape[1 if turned else 2]
    length = right.shape[0] // rows
    cols = rights_hbm[0].shape[1]

    def left_copies(row, step):
        part = pl.ds(step * tile, tile)
        if turned:
            at = pl.ds(row * length, length)
            return [pltpu.make_async_copy(lefts[row].at[part], left.at[step, :, at], left_sem.at[step, row, 0])]
        taken = sum(map(len, groups[:row]))
        copies = []
        at = row * length
        for index, lead in enumerate(groups[row]):
            source = lefts[taken + index]
            source = source if lead is None else source.at[lead]
            count = source.shape[0]
            copies.append(
                pltpu.make_async_copy(
                    source.at[:, part], left.at[step, pl.ds(at, count)], left_sem.at[step, row, index]
                )
            )
            at += count
        return copies

    def right_copy(product, row):
        index = product * rows + row
        return pltpu.make_async_copy(
            rights_hbm[index],
            right.at[pl.ds(row * length, length), pl.ds(product * cols, cols)],
            right_sem.at[index],
        )

    first = [[right_copy(product, row) for product in range(products)] + left_copies(row, 0) for row in range(rows)]
    later = [[copy for row in range(rows) for copy in left_copies(row, step)] for step in range(1, steps)]
    for group in first + later:
        for copy in group:
            copy.start()

    part_rows = tile // 2
    sending = []
    for step in range(steps):
        for group in first if step == 0 else [later[step - 1]]:
            for copy in group:
                copy.wait()
        slot = step % 2
        for half in range(2):
            rows_at = slice(half * part_rows, (half + 1) * part_rows)
            if turned:
                total = dot_nn(left[step, rows_at, :], right[...])
            else:
                total = dot_tn(left[step, :, rows_at], right[...])
            totals = [total[:, product * cols : (product + 1) * cols] for product in range(products)]
            if extra:
                turned_at = slice(step * tile + rows_at.start, step * tile + rows_at.stop)
                totals.append(sum(ref[0, :, turned_at].astype(f32) for ref in extras).T)
            for index, (parts, bit) in enumerate(cuts):
                chunk_rows = outs[2 * index].shape[1]
                count = part_rows // chunk_rows
                chunks = slice(half * count, (half + 1) * count)
                taken = [totals[which][:, where] for which, where in parts]
                value = taken[0] if len(taken) == 1 else jnp.concatenate(taken, axis=1)
                stages[index][slot, chunks] = value.reshape(count, chunk_rows, value.shape[1]).astype(bf16)
        for index, (parts, bit) in enumerate(cuts):
            chunk_rows = outs[2 * index].shape[1]
            mine = place[2 + bit]
            count = tile // chunk_rows // 2
            for chunk in range(count):
                low = chunk % (1 << bit)
                base = (chunk - low) * 2 + low
                for side, which in enumerate((mine, 1 - mine)):
                    copy = pltpu.make_async_copy(
                        stages[index].at[slot, base + which * (1 << bit)],
                        outs[2 * index + side].at[step * count + chunk],
                        out_sem.at[index, side, step * count + chunk],
                    )
                    copy.start()
                    sending.append(copy)
    for copy in sending:
        copy.wait()


def gradient(order, name, place, lefts, rights, cuts, extras=(), turned=False):
    size = lax.axis_size("dp")
    length, cols = rights[0][0].shape
    width = lefts[0][0][0].shape[0 if turned else -1]
    steps = 2
    tile = width // steps
    chunk_rows = width // size
    pieces = [piece for group in lefts for piece in group]
    rows = len(lefts)
    flat = [array for group in rights for array in group]
    widths = [sum(at.stop - at.start for _, at in parts) for parts, _ in cuts]
    plan = [[lead for _, lead in group] for group in lefts]
    results = order.call(
        functools.partial(gradient_kernel, plan, len(rights), turned, len(extras), cuts),
        name,
        (place, *extras, *[array for array, _ in pieces], *flat),
        [smem]
        + [pl.BlockSpec((1,) + extra.shape[1:], lambda *_: (0, 0, 0)) for extra in extras]
        + [anywhere] * (len(pieces) + len(flat)),
        [((size // 2, chunk_rows, w), bf16) for w in widths for _ in range(2)],
        52,
        out_specs=[anywhere] * (2 * len(widths)),
        scratch=[pltpu.VMEM((2, size // steps, chunk_rows, w), bf16) for w in widths]
        + [
            pltpu.VMEM((steps, tile, rows * length) if turned else (steps, rows * length, tile), bf16),
            pltpu.VMEM((rows * length, len(rights) * cols), bf16),
            pltpu.SemaphoreType.DMA((steps, rows, max(map(len, lefts)))),
            pltpu.SemaphoreType.DMA((len(flat),)),
            pltpu.SemaphoreType.DMA((len(cuts), 2, size // 2)),
        ],
    )
    return [results[2 * index : 2 * index + 2] for index in range(len(cuts))]


def exchange(sent, bit):
    return lax.ppermute(sent, "dp", [(i, i ^ (1 << bit)) for i in range(lax.axis_size("dp"))])


def halve_kernel(plans, place, *refs):
    count = sum(map(len, plans))
    inputs, outputs = refs[: 2 * count], refs[2 * count :]
    taken = 0
    for index, plan in enumerate(plans):
        keep_ref, send_ref = outputs[2 * index : 2 * index + 2]
        at = 0
        for stride, bit in plan:
            kept, received = inputs[2 * taken : 2 * taken + 2]
            taken += 1
            parts = kept[...].astype(f32) + received[...].astype(f32)
            keep, send = halves(parts, stride, place[2 + bit])
            cols = slice(at, at + parts.shape[2])
            keep_ref[:, :, cols] = keep.astype(bf16)
            send_ref[:, :, cols] = send.astype(bf16)
            at += parts.shape[2]


def total_kernel(*refs):
    count = 0
    while count < len(refs) and len(refs[count].shape) == 3:
        count += 1
    outs = list(refs[count:])
    for index in range(count // 2):
        total = refs[2 * index][0].astype(f32) + refs[2 * index + 1][0].astype(f32)
        at = 0
        while at < total.shape[1]:
            out = outs.pop(0)
            out[...] = total[:, at : at + out.shape[1]]
            at += out.shape[1]


class Scatter:
    def __init__(self, first, parts, last=False):
        count = lax.axis_size("dp").bit_length() - 1
        self.bits = [first] + [bit for bit in range(count) if bit != first]
        if last:
            self.bits = self.bits[:1] + self.bits[2:] + self.bits[1:2]
        self.left = sorted(self.bits)
        self.widths = [parts[0].shape[2]]
        self.send(*parts)

    def send(self, kept, sent):
        bit = self.bits.pop(0)
        self.left.remove(bit)
        self.parts = kept, exchange(sent, bit)


def halve(order, place, *groups):
    groups = [group if isinstance(group, tuple) else (group,) for group in groups]
    plans = [[(1 << scatter.left.index(scatter.bits[0]), scatter.bits[0]) for scatter in group] for group in groups]
    flat = [scatter for group in groups for scatter in group]
    shapes = [
        (group[0].parts[0].shape[0] // 2, group[0].parts[0].shape[1], sum(s.parts[0].shape[2] for s in group))
        for group in groups
    ]
    results = order.call(
        functools.partial(halve_kernel, plans),
        "halve",
        (place, *[part for scatter in flat for part in scatter.parts]),
        [smem] + [vmem] * (2 * len(flat)),
        [(shape, bf16) for shape in shapes for _ in range(2)],
        24,
    )
    for index, group in enumerate(groups):
        for other in group[1:]:
            assert group[0].left == other.left
            group[0].widths += other.widths
        group[0].send(*results[2 * index : 2 * index + 2])


def finish(order, *scatters):
    for scatter in scatters:
        assert not scatter.bits, scatter.bits
    return order.call(
        total_kernel,
        "gradient_output",
        [part for scatter in scatters for part in scatter.parts],
        [vmem] * (2 * len(scatters)),
        [
            ((scatter.parts[0].shape[1], width), f32, pltpu.HBM) for scatter in scatters for width in scatter.widths
        ],
        16,
    )


def pass_kernel(*refs):
    for keep, received, out in zip(refs[0::2], refs[1::2], refs[-(len(refs) // 3) :]):
        out[...] = (keep[...].reshape(out.shape).astype(f32) + received[...].reshape(out.shape).astype(f32)).astype(bf16)


def pass_on(order, keep, received, lead=None):
    count, width = keep.shape[0] // 2, keep.shape[1]
    second = pl.BlockSpec((count, width), lambda *_: (1, 0))
    other = second if lead is None else pl.BlockSpec((1, count, width), lambda *_: (lead, 1, 0))
    return over_y(
        order.call(pass_kernel, "pass_on", (keep, received), [second, other], [((count, width), bf16)], 8)[0]
    )


def pass_rows_kernel(*refs):
    out = refs[-1]
    for row in range(out.shape[0]):
        received = refs[2 * row + 1][...].reshape(out.shape[1:])
        out[row] = (refs[2 * row][...].astype(f32) + received.astype(f32)).astype(bf16)


def pass_rows(order, parts, lead=None):
    count, width = parts[0][0].shape[0] // 2, parts[0][0].shape[1]
    second = pl.BlockSpec((count, width), lambda *_: (1, 0))
    other = second if lead is None else pl.BlockSpec((1, count, width), lambda *_: (lead, 1, 0))
    return over_y(
        order.call(
            pass_rows_kernel,
            "pass_on",
            [array for pair in parts for array in pair],
            [second, other] * len(parts),
            [((len(parts), count, width), bf16)],
            12,
        )[0]
    )


def outproj_pass(order, keep, received):
    shape = keep.shape[1:]
    second = pl.BlockSpec((1,) + shape, lambda *_: (1, 0, 0))
    return over_y(order.call(pass_kernel, "pass_on", (keep, received), [second] * 2, [((1,) + shape, bf16)], 8)[0])


def join_kernel(bit, place, mine, received, out):
    count = mine.shape[0]
    which = place[2 + bit]
    out[pl.ds(pl.multiple_of(which * count, 16), count), :] = mine[...]
    out[pl.ds(pl.multiple_of((1 - which) * count, 16), count), :] = received[...]


def join(order, place, bit, mine, received):
    shape = (2 * mine.shape[0],) + mine.shape[1:]
    return order.call(
        functools.partial(join_kernel, bit), "join", (place, mine, received), [smem, vmem, vmem], [(shape, mine.dtype)], 8
    )[0]


def pause_kernel(out):
    out[...] = jnp.zeros_like(out)


def pause(order):
    order.call(pause_kernel, "pause", (), [], [((8, 128), f32)], 4)


def fence(order, array):
    return order.call(
        lambda *_: None,
        "fence",
        (array,),
        [anywhere],
        [(array.shape, array.dtype)],
        4,
        out_specs=[anywhere],
        aliases={0: 0},
    )[0]


def relay_kernel(source, target):
    target[...] = source[0] if len(source.shape) == 3 else source[...]


def relay(order, array, row=None):
    shape = array.shape if row is None else array.shape[1:]
    spec = vmem if row is None else row_of(row, array.shape)
    return order.call(relay_kernel, "relay", (array,), [spec], [(shape, array.dtype)], 8)[0]


def summed(keep, received, from_y):
    shape = keep.shape
    return sum(ref[...].reshape(shape).astype(f32) for ref in (keep, received, from_y))


def block_out_kernel(rows, *refs):
    out = refs[-1]
    for row in range(rows):
        middle, keep, received, from_y = refs[4 * row : 4 * row + 4]
        out[row] = middle[...] + summed(keep, received, from_y)


def block_output(order, middles, feeds, from_y):
    rows = len(from_y)
    count, width = from_y[0].shape
    first = pl.BlockSpec((count, width), lambda *_: (0, 0))
    other = pl.BlockSpec((1, count, width), lambda *_: (1, 0, 0))
    return order.call(
        functools.partial(block_out_kernel, rows),
        "block_output",
        [array for row in range(rows) for array in (middles[row], *feeds[row], from_y[row])],
        [vmem, first, other, vmem] * rows,
        [((rows, count, width), f32, pltpu.HBM)],
        30,
    )[0]


def input_grad_kernel(rows, from_y, inputs, gain, *refs):
    out = refs[-1]
    for row in range(rows):
        dmiddle, keep, received = refs[3 * row : 3 * row + 3]
        dnormed = summed(keep, received, from_y.at[row])
        out[row] = dmiddle[...] + norm_backward(dnormed, inputs[row].astype(f32), gain[...])


def input_gradient(order, dmiddles, inner, from_y, inputs, gain):
    rows, count, width = from_y.shape
    first = pl.BlockSpec((count, width), lambda *_: (0, 0))
    return order.call(
        functools.partial(input_grad_kernel, rows),
        "input_gradient",
        [from_y, inputs, gain] + [array for row in range(rows) for array in (dmiddles[row], *inner[row])],
        [vmem] * 3 + [vmem, first, first] * rows,
        [(from_y.shape, f32, pltpu.HBM)],
        36,
    )[0]


def small_kernel(heads, rows, buckets, place, gain, *refs):
    norms_one, norms_two, out = refs[:rows], refs[rows : 2 * rows], refs[-1]
    bands, fars = refs[2 * rows : 3 * rows], refs[3 * rows : 4 * rows]
    lines = gain.shape[1] // 128
    ones = sum(ref[...] for ref in norms_one) / gain[...]
    twos = sum(ref[...] for ref in norms_two)
    for index, vector in enumerate((ones, twos)):
        for line in range(lines):
            out[index * lines + line : index * lines + line + 1, :] = vector[:, line * 128 : (line + 1) * 128]
    side = REACH
    tiles = {}
    for key_block in range(bands[0].shape[1] // side):
        for query_block in range(bands[0].shape[2] // side):
            tiles.setdefault(key_block - 1 - query_block, []).append((key_block, query_block))
    row_at = lax.broadcasted_iota(jnp.int32, (side, side), 0)
    col_at = lax.broadcasted_iota(jnp.int32, (side, side), 1)
    lane = lax.broadcasted_iota(jnp.int32, (1, 128), 1)
    mine = lane == place[1] + 2 * place[0]
    which = lax.broadcasted_iota(jnp.int32, (buckets, 1), 0)
    for head in range(heads):
        sums = [jnp.zeros((1, side), f32) for _ in range(buckets)]
        for distance, blocks in tiles.items():
            grads = sum(
                band[head, key * side : (key + 1) * side, query * side : (query + 1) * side]
                for band in bands
                for key, query in blocks
            )
            index = bucket_of(row_at - col_at + distance * side, buckets)
            near = abs(distance) < 2
            for bucket in range(buckets):
                after = bucket >= buckets // 2
                if (near or bucket in (buckets // 2 - 1, buckets - 1)) and (distance == 0 or after == (distance > 0)):
                    sums[bucket] += jnp.sum(jnp.where(index == bucket, grads, 0.0), axis=0, keepdims=True)
        far = sum(ref[head : head + 1, :] for ref in fars)
        total = jnp.sum(jnp.concatenate(sums, axis=0), axis=1, keepdims=True)
        total = total + jnp.where(which == buckets // 2 - 1, jnp.sum(far[:, :LANES], axis=1, keepdims=True), 0.0)
        total = total + jnp.where(which == buckets - 1, jnp.sum(far[:, LANES:], axis=1, keepdims=True), 0.0)
        at = 2 * lines + head * buckets
        out[at : at + buckets, :] = jnp.where(mine, total, 0.0)


def small_gradients(order, place, heads, buckets, gain, norms_one, norms_two, bands, fars):
    lines = gain.shape[1] // 128
    rows = len(norms_one)
    return order.call(
        functools.partial(small_kernel, heads, rows, buckets),
        "small_gradients",
        (place, gain, *norms_one, *norms_two, *bands, *fars),
        [smem] + [vmem] * (1 + 4 * rows),
        [((2 * lines + heads * buckets, 128), f32)],
        16,
    )[0]


def add_kernel(*refs):
    refs[-1][...] = sum(ref[...] for ref in refs[:-1])


def add_all(order, arrays):
    return order.call(add_kernel, "small_sum", arrays, [vmem] * len(arrays), [(arrays[0].shape, f32)], 4)[0]


def small_rounds(order, vector):
    count = lax.axis_size("dp").bit_length() - 1
    sends = [over_core, over_y] + [functools.partial(exchange, bit=bit) for bit in range(count)]
    for send in sends:
        moved = send(vector)
        yield None
        vector = add_all(order, [vector, moved])
    yield vector


def per_device(
    block_input,
    out_grad,
    seg_lengths,
    norm1_gain,
    norm2_gain,
    rel_bias,
    w_query,
    w_key,
    w_value,
    w_out,
    w_gate,
    w_up,
    w_down,
):
    rows, count, width = block_input.shape
    length = 4 * count
    here = lax.axis_index("tensor")
    dp_bits = lax.axis_size("dp").bit_length() - 1
    dp_at = lax.axis_index("dp")
    place = jnp.stack([here // 2, here % 2] + [(dp_at >> bit) & 1 for bit in range(dp_bits)]).astype(jnp.int32)
    head_width = w_query.shape[1]
    heads = head_width // DK
    buckets = rel_bias.shape[0]
    gain_one = norm1_gain.astype(f32)[None]
    gain_two = norm2_gain.astype(f32)[None]
    first_head = here * heads
    weight_t = jnp.concatenate([w_query.T, w_key.T, w_value.T], axis=0)
    gate_t, up_t = w_gate.T, w_up.T

    order = Order()
    every_row = range(rows)
    last_row = rows - 1

    band, far = bias_parts(lax.dynamic_slice_in_dim(rel_bias, first_head, heads, 1), length)
    order.after(band, far, weight_t)
    first_y = over_y(jnp.concatenate([block_input[:1], out_grad[:1]]))
    first_both = over_core(first_y)
    input_core = over_core(block_input)
    grad_core = over_core(out_grad)
    out_core = over_core(w_out)
    input_y, input_both = [(first_y, 0)], [(first_both, 0)]
    grad_y, grad_both = [(first_y, 1)], [(first_both, 1)]
    bits = (1, 2)
    quarter = w_out.shape[0] // 4
    out_at = (place[2 + bits[0]] + 2 * place[2 + bits[1]]) * quarter
    out_y = over_y(lax.dynamic_slice_in_dim(w_out, out_at, quarter, 0))
    order.after(input_core, grad_core, out_core)
    order.after(first_y)
    for row in range(1, rows):
        input_y.append((over_y(relay(order, block_input, row)), None))
    out_y = (out_y, exchange(out_y, bits[0]))

    normed_one, normed_one_t, qkvs, logsums, attended, middles = [], [], [], [], [], []
    normed_keeps, normed_recvs = [], []

    def second_norm(row):
        middle, normed_keep = attention_branch(
            order, attended[row], out_parts, (block_input, row), input_y[row], gain_two
        )
        middles.append(middle)
        normed_keeps.append(normed_keep)
        normed_recvs.append(over_core(normed_keep))

    for row in every_row:
        if row == 0:
            out_y = join(order, place, bits[0], *out_y)
            out_y = (out_y, exchange(out_y, bits[1]))
        normed, qkv, normed_t = project(
            order, [(block_input, row), input_y[row], (input_core, row), input_both[row]], gain_one, weight_t
        )
        keep, send, logsum = attention_forward(order, row, place, seg_lengths, qkv, band, far)
        other = over_core(send)
        normed_one.append(normed)
        normed_one_t.append(normed_t)
        qkvs.append(qkv)
        logsums.append(logsum)
        attended.append([keep, other, over_y(keep), over_y(other)])
        if row < last_row:
            input_y[row + 1] = (fence(order, input_y[row + 1][0]), None)
            input_both.append((over_core(input_y[row + 1][0]), None))
        if row == 0:
            out_y = join(order, place, bits[1], *out_y)
            out_parts = [w_out, out_core, out_y, over_core(out_y)]
            order.after(other)
    second_norm(0)
    order.after(other)
    for row in range(1, rows):
        grad_y.append((over_y(relay(order, out_grad, row)), None))

    hiddens, dgates, dups, dnormed, feeds = [], [], [], [], []

    def feed(row):
        pieces = [(out_grad, row), grad_y[row], (grad_core, row), grad_both[row]]
        return feed_forward(
            order, normed_keeps[row], normed_recvs[row], (0, 1, 2, 3), pieces, gate_t, up_t, w_down
        )

    def fed(hidden, dgate, dup, dn_keep, ff_keep, sends):
        hiddens.append(hidden)
        dgates.append(dgate)
        dups.append(dup)
        received = over_core(sends)
        dnormed.append([dn_keep, received])
        feeds.append([ff_keep, received])

    fed(*feed(0))
    for row in range(1, rows):
        second_norm(row)
        grad_y[row] = (fence(order, grad_y[row][0]), None)
        grad_both.append((over_core(grad_y[row][0]), None))
    feeds_y = []
    dnormed[0].append(pass_on(order, *dnormed[0], lead=0))
    feeds_y.append(pass_on(order, *feeds[0], lead=1))
    lefts = [
        [piece for r in every_row for piece in ((normed_keeps[r], None), (normed_recvs[r], None))],
        [piece for r in every_row for piece in ((out_grad, r), grad_y[r], (grad_core, r), grad_both[r])],
    ]
    earlier = [(hiddens[r], dgates[r], dups[r]) for r in range(last_row)]
    dn_keep, ff_keep, sends, *parts = feed_last(order, place, lefts, earlier, gate_t, up_t, w_down, (0, 1, 0))
    received = over_core(sends)
    dnormed.append([dn_keep, received])
    feeds.append([ff_keep, received])
    down_scatter, gate_scatter = Scatter(0, parts[:2]), Scatter(1, parts[2:4], last=True)

    dmiddles, dbranches, norm2_sums, douts = [], [], [], []
    def back_to_heads(row):
        dmiddle, dbranch, norm2_sum, dout_own, dout_core, dout_y = branch_backward(
            order, row, *dnormed[row], middles[row], out_grad, gain_two, out_parts
        )
        dmiddles.append(dmiddle)
        dbranches.append(dbranch)
        norm2_sums.append(norm2_sum)
        return dout_own, dout_core, over_y(dout_y)

    def spread(dout_own, dout_core, dout_y):
        dout_y = fence(order, dout_y)
        douts.append((dout_own, dout_y, over_core(jnp.stack([dout_core, dout_y[1]]))))

    dqkvs, norm1_sums, inner, band_grads, far_grads = [], [], [], [], []

    def attend_back(row):
        dqkv, dn_keep, dn_send, band_grad, far_grad, norm1_sum = attention_backward(
            order, row, place, seg_lengths, qkvs[row], douts[row], logsums[row], band, far,
            weight_t, normed_one[row],
        )
        band_grads.append(band_grad)
        far_grads.append(far_grad)
        norm1_sums.append(norm1_sum)
        dqkvs.append(dqkv)
        inner.append([dn_keep, over_core(dn_send)])

    going = back_to_heads(0)
    for row in range(1, rows):
        dnormed[row].append(pass_on(order, *dnormed[row], lead=0))
    spread(*going)
    for row in range(1, rows):
        feeds_y.append(pass_on(order, *feeds[row], lead=1))
    attend_back(0)
    up_scatter = Scatter(0, [parts[4], fence(order, parts[5])])
    order.after(feeds_y[0])
    going = back_to_heads(1)
    order.after(inner[0][1])
    halve(order, place, down_scatter, gate_scatter)
    order.after(feeds_y[1])
    spread(*going)
    out_keep, out_send = outproj_grad(order, [part for group in attended for part in group], dbranches)
    out_recv = over_core(out_send)
    pause(order)
    out_from_y = outproj_pass(order, out_keep, out_recv)
    attend_back(1)
    small = small_gradients(
        order, place, heads, buckets, gain_one, norm1_sums, norm2_sums, band_grads, far_grads
    )
    rounds = small_rounds(order, small)
    next(rounds)
    halve(order, place, down_scatter, gate_scatter, up_scatter)
    first_parts, second_parts = gradient(
        order,
        "projection_gradient",
        place,
        [[(normed_one_t[r], None)] for r in every_row],
        [dqkvs],
        [
            ([(0, slice(0, 2 * head_width))], 0),
            ([(0, slice(2 * head_width, 3 * head_width)), (1, slice(0, head_width))], 1),
        ],
        (out_keep, out_recv, out_from_y),
        turned=True,
    )
    first_scatter, second_scatter = Scatter(0, first_parts), Scatter(1, second_parts)
    next(rounds)
    inner_y = pass_rows(order, inner)
    while len(down_scatter.bits) > 0:
        halve(order, place, down_scatter, gate_scatter)
    down_out, gate_out = finish(order, down_scatter, gate_scatter)
    next(rounds)
    while up_scatter.bits:
        halve(order, place, up_scatter)
    next(rounds)
    block_out = block_output(order, middles, feeds, feeds_y)
    halve(order, place, first_scatter, second_scatter)
    next(rounds)
    input_grad = input_gradient(order, dmiddles, inner, inner_y, block_input, gain_one)
    while first_scatter.bits:
        halve(order, place, first_scatter, second_scatter)
    small = None
    while small is None:
        small = next(rounds)
    (up_out,) = finish(order, up_scatter)
    first_out, second_out = finish(order, first_scatter, second_scatter)
    lines = width // 128
    bias_out = small[2 * lines :, : lax.axis_size("tensor")].reshape(heads, buckets, -1)
    bias_out = jnp.transpose(bias_out, (1, 2, 0)).reshape(rel_bias.shape)
    return (
        block_out,
        input_grad,
        small[:lines].reshape(width),
        small[lines : 2 * lines].reshape(width),
        bias_out,
        first_out[:, :head_width],
        first_out[:, head_width:],
        second_out[:, :head_width],
        second_out[:, head_width:].T,
        gate_out,
        up_out,
        down_out.T,
    )


def solution(mesh):
    in_specs = (
        P("dp", "tensor", None),
        P("dp", "tensor", None),
        P("dp", None),
        P(),
        P(),
        P(),
        P(None, "tensor"),
        P(None, "tensor"),
        P(None, "tensor"),
        P("tensor", None),
        P(None, "tensor"),
        P(None, "tensor"),
        P("tensor", None),
    )
    out_specs = (
        P("dp", "tensor", None),
        P("dp", "tensor", None),
        P(),
        P(),
        P(),
        P("dp", "tensor"),
        P("dp", "tensor"),
        P("dp", "tensor"),
        P("tensor", "dp"),
        P("dp", "tensor"),
        P("dp", "tensor"),
        P("tensor", "dp"),
    )
    return jax.shard_map(
        per_device, mesh=mesh, in_specs=in_specs, out_specs=out_specs, check_vma=False
    )
```

```python
import functools

import jax
import jax.numpy as jnp
import numpy as np
from jax import lax
from jax.experimental import pallas as pl
from jax.experimental.pallas import tpu as pltpu
from jax.sharding import PartitionSpec as P

DK = 64
QUERY_BLOCK = 256
REACH = 128
LANES = 64
MIB = 2**20

bucket_edges = (12, 16, 23, 32, 46, 64, 91)
masked_score = -1000000000.0
epsilon = 1e-06
gelu_scale = float(np.sqrt(2 / np.pi))
gelu_cubic = 0.044715
bf16 = jnp.bfloat16
f32 = jnp.float32

across_y = ((0, 2), (2, 0), (1, 3), (3, 1))
across_core = ((0, 1), (1, 0), (2, 3), (3, 2))
across_both = ((0, 3), (3, 0), (1, 2), (2, 1))


def dot_nn(left, right):
    return lax.dot_general(left, right, (((1,), (0,)), ((), ())), preferred_element_type=f32)


def dot_nt(left, right):
    return lax.dot_general(left, right, (((1,), (1,)), ((), ())), preferred_element_type=f32)


def dot_tn(left, right):
    return lax.dot_general(left, right, (((0,), (0,)), ((), ())), preferred_element_type=f32)


def over_y(array):
    return lax.ppermute(array, "tensor", across_y)


def over_core(array):
    return lax.ppermute(array, "tensor", across_core)


def over_both(array):
    return lax.ppermute(array, "tensor", across_both)


smem = pl.BlockSpec(memory_space=pltpu.SMEM)
vmem = pl.BlockSpec(memory_space=pltpu.VMEM)
anywhere = pl.BlockSpec(memory_space=pl.ANY)


def piece_of(array, lead):
    return vmem if lead is None else row_of(lead, array.shape)


def row_of(row, shape):
    return pl.BlockSpec((1,) + shape[1:], lambda *_: (row, 0, 0))


def placed(shape, kind, space=None):
    return jax.ShapeDtypeStruct(shape, kind) if space is None else space(shape, kind)


class Order:
    def __init__(self):
        self.last = []

    def after(self, *arrays):
        self.last = self.last + list(arrays)

    def call(self, kernel, name, inputs, in_specs, outputs, room, scratch=(), out_specs=None, grid=(1,), aliases=None):
        count, extra = len(inputs), len(self.last)

        def body(*refs):
            kernel(*refs[:count], *refs[count + extra :])

        results = pl.pallas_call(
            body,
            grid=grid,
            in_specs=list(in_specs) + [anywhere] * extra,
            out_specs=out_specs or [vmem] * len(outputs),
            out_shape=[placed(*output) for output in outputs],
            scratch_shapes=scratch,
            input_output_aliases=aliases or {},
            compiler_params=pltpu.CompilerParams(vmem_limit_bytes=room * MIB),
            cost_estimate=pl.CostEstimate(flops=10**13, bytes_accessed=1024, transcendentals=0),
            name=name,
        )(*inputs, *self.last)
        self.last = [results[0]]
        return results


def norm_factor(rows):
    return lax.rsqrt(jnp.mean(rows * rows, axis=-1, keepdims=True) + epsilon)


def norm_backward(dnormed, rows, gain):
    factor = norm_factor(rows)
    scaled = dnormed * gain
    return factor * (scaled - rows * factor * factor * jnp.mean(scaled * rows, axis=-1, keepdims=True))


def project_kernel(own, other_y, other_core, other_both, gain, weight_t, normed, qkv):
    count = own.shape[1]
    for index, piece in enumerate((own, other_y, other_core, other_both)):
        rows = piece[...].reshape(own.shape[1:]).astype(f32)
        result = (rows * norm_factor(rows) * gain[...]).astype(bf16)
        at = slice(index * count, (index + 1) * count)
        normed[at, :] = result
        qkv[at, :] = dot_nt(result, weight_t[...]).astype(bf16)


def project(order, pieces, gain, weight_t):
    count, width = pieces[0][0].shape[1:]
    return order.call(
        project_kernel,
        "normed_projections",
        (*[array for array, _ in pieces], gain, weight_t),
        [piece_of(*piece) for piece in pieces] + [vmem, vmem],
        [((4 * count, width), bf16), ((4 * count, weight_t.shape[0]), bf16)],
        36,
    )


def bucket_of(offset, buckets):
    magnitude = jnp.abs(offset)
    larger = sum(((magnitude >= edge).astype(jnp.int32) for edge in bucket_edges))
    exact = buckets // 4
    inside = jnp.where(magnitude < exact, magnitude, exact + larger)
    return inside + jnp.where(offset > 0, buckets // 2, 0)


def band_buckets(buckets):
    key = jnp.arange(QUERY_BLOCK + 2 * REACH, dtype=jnp.int32) - REACH
    query = jnp.arange(QUERY_BLOCK, dtype=jnp.int32)
    return bucket_of(key[:, None] - query[None, :], buckets)


def bias_parts(bias, length):
    buckets = bias.shape[0]
    index = band_buckets(buckets)
    wide = bias.astype(f32)
    band = jnp.zeros((bias.shape[1],) + index.shape, f32)
    for bucket in range(buckets):
        band = jnp.where((index == bucket)[None], wide[bucket][:, None, None], band)
    key = jnp.arange(length, dtype=jnp.int32)[:, None]
    block = jnp.arange(LANES, dtype=jnp.int32)[None]
    used = block < length // QUERY_BLOCK
    before = (key < block * QUERY_BLOCK - REACH) & used
    after = (key >= (block + 1) * QUERY_BLOCK + REACH) & used
    far_before = bias[buckets // 2 - 1][:, None, None]
    far_after = bias[buckets - 1][:, None, None]
    far = jnp.where(before[None], far_before, jnp.where(after[None], far_after, jnp.zeros((), bias.dtype)))
    return band, far


def near_keys(block, length):
    low = max(0, block * QUERY_BLOCK - REACH)
    high = min(length, (block + 1) * QUERY_BLOCK + REACH)
    return low, high, low - (block * QUERY_BLOCK - REACH)


def segment_of(position, lengths, row):
    end = jnp.int32(0)
    segment = jnp.zeros(position.shape, jnp.int32)
    for part in range(lengths.shape[1]):
        end = end + lengths[row, part]
        segment = segment + (position >= end).astype(jnp.int32)
    return segment


def fill_masks(lengths, row, masks):
    blocks, length, width = masks.shape
    key_segment = segment_of(lax.broadcasted_iota(jnp.int32, (length, width), 0), lengths, row)
    for block in range(blocks):
        at = lax.broadcasted_iota(jnp.int32, (1, width), 1) + block * width
        masks[block] = jnp.where(key_segment == segment_of(at, lengths, row), 0.0, masked_score)


def relative_block(place, block):
    along_y = jnp.bitwise_xor(place[0], block // 2)
    along_core = jnp.bitwise_xor(place[1], block % 2)
    return along_y + 2 * along_core


def rows_at(index):
    return pl.ds(pl.multiple_of(index * QUERY_BLOCK, QUERY_BLOCK), QUERY_BLOCK)


def block_scores(key_wide, query_wide, mask, band, head, block):
    length = key_wide.shape[0]
    scores = dot_nt(key_wide, query_wide) + mask
    low, high, start = near_keys(block, length)
    parts = []
    if low > 0:
        parts.append(scores[:low])
    parts.append(scores[low:high] + band[head, start : start + high - low])
    if high < length:
        parts.append(scores[high:])
    return jnp.concatenate(parts, axis=0)


def block_indicator(block):
    lane = lax.broadcasted_iota(jnp.int32, (QUERY_BLOCK, LANES), 1)
    return jnp.where(lane == block, 1.0, 0.0).astype(bf16)


def attention_forward_kernel(
    row, place, lengths, qkv, band, far, attended_keep, attended_send, logsum, masks, keys, values, attended
):
    length = qkv.shape[0]
    width = qkv.shape[1] // 3
    fill_masks(lengths, row, masks)
    blocks = length // QUERY_BLOCK
    order = [relative_block(place, block) for block in range(blocks)]
    for block in range(blocks):
        at = slice(block * QUERY_BLOCK, (block + 1) * QUERY_BLOCK)
        keys[at, :] = qkv[rows_at(order[block]), width : 2 * width]
        values[at, :] = qkv[rows_at(order[block]), 2 * width :]
    for head in range(width // DK):
        cols = slice(head * DK, (head + 1) * DK)
        key_wide = jnp.concatenate([keys[:, cols], far[head]], axis=1)
        for block in range(blocks):
            query_wide = jnp.concatenate([qkv[rows_at(order[block]), cols], block_indicator(block)], axis=1)
            scores = block_scores(key_wide, query_wide, masks[block], band, head, block)
            peak = jnp.max(scores, axis=0, keepdims=True)
            expo = jnp.exp(scores - peak)
            total = jnp.sum(expo, axis=0, keepdims=True)
            probs_low = (expo * (1.0 / total)).astype(bf16)
            logsum[head : head + 1, block * QUERY_BLOCK : (block + 1) * QUERY_BLOCK] = peak + jnp.log(total)
            result = dot_tn(probs_low, values[:, cols]).astype(bf16)
            attended[rows_at(order[block]), cols] = result
    attended_keep[...] = attended[: length // 2, :]
    attended_send[...] = attended[length // 2 :, :]


def attention_forward(order, row, place, lengths, qkv, band, far):
    length, width = qkv.shape[0], qkv.shape[1] // 3
    return order.call(
        functools.partial(attention_forward_kernel, row),
        "attention_forward",
        (place, lengths, qkv, band, far),
        [smem, smem, vmem, vmem, vmem],
        [((length // 2, width), bf16), ((length // 2, width), bf16), ((8, length), f32)],
        36,
        scratch=[
            pltpu.VMEM((length // QUERY_BLOCK, length, QUERY_BLOCK), f32),
            pltpu.VMEM((length, width), bf16),
            pltpu.VMEM((length, width), bf16),
            pltpu.VMEM((length, width), bf16),
        ],
    )


def attention_backward_kernel(
    row, place, lengths, qkv, dout_own, dout_y, dout_core, logsum, band, far, weight_t, normed,
    dqkv, dnormed_keep, dnormed_send, band_grad, far_grad, gain_sum,
    masks, keys, values, douts, queries_wide, probs_low, dscores,
):
    length = qkv.shape[0]
    width = qkv.shape[1] // 3
    fill_masks(lengths, row, masks)
    blocks = length // QUERY_BLOCK
    order = [relative_block(place, block) for block in range(blocks)]
    for block, piece in enumerate((dout_own[...], dout_y[0], dout_core[0], dout_core[1])):
        at = slice(block * QUERY_BLOCK, (block + 1) * QUERY_BLOCK)
        keys[at, :] = qkv[rows_at(order[block]), width : 2 * width]
        values[at, :] = qkv[rows_at(order[block]), 2 * width :]
        true_block = 2 * jnp.bitwise_xor(place[0], block % 2) + jnp.bitwise_xor(place[1], block // 2)
        douts[rows_at(true_block), :] = piece
    band_grad[...] = jnp.zeros_like(band_grad)
    far_grad[...] = jnp.zeros_like(far_grad)
    key_at = lax.broadcasted_iota(jnp.int32, (length, LANES), 0)
    block_at = lax.broadcasted_iota(jnp.int32, (length, LANES), 1)
    before = key_at < block_at * QUERY_BLOCK - REACH
    after = key_at >= (block_at + 1) * QUERY_BLOCK + REACH
    for head in range(width // DK):
        cols = slice(head * DK, (head + 1) * DK)
        slot = head % 2
        key_head = keys[:, cols]
        key_wide = jnp.concatenate([key_head, far[head]], axis=1)
        value_head = values[:, cols]
        for block in range(blocks):
            at = slice(block * QUERY_BLOCK, (block + 1) * QUERY_BLOCK)
            query_wide = jnp.concatenate([qkv[rows_at(order[block]), cols], block_indicator(block)], axis=1)
            queries_wide[slot, at, :] = query_wide
            scores = block_scores(key_wide, query_wide, masks[block], band, head, block)
            probs = jnp.exp(scores - logsum[head : head + 1, at])
            weighted = probs * dot_nt(value_head, douts[at, cols])
            inner = jnp.sum(weighted, axis=0, keepdims=True)
            low_dscores = (weighted - probs * inner).astype(bf16)
            probs_low[slot, :, at] = probs.astype(bf16)
            dscores[slot, :, at] = low_dscores
            low, high, start = near_keys(block, length)
            band_grad[head, start : start + high - low] += low_dscores[low:high].astype(f32)
        dvalue = dot_nn(probs_low[slot], douts[:, cols])
        dkey_wide = dot_nn(dscores[slot], queries_wide[slot])
        dquery = dot_nn(key_head.T, dscores[slot]).T
        for block in range(blocks):
            at = slice(block * QUERY_BLOCK, (block + 1) * QUERY_BLOCK)
            for index, part in enumerate((dquery, dkey_wide[:, :DK], dvalue)):
                part_cols = slice(index * width + head * DK, index * width + (head + 1) * DK)
                dqkv[rows_at(order[block]), part_cols] = part[at].astype(bf16)
        sums = dkey_wide[:, DK:]
        far_grad[head : head + 1, :] += jnp.concatenate(
            [
                jnp.sum(jnp.where(before, sums, 0.0), axis=0, keepdims=True),
                jnp.sum(jnp.where(after, sums, 0.0), axis=0, keepdims=True),
            ],
            axis=1,
        )
    total = jnp.zeros((1, normed.shape[1]), f32)
    for half, target in enumerate((dnormed_keep, dnormed_send)):
        for part in range(2):
            at = slice((2 * half + part) * QUERY_BLOCK, (2 * half + part + 1) * QUERY_BLOCK)
            dnormed = dot_nn(dqkv[at, :], weight_t[...])
            target[part * QUERY_BLOCK : (part + 1) * QUERY_BLOCK, :] = dnormed.astype(bf16)
            total = total + jnp.sum(dnormed * normed[at, :].astype(f32), axis=0, keepdims=True)
    gain_sum[...] = total


def attention_backward(order, row, place, lengths, qkv, douts, logsum, band, far, weight_t, normed):
    length, width = qkv.shape[0], qkv.shape[1] // 3
    half = ((length // 2, normed.shape[1]), bf16)
    return order.call(
        functools.partial(attention_backward_kernel, row),
        "attention_backward",
        (place, lengths, qkv, *douts, logsum, band, far, weight_t, normed),
        [smem, smem] + [vmem] * 9,
        [(qkv.shape, bf16, pltpu.HBM), half, half, (band.shape, f32), ((8, 2 * LANES), f32)]
        + [((1, normed.shape[1]), f32)],
        52,
        scratch=[pltpu.VMEM((length // QUERY_BLOCK, length, QUERY_BLOCK), f32)]
        + [pltpu.VMEM((length, width), bf16)] * 3
        + [pltpu.VMEM((2, length, DK + LANES), bf16)]
        + [pltpu.VMEM((2, length, length), bf16)] * 2,
    )


def branch_kernel(heads_0, heads_1, heads_2, heads_3, out_0, out_1, out_2, out_3, own, other_y, gain, middle, normed):
    count = own.shape[1]
    for index, piece in enumerate((own, other_y)):
        here = slice(index * count, (index + 1) * count)
        there = slice((1 - index) * count, (2 - index) * count)
        branch = (
            dot_nn(heads_0[here, :], out_0[...])
            + dot_nn(heads_1[here, :], out_1[...])
            + dot_nn(heads_2[there, :], out_2[...])
            + dot_nn(heads_3[there, :], out_3[...])
        )
        rows = piece[...].reshape(branch.shape).astype(f32) + branch
        if index == 0:
            middle[...] = rows
        normed[here, :] = (rows * norm_factor(rows) * gain[...]).astype(bf16)


def attention_branch(order, heads, out_parts, own, other_y, gain):
    count, width = own[0].shape[1:]
    return order.call(
        branch_kernel,
        "attention_branch",
        (*heads, *out_parts, own[0], other_y[0], gain),
        [vmem] * 8 + [piece_of(*own), piece_of(*other_y), vmem],
        [((count, width), f32), ((2 * count, width), bf16)],
        28,
    )


def branch_backward_kernel(
    keep, received, from_y, middle, out_grad, gain, out_0, out_1, out_2, out_3,
    dmiddle, dbranch, gain_sum, douts_own, douts_core, douts_y,
):
    dnormed = summed(keep, received, from_y)
    rows = middle[...]
    result = out_grad[0].astype(f32) + norm_backward(dnormed, rows, gain[...])
    dmiddle[...] = result
    low = result.astype(bf16)
    dbranch[...] = low
    gain_sum[...] = jnp.sum(dnormed * rows * norm_factor(rows), axis=0, keepdims=True)
    douts_own[...] = dot_nt(low, out_0[...]).astype(bf16)
    douts_core[...] = dot_nt(low, out_1[...]).astype(bf16)
    douts_y[0] = dot_nt(low, out_2[...]).astype(bf16)
    douts_y[1] = dot_nt(low, out_3[...]).astype(bf16)


def branch_backward(order, row, keep, received, from_y, middle, out_grad, gain, out_parts):
    count, width = middle.shape
    first = pl.BlockSpec((count, width), lambda *_: (0, 0))
    return order.call(
        branch_backward_kernel,
        "branch_backward",
        (keep, received, from_y, middle, out_grad, gain, *out_parts),
        [first, pl.BlockSpec((1, count, width), lambda *_: (0, 0, 0)), vmem, vmem, row_of(row, out_grad.shape)]
        + [vmem] * 5,
        [((count, width), f32), ((count, width), bf16), ((1, width), f32)]
        + [((count, out_parts[0].shape[0]), bf16)] * 2
        + [((2, count, out_parts[0].shape[0]), bf16)],
        24,
    )


def outproj_grad_kernel(rows, *refs):
    heads, branches, (keep, send) = refs[: 4 * rows], refs[4 * rows : 5 * rows], refs[5 * rows :]
    count = branches[0].shape[0]
    for index in range(4):
        total = None
        for row in range(rows):
            at = slice((index // 2) * count, (index // 2 + 1) * count)
            part = dot_tn(heads[4 * row + index][at, :], branches[row][...])
            total = part if total is None else total + part
        target = keep if index % 2 == 0 else send
        target[index // 2] = total.astype(bf16)


def outproj_grad(order, heads, branches):
    rows, width, cols = len(branches), branches[0].shape[1], heads[0].shape[1]
    return order.call(
        functools.partial(outproj_grad_kernel, rows),
        "outproj_gradient",
        (*heads, *branches),
        [vmem] * (5 * rows),
        [((2, cols, width), bf16)] * 2,
        24,
    )


def feed_kernel(chunk, blocks, leads, normed_keep, normed_recv, *refs):
    count = len(blocks)
    grads_hbm, (gate_hbm, up_hbm, down_hbm), refs = refs[:count], refs[count : count + 3], refs[count + 3 :]
    refs = refs[-12:]
    hidden_ref, dgate_ref, dup_ref, dnormed_keep, feed_keep, sends = refs[:6]
    gate_t, up_t, down, grads, weight_sem, grad_sem = refs[6:]
    step = pl.program_id(0)
    units = down.shape[0]
    chunks = [slice(start, min(units, start + chunk)) for start in range(0, units, chunk)]
    kept = sum(block < 2 for block in blocks)

    def weight_copies(index):
        at = pl.ds(chunks[index].start, chunks[index].stop - chunks[index].start)
        pairs = ((gate_hbm, gate_t), (up_hbm, up_t), (down_hbm, down))
        return [
            pltpu.make_async_copy(source.at[at], target.at[at], weight_sem.at[index, which])
            for which, (source, target) in enumerate(pairs)
        ]

    def grad_copy(index):
        source = grads_hbm[index] if leads[index] is None else grads_hbm[index].at[leads[index]]
        return pltpu.make_async_copy(source, grads.at[index], grad_sem.at[index])

    def work(first):
        normed = jnp.where(step < kept, normed_keep[...], normed_recv[...])
        grad = grads[step]
        for index, at in enumerate(chunks):
            if first:
                for copy in weight_copies(index):
                    copy.wait()
            values = gated_products(normed, grad, gate_t[at, :], up_t[at, :], down[at, :])
            hidden_ref[:, at], dgate_ref[:, at], dup_ref[:, at] = values
        for ref in (dgate_ref, dup_ref):
            ref[:, units:] = jnp.zeros((ref.shape[0], ref.shape[1] - units), bf16)
        dnormed = dot_nn(dgate_ref[:, :units], gate_t[...]) + dot_nn(dup_ref[:, :units], up_t[...])
        dnormed = dnormed.astype(bf16)
        feed = dot_nn(hidden_ref[...], down[...]).astype(bf16)

        @pl.when(step < kept)
        def _():
            dnormed_keep[...] = dnormed
            feed_keep[...] = feed

        @pl.when(step >= kept)
        def _():
            sends[0] = dnormed
            sends[1] = feed

    @pl.when(step == 0)
    def _():
        for index in range(len(chunks)):
            for copy in weight_copies(index):
                copy.start()
            if index == 0:
                grad_copy(0).start()
        for index in range(1, count):
            grad_copy(index).start()
        grad_copy(0).wait()
        work(True)

    @pl.when(step > 0)
    def _():
        for index in range(1, count):
            pl.when(step == index)(grad_copy(index).wait)
        work(False)


def feed_forward(order, normed_keep, normed_recv, blocks, grads, gate_t, up_t, down, before=()):
    units, width = down.shape
    length = 2 * normed_keep.shape[0]
    count = length // 4
    if len(blocks) == 4:
        kept_at, sent_at, at = (lambda s: jnp.minimum(s, 1)), (lambda s: jnp.maximum(s - 2, 0)), (lambda s: s)
    else:
        low, high = blocks
        kept_at = sent_at = lambda s: low
        at = lambda s: low + s * (high - low)
    first = pl.BlockSpec((count, width), lambda step: (kept_at(step), 0))
    last = pl.BlockSpec((count, width), lambda step: (sent_at(step), 0))
    pair = pl.BlockSpec((2, count, width), lambda step: (0, sent_at(step), 0))
    each = pl.BlockSpec((count, units), lambda step: (at(step), 0))
    wide = -(-units // 128) * 128
    padded = pl.BlockSpec((count, wide), lambda step: (at(step), 0))
    half = ((length // 2, width), bf16)
    chunk = 256
    inputs = 5 + len(grads)
    return order.call(
        functools.partial(feed_kernel, chunk, blocks, [lead for _, lead in grads]),
        "feed_forward",
        (normed_keep, normed_recv, *[array for array, _ in grads], gate_t, up_t, down, *before),
        [first, last] + [anywhere] * (inputs - 2 + len(before)),
        [((length, units), bf16, pltpu.HBM)]
        + [((length, wide), bf16, pltpu.HBM)] * 2
        + [half, half, ((2, length // 2, width), bf16)],
        44,
        out_specs=[each, padded, padded, first, first, pair],
        grid=(len(blocks),),
        scratch=[pltpu.VMEM((units, width), bf16)] * 3
        + [
            pltpu.VMEM((len(blocks), count, width), bf16),
            pltpu.SemaphoreType.DMA((-(-units // chunk), 3)),
            pltpu.SemaphoreType.DMA((len(blocks),)),
        ],
        aliases={inputs + index: index for index in range(len(before))},
    )


def gated_products(normed, grad, gate, up, down):
    gate = dot_nt(normed, gate)
    up = dot_nt(normed, up)
    dhidden = dot_nt(grad, down)
    square = gate * gate
    bend = jnp.tanh(gelu_scale * gate * (1.0 + gelu_cubic * square))
    half = 0.5 * (1.0 + bend)
    active = gate * half
    slope = half + (0.5 * gelu_scale) * gate * (1.0 - bend * bend) * (1.0 + (3 * gelu_cubic) * square)
    return (active * up).astype(bf16), (dhidden * up * slope).astype(bf16), (dhidden * active).astype(bf16)


def feed_last_kernel(chunk, pieces, rows, bits, place, *refs):
    count = sum(map(len, pieces))
    arrays, refs = refs[:count], refs[count:]
    earlier, refs = refs[: 3 * (rows - 1)], refs[3 * (rows - 1) :]
    (gate_hbm, up_hbm, down_hbm), refs = refs[:3], refs[3:]
    (dnormed_keep, feed_keep, sends), outs, refs = refs[:3], refs[3:9], refs[9:]
    gate_t, up_t, down, normed, grads, hidden, dgate, dup, stage = refs[:9]
    weight_sem, left_sem, right_sem, out_sem = refs[9:]
    step = pl.program_id(0)
    units = down.shape[0]
    chunks = [slice(start, min(units, start + chunk)) for start in range(0, units, chunk)]
    length = normed.shape[0] // rows
    block = length // 4
    base = (rows - 1) * length

    def weight_copies(index):
        at = pl.ds(chunks[index].start, chunks[index].stop - chunks[index].start)
        pairs = ((gate_hbm, gate_t), (up_hbm, up_t), (down_hbm, down))
        return [
            pltpu.make_async_copy(source.at[at], target.at[at], weight_sem.at[index, which])
            for which, (source, target) in enumerate(pairs)
        ]

    def left_copies(side):
        copies = []
        taken = sum(map(len, pieces[:side]))
        at = 0
        for index, lead in enumerate(pieces[side]):
            source = arrays[taken + index]
            source = source if lead is None else source.at[lead]
            copies.append(
                (
                    at,
                    pltpu.make_async_copy(
                        source, (normed, grads)[side].at[pl.ds(at, source.shape[0])], left_sem.at[side, index]
                    ),
                )
            )
            at += source.shape[0]
        return copies

    def right_copies():
        return [
            pltpu.make_async_copy(
                earlier[3 * row + which], target.at[pl.ds(row * length, length)], right_sem.at[row, which]
            )
            for row in range(rows - 1)
            for which, target in enumerate((hidden, dgate, dup))
        ]

    def work(first):
        at = pl.ds(pl.multiple_of(base + step * block, block), block)
        rows_normed, rows_grad = normed[at, :], grads[at, :]
        for index, part in enumerate(chunks):
            if first:
                for copy in weight_copies(index):
                    copy.wait()
            values = gated_products(rows_normed, rows_grad, gate_t[part, :], up_t[part, :], down[part, :])
            for target, value in zip((hidden, dgate, dup), values):
                target[at, part] = value
        dnormed = dot_nn(dgate[at, :units], gate_t[...]) + dot_nn(dup[at, :units], up_t[...])
        dnormed = dnormed.astype(bf16)
        feed = dot_nn(hidden[at, :], down[...]).astype(bf16)

        @pl.when(step < 2)
        def _():
            dnormed_keep[...] = dnormed
            feed_keep[...] = feed

        @pl.when(step >= 2)
        def _():
            sends[0] = dnormed
            sends[1] = feed

    def gradients():
        width = normed.shape[1]
        chunk_rows = outs[0].shape[1]
        tile = width // 2
        half_rows = tile // 2
        half_chunks = half_rows // chunk_rows
        sending = {}
        turn = 0
        for product, (left, right) in enumerate(((grads, hidden), (normed, dgate), (normed, dup))):
            bit = bits[product]
            for part in range(2):
                slot = turn % 2
                turn += 1
                for copy in sending.get(slot, ()):
                    copy.wait()
                for half in range(2):
                    cols = slice(part * tile + half * half_rows, part * tile + (half + 1) * half_rows)
                    value = dot_tn(left[:, cols], right[:, :units]).reshape(half_chunks, chunk_rows, units)
                    stage[slot, half * half_chunks : (half + 1) * half_chunks] = value.astype(bf16)
                sending[slot] = []
                for index in range(half_chunks):
                    low = index % (1 << bit)
                    first_chunk = (index - low) * 2 + low
                    for side, which in enumerate((place[2 + bit], 1 - place[2 + bit])):
                        copy = pltpu.make_async_copy(
                            stage.at[slot, first_chunk + which * (1 << bit)],
                            outs[2 * product + side].at[part * half_chunks + index],
                            out_sem.at[product, side, part * half_chunks + index],
                        )
                        copy.start()
                        sending[slot].append(copy)
        for copies in sending.values():
            for copy in copies:
                copy.wait()

    @pl.when(step == 0)
    def _():
        mine = [[copy for at, copy in left_copies(side) if at >= base] for side in range(2)]
        for index in range(len(chunks)):
            for copy in weight_copies(index):
                copy.start()
            if index == 0:
                mine[0][0].start()
                mine[1][0].start()
        for copies in mine:
            for copy in copies[1:]:
                copy.start()
        mine[0][0].wait()
        mine[1][0].wait()
        work(True)

    @pl.when(step == 1)
    def _():
        for side in range(2):
            for at, copy in left_copies(side):
                if at < base:
                    copy.start()
                elif at > base:
                    copy.wait()
        for copy in right_copies():
            copy.start()

    pl.when(step > 0)(lambda: work(False))

    @pl.when(step == 3)
    def _():
        for side in range(2):
            for at, copy in left_copies(side):
                if at < base:
                    copy.wait()
        for copy in right_copies():
            copy.wait()
        gradients()


def feed_last(order, place, lefts, earlier, gate_t, up_t, down, bits):
    units, width = down.shape
    size = lax.axis_size("dp")
    rows = len(earlier) + 1
    length = 4 * lefts[1][-1][0].shape[-2]
    count = length // 4
    first = pl.BlockSpec((count, width), lambda step: (jnp.minimum(step, 1), 0))
    pair = pl.BlockSpec((2, count, width), lambda step: (0, jnp.maximum(step - 2, 0), 0))
    half = ((length // 2, width), bf16)
    chunk = 256
    chunk_rows = width // size
    wide = -(-units // 128) * 128
    plan = [[lead for _, lead in side] for side in lefts]
    inputs = [array for side in lefts for array, _ in side] + [array for row in earlier for array in row]
    return order.call(
        functools.partial(feed_last_kernel, chunk, plan, rows, bits),
        "feed_forward_and_gradients",
        (place, *inputs, gate_t, up_t, down),
        [smem] + [anywhere] * (len(inputs) + 3),
        [half, half, ((2, length // 2, width), bf16)] + [((size // 2, chunk_rows, units), bf16)] * 6,
        50,
        out_specs=[first, first, pair] + [anywhere] * 6,
        grid=(4,),
        scratch=[pltpu.VMEM((units, width), bf16)] * 3
        + [pltpu.VMEM((rows * length, width), bf16)] * 2
        + [pltpu.VMEM((rows * length, units), bf16)]
        + [pltpu.VMEM((rows * length, wide), bf16)] * 2
        + [pltpu.VMEM((2, size // 2, chunk_rows, units), bf16)]
        + [
            pltpu.SemaphoreType.DMA((-(-units // chunk), 3)),
            pltpu.SemaphoreType.DMA((2, max(map(len, lefts)))),
            pltpu.SemaphoreType.DMA((max(rows - 1, 1), 3)),
            pltpu.SemaphoreType.DMA((3, 2, size // 2)),
        ],
    )


def halves(parts, stride, bit):
    count, rows, width = parts.shape
    pairs = parts.reshape(count // (2 * stride), 2, stride, rows, width)
    low, high = pairs[:, 0], pairs[:, 1]
    shape = (count // 2, rows, width)
    return jnp.where(bit == 0, low, high).reshape(shape), jnp.where(bit == 0, high, low).reshape(shape)


def gradient_kernel(groups, products, extra, cuts, place, *refs):
    rows = len(groups)
    extras, refs = refs[:extra], refs[extra:]
    pieces = sum(map(len, groups))
    lefts, refs = refs[:pieces], refs[pieces:]
    rights_hbm, refs = refs[: products * rows], refs[products * rows :]
    outs, refs = refs[: 2 * len(cuts)], refs[2 * len(cuts) :]
    stages, (left, right, left_sem, right_sem, out_sem) = refs[: len(cuts)], refs[len(cuts) :]
    steps = left.shape[0]
    tile = left.shape[2]
    length = right.shape[0] // rows
    cols = rights_hbm[0].shape[1]

    def left_copies(row, step):
        part = pl.ds(step * tile, tile)
        taken = sum(map(len, groups[:row]))
        copies = []
        at = row * length
        for index, lead in enumerate(groups[row]):
            source = lefts[taken + index]
            source = source if lead is None else source.at[lead]
            count = source.shape[0]
            copies.append(
                pltpu.make_async_copy(
                    source.at[:, part], left.at[step, pl.ds(at, count)], left_sem.at[step, row, index]
                )
            )
            at += count
        return copies

    def right_copy(product, row):
        index = product * rows + row
        return pltpu.make_async_copy(
            rights_hbm[index],
            right.at[pl.ds(row * length, length), pl.ds(product * cols, cols)],
            right_sem.at[index],
        )

    first = [[right_copy(product, row) for product in range(products)] + left_copies(row, 0) for row in range(rows)]
    later = [[copy for row in range(rows) for copy in left_copies(row, step)] for step in range(1, steps)]
    for group in first + later:
        for copy in group:
            copy.start()

    part_rows = tile // 2
    sending = []
    for step in range(steps):
        slot = step % 2
        sums = [None, None]
        spans = [slice(row * length, (row + 1) * length) for row in range(rows)] if step == 0 else [slice(None)]
        for span, group in zip(spans, first if step == 0 else [later[step - 1]]):
            for copy in group:
                copy.wait()
            for half in range(2):
                rows_at = slice(half * part_rows, (half + 1) * part_rows)
                part = dot_tn(left[step, span, rows_at], right[span, :])
                sums[half] = part if sums[half] is None else sums[half] + part
        for half in range(2):
            rows_at = slice(half * part_rows, (half + 1) * part_rows)
            total = sums[half]
            totals = [total[:, product * cols : (product + 1) * cols] for product in range(products)]
            if extra:
                turned_at = slice(step * tile + rows_at.start, step * tile + rows_at.stop)
                totals.append(sum(ref[0, :, turned_at].astype(f32) for ref in extras).T)
            for index, (parts, bit) in enumerate(cuts):
                chunk_rows = outs[2 * index].shape[1]
                count = part_rows // chunk_rows
                chunks = slice(half * count, (half + 1) * count)
                taken = [totals[which][:, where] for which, where in parts]
                value = taken[0] if len(taken) == 1 else jnp.concatenate(taken, axis=1)
                stages[index][slot, chunks] = value.reshape(count, chunk_rows, value.shape[1]).astype(bf16)
        for index, (parts, bit) in enumerate(cuts):
            chunk_rows = outs[2 * index].shape[1]
            mine = place[2 + bit]
            count = tile // chunk_rows // 2
            for chunk in range(count):
                low = chunk % (1 << bit)
                base = (chunk - low) * 2 + low
                for side, which in enumerate((mine, 1 - mine)):
                    copy = pltpu.make_async_copy(
                        stages[index].at[slot, base + which * (1 << bit)],
                        outs[2 * index + side].at[step * count + chunk],
                        out_sem.at[index, side, step * count + chunk],
                    )
                    copy.start()
                    sending.append(copy)
    for copy in sending:
        copy.wait()


def gradient(order, name, place, lefts, rights, cuts, extras=()):
    size = lax.axis_size("dp")
    length, cols = rights[0][0].shape
    width = lefts[0][0][0].shape[-1]
    steps = 2
    tile = width // steps
    chunk_rows = width // size
    pieces = [piece for group in lefts for piece in group]
    rows = len(lefts)
    flat = [array for group in rights for array in group]
    widths = [sum(at.stop - at.start for _, at in parts) for parts, _ in cuts]
    plan = [[lead for _, lead in group] for group in lefts]
    results = order.call(
        functools.partial(gradient_kernel, plan, len(rights), len(extras), cuts),
        name,
        (place, *extras, *[array for array, _ in pieces], *flat),
        [smem]
        + [pl.BlockSpec((1,) + extra.shape[1:], lambda *_: (0, 0, 0)) for extra in extras]
        + [anywhere] * (len(pieces) + len(flat)),
        [((size // 2, chunk_rows, w), bf16) for w in widths for _ in range(2)],
        52,
        out_specs=[anywhere] * (2 * len(widths)),
        scratch=[pltpu.VMEM((2, size // steps, chunk_rows, w), bf16) for w in widths]
        + [
            pltpu.VMEM((steps, rows * length, tile), bf16),
            pltpu.VMEM((rows * length, len(rights) * cols), bf16),
            pltpu.SemaphoreType.DMA((steps, rows, max(map(len, lefts)))),
            pltpu.SemaphoreType.DMA((len(flat),)),
            pltpu.SemaphoreType.DMA((len(cuts), 2, size // 2)),
        ],
    )
    return [results[2 * index : 2 * index + 2] for index in range(len(cuts))]


def exchange(sent, bit):
    return lax.ppermute(sent, "dp", [(i, i ^ (1 << bit)) for i in range(lax.axis_size("dp"))])


def halve_kernel(plans, place, *refs):
    count = sum(map(len, plans))
    inputs, outputs = refs[: 2 * count], refs[2 * count :]
    taken = 0
    for index, plan in enumerate(plans):
        keep_ref, send_ref = outputs[2 * index : 2 * index + 2]
        at = 0
        for stride, bit in plan:
            kept, received = inputs[2 * taken : 2 * taken + 2]
            taken += 1
            parts = kept[...].astype(f32) + received[...].astype(f32)
            keep, send = halves(parts, stride, place[2 + bit])
            cols = slice(at, at + parts.shape[2])
            keep_ref[:, :, cols] = keep.astype(bf16)
            send_ref[:, :, cols] = send.astype(bf16)
            at += parts.shape[2]


def total_kernel(*refs):
    count = 0
    while count < len(refs) and len(refs[count].shape) == 3:
        count += 1
    outs = list(refs[count:])
    for index in range(count // 2):
        total = refs[2 * index][0].astype(f32) + refs[2 * index + 1][0].astype(f32)
        at = 0
        while at < total.shape[1]:
            out = outs.pop(0)
            out[...] = total[:, at : at + out.shape[1]]
            at += out.shape[1]


class Scatter:
    def __init__(self, first, parts, last=False, widths=None):
        count = lax.axis_size("dp").bit_length() - 1
        self.bits = [first] + [bit for bit in range(count) if bit != first]
        if last:
            self.bits = self.bits[:1] + self.bits[2:] + self.bits[1:2]
        self.left = sorted(self.bits)
        self.widths = widths or [parts[0].shape[2]]
        self.send(*parts)

    def send(self, kept, sent):
        bit = self.bits.pop(0)
        self.left.remove(bit)
        self.parts = kept, exchange(sent, bit)


def halve(order, place, *groups):
    groups = [group if isinstance(group, tuple) else (group,) for group in groups]
    plans = [[(1 << scatter.left.index(scatter.bits[0]), scatter.bits[0]) for scatter in group] for group in groups]
    flat = [scatter for group in groups for scatter in group]
    shapes = [
        (group[0].parts[0].shape[0] // 2, group[0].parts[0].shape[1], sum(s.parts[0].shape[2] for s in group))
        for group in groups
    ]
    results = order.call(
        functools.partial(halve_kernel, plans),
        "halve",
        (place, *[part for scatter in flat for part in scatter.parts]),
        [smem] + [vmem] * (2 * len(flat)),
        [(shape, bf16) for shape in shapes for _ in range(2)],
        24,
    )
    for index, group in enumerate(groups):
        for other in group[1:]:
            assert group[0].left == other.left
            group[0].widths += other.widths
        group[0].send(*results[2 * index : 2 * index + 2])


def finish(order, *scatters):
    for scatter in scatters:
        assert not scatter.bits, scatter.bits
    return order.call(
        total_kernel,
        "gradient_output",
        [part for scatter in scatters for part in scatter.parts],
        [vmem] * (2 * len(scatters)),
        [
            ((scatter.parts[0].shape[1], width), f32, pltpu.HBM) for scatter in scatters for width in scatter.widths
        ],
        16,
    )


def pass_kernel(*refs):
    for keep, received, out in zip(refs[0::2], refs[1::2], refs[-(len(refs) // 3) :]):
        out[...] = (keep[...].reshape(out.shape).astype(f32) + received[...].reshape(out.shape).astype(f32)).astype(bf16)


def pass_on(order, keep, received, lead=None):
    count, width = keep.shape[0] // 2, keep.shape[1]
    second = pl.BlockSpec((count, width), lambda *_: (1, 0))
    other = second if lead is None else pl.BlockSpec((1, count, width), lambda *_: (lead, 1, 0))
    return over_y(
        order.call(pass_kernel, "pass_on", (keep, received), [second, other], [((count, width), bf16)], 8)[0]
    )


def pass_rows_kernel(*refs):
    out = refs[-1]
    for row in range(out.shape[0]):
        received = refs[2 * row + 1][...].reshape(out.shape[1:])
        out[row] = (refs[2 * row][...].astype(f32) + received.astype(f32)).astype(bf16)


def pass_rows(order, parts, lead=None):
    count, width = parts[0][0].shape[0] // 2, parts[0][0].shape[1]
    second = pl.BlockSpec((count, width), lambda *_: (1, 0))
    other = second if lead is None else pl.BlockSpec((1, count, width), lambda *_: (lead, 1, 0))
    return over_y(
        order.call(
            pass_rows_kernel,
            "pass_on",
            [array for pair in parts for array in pair],
            [second, other] * len(parts),
            [((len(parts), count, width), bf16)],
            12,
        )[0]
    )


def outproj_pass(order, keep, received):
    shape = keep.shape[1:]
    second = pl.BlockSpec((1,) + shape, lambda *_: (1, 0, 0))
    return over_y(order.call(pass_kernel, "pass_on", (keep, received), [second] * 2, [((1,) + shape, bf16)], 8)[0])


def join_kernel(bit, place, mine, received, out):
    count = mine.shape[0]
    which = place[2 + bit]
    out[pl.ds(pl.multiple_of(which * count, 16), count), :] = mine[...]
    out[pl.ds(pl.multiple_of((1 - which) * count, 16), count), :] = received[...]


def join(order, place, bit, mine, received):
    shape = (2 * mine.shape[0],) + mine.shape[1:]
    return order.call(
        functools.partial(join_kernel, bit), "join", (place, mine, received), [smem, vmem, vmem], [(shape, mine.dtype)], 8
    )[0]


def pause_kernel(out):
    out[...] = jnp.zeros_like(out)


def pause(order):
    order.call(pause_kernel, "pause", (), [], [((8, 128), f32)], 4)


def fence(order, *arrays):
    return order.call(
        lambda *_: None,
        "fence",
        arrays,
        [anywhere] * len(arrays),
        [(array.shape, array.dtype) for array in arrays],
        4,
        out_specs=[anywhere] * len(arrays),
        aliases={index: index for index in range(len(arrays))},
    )


def relay_kernel(source, target):
    target[...] = source[0] if len(source.shape) == 3 else source[...]


def relay(order, array, row=None):
    shape = array.shape if row is None else array.shape[1:]
    spec = vmem if row is None else row_of(row, array.shape)
    return order.call(relay_kernel, "relay", (array,), [spec], [(shape, array.dtype)], 8)[0]


def summed(keep, received, from_y):
    shape = keep.shape
    return sum(ref[...].reshape(shape).astype(f32) for ref in (keep, received, from_y))


def block_out_kernel(rows, *refs):
    out = refs[-1]
    for row in range(rows):
        middle, keep, received, from_y = refs[4 * row : 4 * row + 4]
        out[row] = middle[...] + summed(keep, received, from_y)


def block_output(order, middles, feeds, from_y):
    rows = len(from_y)
    count, width = from_y[0].shape
    first = pl.BlockSpec((count, width), lambda *_: (0, 0))
    other = pl.BlockSpec((1, count, width), lambda *_: (1, 0, 0))
    return order.call(
        functools.partial(block_out_kernel, rows),
        "block_output",
        [array for row in range(rows) for array in (middles[row], *feeds[row], from_y[row])],
        [vmem, first, other, vmem] * rows,
        [((rows, count, width), f32, pltpu.HBM)],
        30,
    )[0]


def input_grad_kernel(rows, from_y, inputs, gain, *refs):
    out = refs[-1]
    for row in range(rows):
        dmiddle, keep, received = refs[3 * row : 3 * row + 3]
        dnormed = summed(keep, received, from_y.at[row])
        out[row] = dmiddle[...] + norm_backward(dnormed, inputs[row].astype(f32), gain[...])


def input_gradient(order, dmiddles, inner, from_y, inputs, gain):
    rows, count, width = from_y.shape
    first = pl.BlockSpec((count, width), lambda *_: (0, 0))
    return order.call(
        functools.partial(input_grad_kernel, rows),
        "input_gradient",
        [from_y, inputs, gain] + [array for row in range(rows) for array in (dmiddles[row], *inner[row])],
        [vmem] * 3 + [vmem, first, first] * rows,
        [(from_y.shape, f32, pltpu.HBM)],
        36,
    )[0]


def small_kernel(heads, rows, buckets, place, gain, *refs):
    norms_one, norms_two, out = refs[:rows], refs[rows : 2 * rows], refs[-1]
    bands, fars = refs[2 * rows : 3 * rows], refs[3 * rows : 4 * rows]
    lines = gain.shape[1] // 128
    ones = sum(ref[...] for ref in norms_one) / gain[...]
    twos = sum(ref[...] for ref in norms_two)
    for index, vector in enumerate((ones, twos)):
        for line in range(lines):
            out[index * lines + line : index * lines + line + 1, :] = vector[:, line * 128 : (line + 1) * 128]
    side = REACH
    tiles = {}
    for key_block in range(bands[0].shape[1] // side):
        for query_block in range(bands[0].shape[2] // side):
            tiles.setdefault(key_block - 1 - query_block, []).append((key_block, query_block))
    row_at = lax.broadcasted_iota(jnp.int32, (side, side), 0)
    col_at = lax.broadcasted_iota(jnp.int32, (side, side), 1)
    lane = lax.broadcasted_iota(jnp.int32, (1, 128), 1)
    mine = lane == place[1] + 2 * place[0]
    which = lax.broadcasted_iota(jnp.int32, (buckets, 1), 0)
    for head in range(heads):
        sums = [jnp.zeros((1, side), f32) for _ in range(buckets)]
        for distance, blocks in tiles.items():
            grads = sum(
                band[head, key * side : (key + 1) * side, query * side : (query + 1) * side]
                for band in bands
                for key, query in blocks
            )
            index = bucket_of(row_at - col_at + distance * side, buckets)
            near = abs(distance) < 2
            for bucket in range(buckets):
                after = bucket >= buckets // 2
                if (near or bucket in (buckets // 2 - 1, buckets - 1)) and (distance == 0 or after == (distance > 0)):
                    sums[bucket] += jnp.sum(jnp.where(index == bucket, grads, 0.0), axis=0, keepdims=True)
        far = sum(ref[head : head + 1, :] for ref in fars)
        total = jnp.sum(jnp.concatenate(sums, axis=0), axis=1, keepdims=True)
        total = total + jnp.where(which == buckets // 2 - 1, jnp.sum(far[:, :LANES], axis=1, keepdims=True), 0.0)
        total = total + jnp.where(which == buckets - 1, jnp.sum(far[:, LANES:], axis=1, keepdims=True), 0.0)
        at = 2 * lines + head * buckets
        out[at : at + buckets, :] = jnp.where(mine, total, 0.0)


def small_gradients(order, place, heads, buckets, gain, norms_one, norms_two, bands, fars):
    lines = gain.shape[1] // 128
    rows = len(norms_one)
    return order.call(
        functools.partial(small_kernel, heads, rows, buckets),
        "small_gradients",
        (place, gain, *norms_one, *norms_two, *bands, *fars),
        [smem] + [vmem] * (1 + 4 * rows),
        [((2 * lines + heads * buckets, 128), f32)],
        16,
    )[0]


def add_kernel(*refs):
    refs[-1][...] = sum(ref[...] for ref in refs[:-1])


def add_all(order, arrays):
    return order.call(add_kernel, "small_sum", arrays, [vmem] * len(arrays), [(arrays[0].shape, f32)], 4)[0]


def small_rounds(order, vector):
    count = lax.axis_size("dp").bit_length() - 1
    sends = [over_core, over_y] + [functools.partial(exchange, bit=bit) for bit in range(count)]
    for send in sends:
        moved = send(vector)
        yield None
        vector = add_all(order, [vector, moved])
    yield vector


def per_device(
    block_input,
    out_grad,
    seg_lengths,
    norm1_gain,
    norm2_gain,
    rel_bias,
    w_query,
    w_key,
    w_value,
    w_out,
    w_gate,
    w_up,
    w_down,
):
    rows, count, width = block_input.shape
    length = 4 * count
    here = lax.axis_index("tensor")
    dp_bits = lax.axis_size("dp").bit_length() - 1
    dp_at = lax.axis_index("dp")
    place = jnp.stack([here // 2, here % 2] + [(dp_at >> bit) & 1 for bit in range(dp_bits)]).astype(jnp.int32)
    head_width = w_query.shape[1]
    heads = head_width // DK
    buckets = rel_bias.shape[0]
    gain_one = norm1_gain.astype(f32)[None]
    gain_two = norm2_gain.astype(f32)[None]
    first_head = here * heads
    weight_t = jnp.concatenate([w_query.T, w_key.T, w_value.T], axis=0)
    gate_t, up_t = w_gate.T, w_up.T

    order = Order()
    every_row = range(rows)
    last_row = rows - 1

    band, far = bias_parts(lax.dynamic_slice_in_dim(rel_bias, first_head, heads, 1), length)
    order.after(band, far, weight_t)
    first_y = over_y(block_input[0])
    input_core = over_core(block_input)
    grad_core = over_core(out_grad)
    out_core = over_core(w_out)
    input_y, input_both = [(first_y, None)], [(over_core(first_y), None)]
    grad_y, grad_both = [], []
    bits = (1, 2)
    quarter = w_out.shape[0] // 4
    out_at = (place[2 + bits[0]] + 2 * place[2 + bits[1]]) * quarter
    out_y = over_y(lax.dynamic_slice_in_dim(w_out, out_at, quarter, 0))
    order.after(input_core, grad_core, out_core)
    order.after(first_y)
    for row in range(1, rows):
        input_y.append((over_y(relay(order, block_input, row)), None))
    grad_y.append((over_y(relay(order, out_grad, 0)), None))
    out_y = (out_y, exchange(out_y, bits[0]))

    normed_one, qkvs, logsums, attended, middles = [], [], [], [], []
    normed_keeps, normed_recvs = [], []

    def second_norm(row):
        middle, normed_keep = attention_branch(
            order, attended[row], out_parts, (block_input, row), input_y[row], gain_two
        )
        middles.append(middle)
        normed_keeps.append(normed_keep)
        normed_recvs.append(over_core(normed_keep))

    def heads_arrived(row, other):
        (other,) = fence(order, other)
        attended[row][1], attended[row][3] = other, over_y(other)

    for row in every_row:
        if row == 0:
            out_y = join(order, place, bits[0], *out_y)
            out_y = (out_y, exchange(out_y, bits[1]))
        if row == 1:
            first_other = other
        normed, qkv = project(
            order, [(block_input, row), input_y[row], (input_core, row), input_both[row]], gain_one, weight_t
        )
        if row == 1:
            heads_arrived(0, first_other)
        keep, send, logsum = attention_forward(order, row, place, seg_lengths, qkv, band, far)
        normed_one.append(normed)
        qkvs.append(qkv)
        logsums.append(logsum)
        attended.append([keep, None, over_y(keep), None])
        if row == 0:
            (next_y,) = fence(order, input_y[1][0])
            input_y[1] = (next_y, None)
            input_both.append((over_core(next_y), None))
            out_y = join(order, place, bits[1], *out_y)
            out_parts = [w_out, out_core, out_y, over_core(out_y)]
            (send,) = fence(order, send)
        other = over_core(send)

    (first_grad,) = fence(order, grad_y[0][0])
    grad_y[0] = (first_grad, None)
    grad_both.append((over_core(first_grad), None))
    second_norm(0)
    heads_arrived(1, other)
    for row in range(1, rows):
        grad_y.append((over_y(relay(order, out_grad, row)), None))

    hiddens, dgates, dups, dnormed, feeds = [], [], [], [], []

    def feed(row):
        pieces = [(out_grad, row), grad_y[row], (grad_core, row), grad_both[row]]
        return feed_forward(
            order, normed_keeps[row], normed_recvs[row], (0, 1, 2, 3), pieces, gate_t, up_t, w_down
        )

    def fed(hidden, dgate, dup, dn_keep, ff_keep, sends):
        hiddens.append(hidden)
        dgates.append(dgate)
        dups.append(dup)
        received = over_core(sends)
        dnormed.append([dn_keep, received])
        feeds.append([ff_keep, received])

    fed(*feed(0))
    for row in range(1, rows):
        second_norm(row)
        grad_y[row] = (fence(order, grad_y[row][0])[0], None)
        grad_both.append((over_core(grad_y[row][0]), None))
    feeds_y = []
    dnormed[0].append(pass_on(order, *dnormed[0], lead=0))
    feeds_y.append(pass_on(order, *feeds[0], lead=1))
    lefts = [
        [piece for r in every_row for piece in ((normed_keeps[r], None), (normed_recvs[r], None))],
        [piece for r in every_row for piece in ((out_grad, r), grad_y[r], (grad_core, r), grad_both[r])],
    ]
    earlier = [(hiddens[r], dgates[r], dups[r]) for r in range(last_row)]
    dn_keep, ff_keep, sends, *parts = feed_last(order, place, lefts, earlier, gate_t, up_t, w_down, (0, 1, 0))
    received = over_core(sends)
    dnormed.append([dn_keep, received])
    feeds.append([ff_keep, received])
    down_scatter, gate_scatter = Scatter(0, parts[:2]), Scatter(1, parts[2:4], last=True)

    dmiddles, dbranches, norm2_sums, douts = [], [], [], []
    def back_to_heads(row):
        dmiddle, dbranch, norm2_sum, dout_own, dout_core, dout_y = branch_backward(
            order, row, *dnormed[row], middles[row], out_grad, gain_two, out_parts
        )
        dmiddles.append(dmiddle)
        dbranches.append(dbranch)
        norm2_sums.append(norm2_sum)
        return dout_own, dout_core, over_y(dout_y)

    def spread(dout_own, dout_core, dout_y):
        (dout_y,) = fence(order, dout_y)
        douts.append((dout_own, dout_y, over_core(jnp.stack([dout_core, dout_y[1]]))))

    dqkvs, norm1_sums, inner, band_grads, far_grads = [], [], [], [], []

    def attend_back(row):
        dqkv, dn_keep, dn_send, band_grad, far_grad, norm1_sum = attention_backward(
            order, row, place, seg_lengths, qkvs[row], douts[row], logsums[row], band, far,
            weight_t, normed_one[row],
        )
        band_grads.append(band_grad)
        far_grads.append(far_grad)
        norm1_sums.append(norm1_sum)
        dqkvs.append(dqkv)
        inner.append([dn_keep, over_core(dn_send)])

    going = back_to_heads(0)
    for row in range(1, rows):
        dnormed[row].append(pass_on(order, *dnormed[row], lead=0))
    spread(*going)
    for row in range(1, rows):
        feeds_y.append(pass_on(order, *feeds[row], lead=1))
    attend_back(0)
    up_scatter = Scatter(0, [parts[4], *fence(order, parts[5])])
    order.after(feeds_y[0])
    going = back_to_heads(1)
    order.after(inner[0][1])
    halve(order, place, down_scatter, gate_scatter)
    order.after(feeds_y[1])
    out_keep, out_send = outproj_grad(order, [part for group in attended for part in group], dbranches)
    out_recv = over_core(out_send)
    spread(*going)
    pause(order)
    out_from_y = outproj_pass(order, out_keep, out_recv)
    attend_back(1)
    small = small_gradients(
        order, place, heads, buckets, gain_one, norm1_sums, norm2_sums, band_grads, far_grads
    )
    rounds = small_rounds(order, small)
    next(rounds)
    halve(order, place, up_scatter)
    (attention_parts,) = gradient(
        order,
        "projection_gradient",
        place,
        [[(normed_one[r], None)] for r in every_row],
        [dqkvs],
        [([(0, slice(0, 3 * head_width)), (1, slice(0, head_width))], 0)],
        (out_keep, out_recv, out_from_y),
    )
    attention_scatter = Scatter(0, attention_parts, widths=[head_width] * 4)
    order.after(down_scatter.parts[1], gate_scatter.parts[1])
    next(rounds)
    inner_y = pass_rows(order, inner)
    halve(order, place, up_scatter)
    while up_scatter.bits:
        halve(order, place, up_scatter)
    block_out = block_output(order, middles, feeds, feeds_y)
    halve(order, place, attention_scatter)
    next(rounds)
    while down_scatter.bits:
        halve(order, place, down_scatter, gate_scatter)
    while attention_scatter.bits:
        halve(order, place, attention_scatter)
    next(rounds)
    input_grad = input_gradient(order, dmiddles, inner, inner_y, block_input, gain_one)
    next(rounds)
    up_out, down_out, gate_out = finish(order, up_scatter, down_scatter, gate_scatter)
    small = None
    while small is None:
        small = next(rounds)
    query_out, key_out, value_out, outproj_out = finish(order, attention_scatter)
    lines = width // 128
    bias_out = small[2 * lines :, : lax.axis_size("tensor")].reshape(heads, buckets, -1)
    bias_out = jnp.transpose(bias_out, (1, 2, 0)).reshape(rel_bias.shape)
    return (
        block_out,
        input_grad,
        small[:lines].reshape(width),
        small[lines : 2 * lines].reshape(width),
        bias_out,
        query_out,
        key_out,
        value_out,
        outproj_out.T,
        gate_out,
        up_out,
        down_out.T,
    )


def solution(mesh):
    in_specs = (
        P("dp", "tensor", None),
        P("dp", "tensor", None),
        P("dp", None),
        P(),
        P(),
        P(),
        P(None, "tensor"),
        P(None, "tensor"),
        P(None, "tensor"),
        P("tensor", None),
        P(None, "tensor"),
        P(None, "tensor"),
        P("tensor", None),
    )
    out_specs = (
        P("dp", "tensor", None),
        P("dp", "tensor", None),
        P(),
        P(),
        P(),
        P("dp", "tensor"),
        P("dp", "tensor"),
        P("dp", "tensor"),
        P("tensor", "dp"),
        P("dp", "tensor"),
        P("dp", "tensor"),
        P("tensor", "dp"),
    )
    return jax.shard_map(
        per_device, mesh=mesh, in_specs=in_specs, out_specs=out_specs, check_vma=False
    )
```

```python
import functools

import jax
import jax.numpy as jnp
import numpy as np
from jax import lax
from jax.experimental import pallas as pl
from jax.experimental.pallas import tpu as pltpu
from jax.sharding import PartitionSpec as P

DK = 64
QUERY_BLOCK = 256
REACH = 128
LANES = 64
MIB = 2**20

bucket_edges = (12, 16, 23, 32, 46, 64, 91)
masked_score = -1000000000.0
epsilon = 1e-06
gelu_scale = float(np.sqrt(2 / np.pi))
gelu_cubic = 0.044715
bf16 = jnp.bfloat16
f32 = jnp.float32

across_y = ((0, 2), (2, 0), (1, 3), (3, 1))
across_core = ((0, 1), (1, 0), (2, 3), (3, 2))
across_both = ((0, 3), (3, 0), (1, 2), (2, 1))


def dot_nn(left, right):
    return lax.dot_general(left, right, (((1,), (0,)), ((), ())), preferred_element_type=f32)


def dot_nt(left, right):
    return lax.dot_general(left, right, (((1,), (1,)), ((), ())), preferred_element_type=f32)


def dot_tn(left, right):
    return lax.dot_general(left, right, (((0,), (0,)), ((), ())), preferred_element_type=f32)


def over_y(array):
    return lax.ppermute(array, "tensor", across_y)


def over_core(array):
    return lax.ppermute(array, "tensor", across_core)


def over_both(array):
    return lax.ppermute(array, "tensor", across_both)


smem = pl.BlockSpec(memory_space=pltpu.SMEM)
vmem = pl.BlockSpec(memory_space=pltpu.VMEM)
anywhere = pl.BlockSpec(memory_space=pl.ANY)


def piece_of(array, lead):
    return vmem if lead is None else row_of(lead, array.shape)


def row_of(row, shape):
    return pl.BlockSpec((1,) + shape[1:], lambda *_: (row, 0, 0))


def placed(shape, kind, space=None):
    return jax.ShapeDtypeStruct(shape, kind) if space is None else space(shape, kind)


class Order:
    def __init__(self):
        self.last = []

    def after(self, *arrays):
        self.last = self.last + list(arrays)

    def call(self, kernel, name, inputs, in_specs, outputs, room, scratch=(), out_specs=None, grid=(1,), aliases=None):
        count, extra = len(inputs), len(self.last)

        def body(*refs):
            kernel(*refs[:count], *refs[count + extra :])

        results = pl.pallas_call(
            body,
            grid=grid,
            in_specs=list(in_specs) + [anywhere] * extra,
            out_specs=out_specs or [vmem] * len(outputs),
            out_shape=[placed(*output) for output in outputs],
            scratch_shapes=scratch,
            input_output_aliases=aliases or {},
            compiler_params=pltpu.CompilerParams(vmem_limit_bytes=room * MIB),
            cost_estimate=pl.CostEstimate(flops=10**13, bytes_accessed=1024, transcendentals=0),
            name=name,
        )(*inputs, *self.last)
        self.last = [results[0]]
        return results


def norm_factor(rows):
    return lax.rsqrt(jnp.mean(rows * rows, axis=-1, keepdims=True) + epsilon)


def norm_backward(dnormed, rows, gain):
    factor = norm_factor(rows)
    scaled = dnormed * gain
    return factor * (scaled - rows * factor * factor * jnp.mean(scaled * rows, axis=-1, keepdims=True))


def project_kernel(own, other_y, other_core, other_both, gain, weight_t, normed, qkv):
    count = own.shape[1]
    for index, piece in enumerate((own, other_y, other_core, other_both)):
        rows = piece[...].reshape(own.shape[1:]).astype(f32)
        result = (rows * norm_factor(rows) * gain[...]).astype(bf16)
        at = slice(index * count, (index + 1) * count)
        normed[at, :] = result
        qkv[at, :] = dot_nt(result, weight_t[...]).astype(bf16)


def project(order, pieces, gain, weight_t):
    count, width = pieces[0][0].shape[1:]
    return order.call(
        project_kernel,
        "normed_projections",
        (*[array for array, _ in pieces], gain, weight_t),
        [piece_of(*piece) for piece in pieces] + [vmem, vmem],
        [((4 * count, width), bf16), ((4 * count, weight_t.shape[0]), bf16)],
        36,
    )


def bucket_of(offset, buckets):
    magnitude = jnp.abs(offset)
    larger = sum(((magnitude >= edge).astype(jnp.int32) for edge in bucket_edges))
    exact = buckets // 4
    inside = jnp.where(magnitude < exact, magnitude, exact + larger)
    return inside + jnp.where(offset > 0, buckets // 2, 0)


def band_buckets(buckets):
    key = jnp.arange(QUERY_BLOCK + 2 * REACH, dtype=jnp.int32) - REACH
    query = jnp.arange(QUERY_BLOCK, dtype=jnp.int32)
    return bucket_of(key[:, None] - query[None, :], buckets)


def bias_parts(bias, length):
    buckets = bias.shape[0]
    index = band_buckets(buckets)
    wide = bias.astype(f32)
    band = jnp.zeros((bias.shape[1],) + index.shape, f32)
    for bucket in range(buckets):
        band = jnp.where((index == bucket)[None], wide[bucket][:, None, None], band)
    key = jnp.arange(length, dtype=jnp.int32)[:, None]
    block = jnp.arange(LANES, dtype=jnp.int32)[None]
    used = block < length // QUERY_BLOCK
    before = (key < block * QUERY_BLOCK - REACH) & used
    after = (key >= (block + 1) * QUERY_BLOCK + REACH) & used
    far_before = bias[buckets // 2 - 1][:, None, None]
    far_after = bias[buckets - 1][:, None, None]
    far = jnp.where(before[None], far_before, jnp.where(after[None], far_after, jnp.zeros((), bias.dtype)))
    return band, far


def near_keys(block, length):
    low = max(0, block * QUERY_BLOCK - REACH)
    high = min(length, (block + 1) * QUERY_BLOCK + REACH)
    return low, high, low - (block * QUERY_BLOCK - REACH)


def segment_of(position, lengths, row):
    end = jnp.int32(0)
    segment = jnp.zeros(position.shape, jnp.int32)
    for part in range(lengths.shape[1]):
        end = end + lengths[row, part]
        segment = segment + (position >= end).astype(jnp.int32)
    return segment


def fill_masks(lengths, row, masks):
    blocks, length, width = masks.shape
    key_segment = segment_of(lax.broadcasted_iota(jnp.int32, (length, width), 0), lengths, row)
    for block in range(blocks):
        at = lax.broadcasted_iota(jnp.int32, (1, width), 1) + block * width
        masks[block] = jnp.where(key_segment == segment_of(at, lengths, row), 0.0, masked_score)


def relative_block(place, block):
    along_y = jnp.bitwise_xor(place[0], block // 2)
    along_core = jnp.bitwise_xor(place[1], block % 2)
    return along_y + 2 * along_core


def rows_at(index):
    return pl.ds(pl.multiple_of(index * QUERY_BLOCK, QUERY_BLOCK), QUERY_BLOCK)


def block_scores(key_wide, query_wide, mask, band, head, block):
    length = key_wide.shape[0]
    scores = dot_nt(key_wide, query_wide) + mask
    low, high, start = near_keys(block, length)
    parts = []
    if low > 0:
        parts.append(scores[:low])
    parts.append(scores[low:high] + band[head, start : start + high - low])
    if high < length:
        parts.append(scores[high:])
    return jnp.concatenate(parts, axis=0)


def block_indicator(block):
    lane = lax.broadcasted_iota(jnp.int32, (QUERY_BLOCK, LANES), 1)
    return jnp.where(lane == block, 1.0, 0.0).astype(bf16)


def attention_forward_kernel(
    row, place, lengths, qkv, band, far, attended_keep, attended_send, logsum, masks, keys, values, attended
):
    length = qkv.shape[0]
    width = qkv.shape[1] // 3
    fill_masks(lengths, row, masks)
    blocks = length // QUERY_BLOCK
    order = [relative_block(place, block) for block in range(blocks)]
    for block in range(blocks):
        at = slice(block * QUERY_BLOCK, (block + 1) * QUERY_BLOCK)
        keys[at, :] = qkv[rows_at(order[block]), width : 2 * width]
        values[at, :] = qkv[rows_at(order[block]), 2 * width :]
    for head in range(width // DK):
        cols = slice(head * DK, (head + 1) * DK)
        key_wide = jnp.concatenate([keys[:, cols], far[head]], axis=1)
        for block in range(blocks):
            query_wide = jnp.concatenate([qkv[rows_at(order[block]), cols], block_indicator(block)], axis=1)
            scores = block_scores(key_wide, query_wide, masks[block], band, head, block)
            peak = jnp.max(scores, axis=0, keepdims=True)
            expo = jnp.exp(scores - peak)
            total = jnp.sum(expo, axis=0, keepdims=True)
            probs_low = (expo * (1.0 / total)).astype(bf16)
            logsum[head : head + 1, block * QUERY_BLOCK : (block + 1) * QUERY_BLOCK] = peak + jnp.log(total)
            result = dot_tn(probs_low, values[:, cols]).astype(bf16)
            attended[rows_at(order[block]), cols] = result
    attended_keep[...] = attended[: length // 2, :]
    attended_send[...] = attended[length // 2 :, :]


def attention_forward(order, row, place, lengths, qkv, band, far):
    length, width = qkv.shape[0], qkv.shape[1] // 3
    return order.call(
        functools.partial(attention_forward_kernel, row),
        "attention_forward",
        (place, lengths, qkv, band, far),
        [smem, smem, vmem, vmem, vmem],
        [((length // 2, width), bf16), ((length // 2, width), bf16), ((8, length), f32)],
        36,
        scratch=[
            pltpu.VMEM((length // QUERY_BLOCK, length, QUERY_BLOCK), f32),
            pltpu.VMEM((length, width), bf16),
            pltpu.VMEM((length, width), bf16),
            pltpu.VMEM((length, width), bf16),
        ],
    )


def attention_backward_kernel(
    row, place, lengths, qkv, dout_own, dout_y, dout_core, logsum, band, far, weight_t, normed,
    dqkv, dnormed_keep, dnormed_send, band_grad, far_grad, gain_sum,
    masks, keys, values, douts, queries_wide, probs_low, dscores,
):
    length = qkv.shape[0]
    width = qkv.shape[1] // 3
    fill_masks(lengths, row, masks)
    blocks = length // QUERY_BLOCK
    order = [relative_block(place, block) for block in range(blocks)]
    for block, piece in enumerate((dout_own[...], dout_y[0], dout_core[0], dout_core[1])):
        at = slice(block * QUERY_BLOCK, (block + 1) * QUERY_BLOCK)
        keys[at, :] = qkv[rows_at(order[block]), width : 2 * width]
        values[at, :] = qkv[rows_at(order[block]), 2 * width :]
        true_block = 2 * jnp.bitwise_xor(place[0], block % 2) + jnp.bitwise_xor(place[1], block // 2)
        douts[rows_at(true_block), :] = piece
    band_grad[...] = jnp.zeros_like(band_grad)
    far_grad[...] = jnp.zeros_like(far_grad)
    key_at = lax.broadcasted_iota(jnp.int32, (length, LANES), 0)
    block_at = lax.broadcasted_iota(jnp.int32, (length, LANES), 1)
    before = key_at < block_at * QUERY_BLOCK - REACH
    after = key_at >= (block_at + 1) * QUERY_BLOCK + REACH
    for head in range(width // DK):
        cols = slice(head * DK, (head + 1) * DK)
        slot = head % 2
        key_head = keys[:, cols]
        key_wide = jnp.concatenate([key_head, far[head]], axis=1)
        value_head = values[:, cols]
        for block in range(blocks):
            at = slice(block * QUERY_BLOCK, (block + 1) * QUERY_BLOCK)
            query_wide = jnp.concatenate([qkv[rows_at(order[block]), cols], block_indicator(block)], axis=1)
            queries_wide[slot, at, :] = query_wide
            scores = block_scores(key_wide, query_wide, masks[block], band, head, block)
            probs = jnp.exp(scores - logsum[head : head + 1, at])
            weighted = probs * dot_nt(value_head, douts[at, cols])
            inner = jnp.sum(weighted, axis=0, keepdims=True)
            low_dscores = (weighted - probs * inner).astype(bf16)
            probs_low[slot, :, at] = probs.astype(bf16)
            dscores[slot, :, at] = low_dscores
            low, high, start = near_keys(block, length)
            band_grad[head, start : start + high - low] += low_dscores[low:high].astype(f32)
        dvalue = dot_nn(probs_low[slot], douts[:, cols])
        dkey_wide = dot_nn(dscores[slot], queries_wide[slot])
        dquery = dot_nn(key_head.T, dscores[slot]).T
        for block in range(blocks):
            at = slice(block * QUERY_BLOCK, (block + 1) * QUERY_BLOCK)
            for index, part in enumerate((dquery, dkey_wide[:, :DK], dvalue)):
                part_cols = slice(index * width + head * DK, index * width + (head + 1) * DK)
                dqkv[rows_at(order[block]), part_cols] = part[at].astype(bf16)
        sums = dkey_wide[:, DK:]
        far_grad[head : head + 1, :] += jnp.concatenate(
            [
                jnp.sum(jnp.where(before, sums, 0.0), axis=0, keepdims=True),
                jnp.sum(jnp.where(after, sums, 0.0), axis=0, keepdims=True),
            ],
            axis=1,
        )
    total = jnp.zeros((1, normed.shape[1]), f32)
    for half, target in enumerate((dnormed_keep, dnormed_send)):
        for part in range(2):
            at = slice((2 * half + part) * QUERY_BLOCK, (2 * half + part + 1) * QUERY_BLOCK)
            dnormed = dot_nn(dqkv[at, :], weight_t[...])
            target[part * QUERY_BLOCK : (part + 1) * QUERY_BLOCK, :] = dnormed.astype(bf16)
            total = total + jnp.sum(dnormed * normed[at, :].astype(f32), axis=0, keepdims=True)
    gain_sum[...] = total


def attention_backward(order, row, place, lengths, qkv, douts, logsum, band, far, weight_t, normed):
    length, width = qkv.shape[0], qkv.shape[1] // 3
    half = ((length // 2, normed.shape[1]), bf16)
    return order.call(
        functools.partial(attention_backward_kernel, row),
        "attention_backward",
        (place, lengths, qkv, *douts, logsum, band, far, weight_t, normed),
        [smem, smem] + [vmem] * 9,
        [(qkv.shape, bf16, pltpu.HBM), half, half, (band.shape, f32), ((8, 2 * LANES), f32)]
        + [((1, normed.shape[1]), f32)],
        52,
        scratch=[pltpu.VMEM((length // QUERY_BLOCK, length, QUERY_BLOCK), f32)]
        + [pltpu.VMEM((length, width), bf16)] * 3
        + [pltpu.VMEM((2, length, DK + LANES), bf16)]
        + [pltpu.VMEM((2, length, length), bf16)] * 2,
    )


def branch_kernel(heads_0, heads_1, heads_2, heads_3, out_0, out_1, out_2, out_3, own, other_y, gain, middle, normed):
    count = own.shape[1]
    for index, piece in enumerate((own, other_y)):
        here = slice(index * count, (index + 1) * count)
        there = slice((1 - index) * count, (2 - index) * count)
        branch = (
            dot_nn(heads_0[here, :], out_0[...])
            + dot_nn(heads_1[here, :], out_1[...])
            + dot_nn(heads_2[there, :], out_2[...])
            + dot_nn(heads_3[there, :], out_3[...])
        )
        rows = piece[...].reshape(branch.shape).astype(f32) + branch
        if index == 0:
            middle[...] = rows
        normed[here, :] = (rows * norm_factor(rows) * gain[...]).astype(bf16)


def attention_branch(order, heads, out_parts, own, other_y, gain):
    count, width = own[0].shape[1:]
    return order.call(
        branch_kernel,
        "attention_branch",
        (*heads, *out_parts, own[0], other_y[0], gain),
        [vmem] * 8 + [piece_of(*own), piece_of(*other_y), vmem],
        [((count, width), f32), ((2 * count, width), bf16)],
        28,
    )


def branch_backward_kernel(
    keep, received, from_y, middle, out_grad, gain, out_0, out_1, out_2, out_3,
    dmiddle, dbranch, gain_sum, douts_own, douts_core, douts_y,
):
    dnormed = summed(keep, received, from_y)
    rows = middle[...]
    result = out_grad[0].astype(f32) + norm_backward(dnormed, rows, gain[...])
    dmiddle[...] = result
    low = result.astype(bf16)
    dbranch[...] = low
    gain_sum[...] = jnp.sum(dnormed * rows * norm_factor(rows), axis=0, keepdims=True)
    douts_own[...] = dot_nt(low, out_0[...]).astype(bf16)
    douts_core[...] = dot_nt(low, out_1[...]).astype(bf16)
    douts_y[0] = dot_nt(low, out_2[...]).astype(bf16)
    douts_y[1] = dot_nt(low, out_3[...]).astype(bf16)


def branch_backward(order, row, keep, received, from_y, middle, out_grad, gain, out_parts):
    count, width = middle.shape
    first = pl.BlockSpec((count, width), lambda *_: (0, 0))
    return order.call(
        branch_backward_kernel,
        "branch_backward",
        (keep, received, from_y, middle, out_grad, gain, *out_parts),
        [first, pl.BlockSpec((1, count, width), lambda *_: (0, 0, 0)), vmem, vmem, row_of(row, out_grad.shape)]
        + [vmem] * 5,
        [((count, width), f32), ((count, width), bf16), ((1, width), f32)]
        + [((count, out_parts[0].shape[0]), bf16)] * 2
        + [((2, count, out_parts[0].shape[0]), bf16)],
        24,
    )


def outproj_grad_kernel(rows, *refs):
    heads, branches, (keep, send) = refs[: 4 * rows], refs[4 * rows : 5 * rows], refs[5 * rows :]
    count = branches[0].shape[0]
    for index in range(4):
        total = None
        for row in range(rows):
            at = slice((index // 2) * count, (index // 2 + 1) * count)
            part = dot_tn(heads[4 * row + index][at, :], branches[row][...])
            total = part if total is None else total + part
        target = keep if index % 2 == 0 else send
        target[index // 2] = total.astype(bf16)


def outproj_grad(order, heads, branches):
    rows, width, cols = len(branches), branches[0].shape[1], heads[0].shape[1]
    return order.call(
        functools.partial(outproj_grad_kernel, rows),
        "outproj_gradient",
        (*heads, *branches),
        [vmem] * (5 * rows),
        [((2, cols, width), bf16)] * 2,
        24,
    )


def feed_kernel(chunk, blocks, leads, normed_keep, normed_recv, *refs):
    count = len(blocks)
    grads_hbm, (gate_hbm, up_hbm, down_hbm), refs = refs[:count], refs[count : count + 3], refs[count + 3 :]
    refs = refs[-12:]
    hidden_ref, dgate_ref, dup_ref, dnormed_keep, feed_keep, sends = refs[:6]
    gate_t, up_t, down, grads, weight_sem, grad_sem = refs[6:]
    step = pl.program_id(0)
    units = down.shape[0]
    chunks = [slice(start, min(units, start + chunk)) for start in range(0, units, chunk)]
    kept = sum(block < 2 for block in blocks)

    def weight_copies(index):
        at = pl.ds(chunks[index].start, chunks[index].stop - chunks[index].start)
        pairs = ((gate_hbm, gate_t), (up_hbm, up_t), (down_hbm, down))
        return [
            pltpu.make_async_copy(source.at[at], target.at[at], weight_sem.at[index, which])
            for which, (source, target) in enumerate(pairs)
        ]

    def grad_copy(index):
        source = grads_hbm[index] if leads[index] is None else grads_hbm[index].at[leads[index]]
        return pltpu.make_async_copy(source, grads.at[index], grad_sem.at[index])

    def work(first):
        normed = jnp.where(step < kept, normed_keep[...], normed_recv[...])
        grad = grads[step]
        for index, at in enumerate(chunks):
            if first:
                for copy in weight_copies(index):
                    copy.wait()
            values = gated_products(normed, grad, gate_t[at, :], up_t[at, :], down[at, :])
            hidden_ref[:, at], dgate_ref[:, at], dup_ref[:, at] = values
        for ref in (dgate_ref, dup_ref):
            ref[:, units:] = jnp.zeros((ref.shape[0], ref.shape[1] - units), bf16)
        dnormed = dot_nn(dgate_ref[:, :units], gate_t[...]) + dot_nn(dup_ref[:, :units], up_t[...])
        dnormed = dnormed.astype(bf16)
        feed = dot_nn(hidden_ref[...], down[...]).astype(bf16)

        @pl.when(step < kept)
        def _():
            dnormed_keep[...] = dnormed
            feed_keep[...] = feed

        @pl.when(step >= kept)
        def _():
            sends[0] = dnormed
            sends[1] = feed

    @pl.when(step == 0)
    def _():
        for index in range(len(chunks)):
            for copy in weight_copies(index):
                copy.start()
            if index == 0:
                grad_copy(0).start()
        for index in range(1, count):
            grad_copy(index).start()
        grad_copy(0).wait()
        work(True)

    @pl.when(step > 0)
    def _():
        for index in range(1, count):
            pl.when(step == index)(grad_copy(index).wait)
        work(False)


def feed_forward(order, normed_keep, normed_recv, blocks, grads, gate_t, up_t, down, before=()):
    units, width = down.shape
    length = 2 * normed_keep.shape[0]
    count = length // 4
    if len(blocks) == 4:
        kept_at, sent_at, at = (lambda s: jnp.minimum(s, 1)), (lambda s: jnp.maximum(s - 2, 0)), (lambda s: s)
    else:
        low, high = blocks
        kept_at = sent_at = lambda s: low
        at = lambda s: low + s * (high - low)
    first = pl.BlockSpec((count, width), lambda step: (kept_at(step), 0))
    last = pl.BlockSpec((count, width), lambda step: (sent_at(step), 0))
    pair = pl.BlockSpec((2, count, width), lambda step: (0, sent_at(step), 0))
    each = pl.BlockSpec((count, units), lambda step: (at(step), 0))
    wide = -(-units // 128) * 128
    padded = pl.BlockSpec((count, wide), lambda step: (at(step), 0))
    half = ((length // 2, width), bf16)
    chunk = 256
    inputs = 5 + len(grads)
    return order.call(
        functools.partial(feed_kernel, chunk, blocks, [lead for _, lead in grads]),
        "feed_forward",
        (normed_keep, normed_recv, *[array for array, _ in grads], gate_t, up_t, down, *before),
        [first, last] + [anywhere] * (inputs - 2 + len(before)),
        [((length, units), bf16, pltpu.HBM)]
        + [((length, wide), bf16, pltpu.HBM)] * 2
        + [half, half, ((2, length // 2, width), bf16)],
        44,
        out_specs=[each, padded, padded, first, first, pair],
        grid=(len(blocks),),
        scratch=[pltpu.VMEM((units, width), bf16)] * 3
        + [
            pltpu.VMEM((len(blocks), count, width), bf16),
            pltpu.SemaphoreType.DMA((-(-units // chunk), 3)),
            pltpu.SemaphoreType.DMA((len(blocks),)),
        ],
        aliases={inputs + index: index for index in range(len(before))},
    )


def gated_products(normed, grad, gate, up, down):
    gate = dot_nt(normed, gate)
    up = dot_nt(normed, up)
    dhidden = dot_nt(grad, down)
    square = gate * gate
    bend = jnp.tanh(gelu_scale * gate * (1.0 + gelu_cubic * square))
    half = 0.5 * (1.0 + bend)
    active = gate * half
    slope = half + (0.5 * gelu_scale) * gate * (1.0 - bend * bend) * (1.0 + (3 * gelu_cubic) * square)
    return (active * up).astype(bf16), (dhidden * up * slope).astype(bf16), (dhidden * active).astype(bf16)


def feed_last_kernel(chunk, pieces, rows, bits, place, *refs):
    count = sum(map(len, pieces))
    arrays, refs = refs[:count], refs[count:]
    earlier, refs = refs[: 3 * (rows - 1)], refs[3 * (rows - 1) :]
    (gate_hbm, up_hbm, down_hbm), refs = refs[:3], refs[3:]
    (dnormed_keep, feed_keep, sends), outs, refs = refs[:3], refs[3:9], refs[9:]
    gate_t, up_t, down, normed, grads, hidden, dgate, dup, stage = refs[:9]
    weight_sem, left_sem, right_sem, out_sem = refs[9:]
    step = pl.program_id(0)
    units = down.shape[0]
    chunks = [slice(start, min(units, start + chunk)) for start in range(0, units, chunk)]
    length = normed.shape[0] // rows
    block = length // 4
    base = (rows - 1) * length

    def weight_copies(index):
        at = pl.ds(chunks[index].start, chunks[index].stop - chunks[index].start)
        pairs = ((gate_hbm, gate_t), (up_hbm, up_t), (down_hbm, down))
        return [
            pltpu.make_async_copy(source.at[at], target.at[at], weight_sem.at[index, which])
            for which, (source, target) in enumerate(pairs)
        ]

    def left_copies(side):
        copies = []
        taken = sum(map(len, pieces[:side]))
        at = 0
        for index, lead in enumerate(pieces[side]):
            source = arrays[taken + index]
            source = source if lead is None else source.at[lead]
            copies.append(
                (
                    at,
                    pltpu.make_async_copy(
                        source, (normed, grads)[side].at[pl.ds(at, source.shape[0])], left_sem.at[side, index]
                    ),
                )
            )
            at += source.shape[0]
        return copies

    def right_copies():
        return [
            pltpu.make_async_copy(
                earlier[3 * row + which], target.at[pl.ds(row * length, length)], right_sem.at[row, which]
            )
            for row in range(rows - 1)
            for which, target in enumerate((hidden, dgate, dup))
        ]

    def work(first):
        at = pl.ds(pl.multiple_of(base + step * block, block), block)
        rows_normed, rows_grad = normed[at, :], grads[at, :]
        for index, part in enumerate(chunks):
            if first:
                for copy in weight_copies(index):
                    copy.wait()
            values = gated_products(rows_normed, rows_grad, gate_t[part, :], up_t[part, :], down[part, :])
            for target, value in zip((hidden, dgate, dup), values):
                target[at, part] = value
        dnormed = dot_nn(dgate[at, :units], gate_t[...]) + dot_nn(dup[at, :units], up_t[...])
        dnormed = dnormed.astype(bf16)
        feed = dot_nn(hidden[at, :], down[...]).astype(bf16)

        @pl.when(step < 2)
        def _():
            dnormed_keep[...] = dnormed
            feed_keep[...] = feed

        @pl.when(step >= 2)
        def _():
            sends[0] = dnormed
            sends[1] = feed

    def gradients():
        width = normed.shape[1]
        chunk_rows = outs[0].shape[1]
        tile = width // 2
        half_rows = tile // 2
        half_chunks = half_rows // chunk_rows
        sending = {}
        turn = 0
        for product, (left, right) in enumerate(((grads, hidden), (normed, dgate), (normed, dup))):
            bit = bits[product]
            for part in range(2):
                slot = turn % 2
                turn += 1
                for copy in sending.get(slot, ()):
                    copy.wait()
                for half in range(2):
                    cols = slice(part * tile + half * half_rows, part * tile + (half + 1) * half_rows)
                    value = dot_tn(left[:, cols], right[:, :units]).reshape(half_chunks, chunk_rows, units)
                    stage[slot, half * half_chunks : (half + 1) * half_chunks] = value.astype(bf16)
                sending[slot] = []
                for index in range(half_chunks):
                    low = index % (1 << bit)
                    first_chunk = (index - low) * 2 + low
                    for side, which in enumerate((place[2 + bit], 1 - place[2 + bit])):
                        copy = pltpu.make_async_copy(
                            stage.at[slot, first_chunk + which * (1 << bit)],
                            outs[2 * product + side].at[part * half_chunks + index],
                            out_sem.at[product, side, part * half_chunks + index],
                        )
                        copy.start()
                        sending[slot].append(copy)
        for copies in sending.values():
            for copy in copies:
                copy.wait()

    @pl.when(step == 0)
    def _():
        mine = [[copy for at, copy in left_copies(side) if at >= base] for side in range(2)]
        for index in range(len(chunks)):
            for copy in weight_copies(index):
                copy.start()
            if index == 0:
                mine[0][0].start()
                mine[1][0].start()
        for copies in mine:
            for copy in copies[1:]:
                copy.start()
        mine[0][0].wait()
        mine[1][0].wait()
        work(True)

    @pl.when(step == 1)
    def _():
        for side in range(2):
            for at, copy in left_copies(side):
                if at < base:
                    copy.start()
                elif at > base:
                    copy.wait()
        for copy in right_copies():
            copy.start()

    pl.when(step > 0)(lambda: work(False))

    @pl.when(step == 3)
    def _():
        for side in range(2):
            for at, copy in left_copies(side):
                if at < base:
                    copy.wait()
        for copy in right_copies():
            copy.wait()
        gradients()


def feed_last(order, place, lefts, earlier, gate_t, up_t, down, bits):
    units, width = down.shape
    size = lax.axis_size("dp")
    rows = len(earlier) + 1
    length = 4 * lefts[1][-1][0].shape[-2]
    count = length // 4
    first = pl.BlockSpec((count, width), lambda step: (jnp.minimum(step, 1), 0))
    pair = pl.BlockSpec((2, count, width), lambda step: (0, jnp.maximum(step - 2, 0), 0))
    half = ((length // 2, width), bf16)
    chunk = 256
    chunk_rows = width // size
    wide = -(-units // 128) * 128
    plan = [[lead for _, lead in side] for side in lefts]
    inputs = [array for side in lefts for array, _ in side] + [array for row in earlier for array in row]
    return order.call(
        functools.partial(feed_last_kernel, chunk, plan, rows, bits),
        "feed_forward_and_gradients",
        (place, *inputs, gate_t, up_t, down),
        [smem] + [anywhere] * (len(inputs) + 3),
        [half, half, ((2, length // 2, width), bf16)] + [((size // 2, chunk_rows, units), bf16)] * 6,
        50,
        out_specs=[first, first, pair] + [anywhere] * 6,
        grid=(4,),
        scratch=[pltpu.VMEM((units, width), bf16)] * 3
        + [pltpu.VMEM((rows * length, width), bf16)] * 2
        + [pltpu.VMEM((rows * length, units), bf16)]
        + [pltpu.VMEM((rows * length, wide), bf16)] * 2
        + [pltpu.VMEM((2, size // 2, chunk_rows, units), bf16)]
        + [
            pltpu.SemaphoreType.DMA((-(-units // chunk), 3)),
            pltpu.SemaphoreType.DMA((2, max(map(len, lefts)))),
            pltpu.SemaphoreType.DMA((max(rows - 1, 1), 3)),
            pltpu.SemaphoreType.DMA((3, 2, size // 2)),
        ],
    )


def halves(parts, stride, bit):
    count, rows, width = parts.shape
    pairs = parts.reshape(count // (2 * stride), 2, stride, rows, width)
    low, high = pairs[:, 0], pairs[:, 1]
    shape = (count // 2, rows, width)
    return jnp.where(bit == 0, low, high).reshape(shape), jnp.where(bit == 0, high, low).reshape(shape)


def gradient_kernel(groups, products, extra, cuts, place, *refs):
    rows = len(groups)
    extras, refs = refs[:extra], refs[extra:]
    pieces = sum(map(len, groups))
    lefts, refs = refs[:pieces], refs[pieces:]
    rights_hbm, refs = refs[: products * rows], refs[products * rows :]
    outs, refs = refs[: 2 * len(cuts)], refs[2 * len(cuts) :]
    stages, (left, right, left_sem, right_sem, out_sem) = refs[: len(cuts)], refs[len(cuts) :]
    steps = left.shape[0]
    tile = left.shape[2]
    length = right.shape[0] // rows
    cols = rights_hbm[0].shape[1]

    def left_copies(row, step):
        part = pl.ds(step * tile, tile)
        taken = sum(map(len, groups[:row]))
        copies = []
        at = row * length
        for index, lead in enumerate(groups[row]):
            source = lefts[taken + index]
            source = source if lead is None else source.at[lead]
            count = source.shape[0]
            copies.append(
                pltpu.make_async_copy(
                    source.at[:, part], left.at[step, pl.ds(at, count)], left_sem.at[step, row, index]
                )
            )
            at += count
        return copies

    def right_copy(product, row):
        index = product * rows + row
        return pltpu.make_async_copy(
            rights_hbm[index],
            right.at[pl.ds(row * length, length), pl.ds(product * cols, cols)],
            right_sem.at[index],
        )

    first = [[right_copy(product, row) for product in range(products)] + left_copies(row, 0) for row in range(rows)]
    later = [[copy for row in range(rows) for copy in left_copies(row, step)] for step in range(1, steps)]
    for group in first + later:
        for copy in group:
            copy.start()

    part_rows = tile // 2
    sending = []
    for step in range(steps):
        slot = step % 2
        sums = [None, None]
        spans = [slice(row * length, (row + 1) * length) for row in range(rows)] if step == 0 else [slice(None)]
        for span, group in zip(spans, first if step == 0 else [later[step - 1]]):
            for copy in group:
                copy.wait()
            for half in range(2):
                rows_at = slice(half * part_rows, (half + 1) * part_rows)
                part = dot_tn(left[step, span, rows_at], right[span, :])
                sums[half] = part if sums[half] is None else sums[half] + part
        for half in range(2):
            rows_at = slice(half * part_rows, (half + 1) * part_rows)
            total = sums[half]
            totals = [total[:, product * cols : (product + 1) * cols] for product in range(products)]
            if extra:
                turned_at = slice(step * tile + rows_at.start, step * tile + rows_at.stop)
                totals.append(sum(ref[0, :, turned_at].astype(f32) for ref in extras).T)
            for index, (parts, bit) in enumerate(cuts):
                chunk_rows = outs[2 * index].shape[1]
                count = part_rows // chunk_rows
                chunks = slice(half * count, (half + 1) * count)
                taken = [totals[which][:, where] for which, where in parts]
                value = taken[0] if len(taken) == 1 else jnp.concatenate(taken, axis=1)
                stages[index][slot, chunks] = value.reshape(count, chunk_rows, value.shape[1]).astype(bf16)
        for index, (parts, bit) in enumerate(cuts):
            chunk_rows = outs[2 * index].shape[1]
            mine = place[2 + bit]
            count = tile // chunk_rows // 2
            for chunk in range(count):
                low = chunk % (1 << bit)
                base = (chunk - low) * 2 + low
                for side, which in enumerate((mine, 1 - mine)):
                    copy = pltpu.make_async_copy(
                        stages[index].at[slot, base + which * (1 << bit)],
                        outs[2 * index + side].at[step * count + chunk],
                        out_sem.at[index, side, step * count + chunk],
                    )
                    copy.start()
                    sending.append(copy)
    for copy in sending:
        copy.wait()


def gradient(order, name, place, lefts, rights, cuts, extras=()):
    size = lax.axis_size("dp")
    length, cols = rights[0][0].shape
    width = lefts[0][0][0].shape[-1]
    steps = 2
    tile = width // steps
    chunk_rows = width // size
    pieces = [piece for group in lefts for piece in group]
    rows = len(lefts)
    flat = [array for group in rights for array in group]
    widths = [sum(at.stop - at.start for _, at in parts) for parts, _ in cuts]
    plan = [[lead for _, lead in group] for group in lefts]
    results = order.call(
        functools.partial(gradient_kernel, plan, len(rights), len(extras), cuts),
        name,
        (place, *extras, *[array for array, _ in pieces], *flat),
        [smem]
        + [pl.BlockSpec((1,) + extra.shape[1:], lambda *_: (0, 0, 0)) for extra in extras]
        + [anywhere] * (len(pieces) + len(flat)),
        [((size // 2, chunk_rows, w), bf16) for w in widths for _ in range(2)],
        52,
        out_specs=[anywhere] * (2 * len(widths)),
        scratch=[pltpu.VMEM((2, size // steps, chunk_rows, w), bf16) for w in widths]
        + [
            pltpu.VMEM((steps, rows * length, tile), bf16),
            pltpu.VMEM((rows * length, len(rights) * cols), bf16),
            pltpu.SemaphoreType.DMA((steps, rows, max(map(len, lefts)))),
            pltpu.SemaphoreType.DMA((len(flat),)),
            pltpu.SemaphoreType.DMA((len(cuts), 2, size // 2)),
        ],
    )
    return [results[2 * index : 2 * index + 2] for index in range(len(cuts))]


def exchange(sent, bit):
    return lax.ppermute(sent, "dp", [(i, i ^ (1 << bit)) for i in range(lax.axis_size("dp"))])


def halve_kernel(plans, place, *refs):
    count = sum(map(len, plans))
    inputs, outputs = refs[: 2 * count], refs[2 * count :]
    taken = 0
    for index, plan in enumerate(plans):
        keep_ref, send_ref = outputs[2 * index : 2 * index + 2]
        at = 0
        for stride, bit in plan:
            kept, received = inputs[2 * taken : 2 * taken + 2]
            taken += 1
            parts = kept[...].astype(f32) + received[...].astype(f32)
            keep, send = halves(parts, stride, place[2 + bit])
            cols = slice(at, at + parts.shape[2])
            keep_ref[:, :, cols] = keep.astype(bf16)
            send_ref[:, :, cols] = send.astype(bf16)
            at += parts.shape[2]


def total_kernel(*refs):
    count = 0
    while count < len(refs) and len(refs[count].shape) == 3:
        count += 1
    outs = list(refs[count:])
    for index in range(count // 2):
        total = refs[2 * index][0].astype(f32) + refs[2 * index + 1][0].astype(f32)
        at = 0
        while at < total.shape[1]:
            out = outs.pop(0)
            out[...] = total[:, at : at + out.shape[1]]
            at += out.shape[1]


class Scatter:
    def __init__(self, first, parts, last=False, widths=None):
        count = lax.axis_size("dp").bit_length() - 1
        self.bits = [first] + [bit for bit in range(count) if bit != first]
        if last:
            self.bits = self.bits[:1] + self.bits[2:] + self.bits[1:2]
        self.left = sorted(self.bits)
        self.widths = widths or [parts[0].shape[2]]
        self.send(*parts)

    def send(self, kept, sent):
        bit = self.bits.pop(0)
        self.left.remove(bit)
        self.parts = kept, exchange(sent, bit)


def halve(order, place, *groups):
    groups = [group if isinstance(group, tuple) else (group,) for group in groups]
    plans = [[(1 << scatter.left.index(scatter.bits[0]), scatter.bits[0]) for scatter in group] for group in groups]
    flat = [scatter for group in groups for scatter in group]
    shapes = [
        (group[0].parts[0].shape[0] // 2, group[0].parts[0].shape[1], sum(s.parts[0].shape[2] for s in group))
        for group in groups
    ]
    results = order.call(
        functools.partial(halve_kernel, plans),
        "halve",
        (place, *[part for scatter in flat for part in scatter.parts]),
        [smem] + [vmem] * (2 * len(flat)),
        [(shape, bf16) for shape in shapes for _ in range(2)],
        24,
    )
    for index, group in enumerate(groups):
        for other in group[1:]:
            assert group[0].left == other.left
            group[0].widths += other.widths
        group[0].send(*results[2 * index : 2 * index + 2])


def finish(order, *scatters):
    for scatter in scatters:
        assert not scatter.bits, scatter.bits
    return order.call(
        total_kernel,
        "gradient_output",
        [part for scatter in scatters for part in scatter.parts],
        [vmem] * (2 * len(scatters)),
        [
            ((scatter.parts[0].shape[1], width), f32, pltpu.HBM) for scatter in scatters for width in scatter.widths
        ],
        16,
    )


def attention_total_kernel(kept, received, query, key, value, out):
    total = kept[0].astype(f32) + received[0].astype(f32)
    cols = query.shape[1]
    for index, target in enumerate((query, key, value)):
        target[...] = total[:, index * cols : (index + 1) * cols]
    out[...] = total[:, 3 * cols :].T


def finish_attention(order, scatter):
    assert not scatter.bits, scatter.bits
    rows, cols = scatter.parts[0].shape[1], scatter.widths[0]
    return order.call(
        attention_total_kernel,
        "projection_outputs",
        scatter.parts,
        [vmem] * 2,
        [((rows, cols), f32, pltpu.HBM)] * 3 + [((cols, rows), f32, pltpu.HBM)],
        16,
    )


def pass_kernel(*refs):
    for keep, received, out in zip(refs[0::2], refs[1::2], refs[-(len(refs) // 3) :]):
        out[...] = (keep[...].reshape(out.shape).astype(f32) + received[...].reshape(out.shape).astype(f32)).astype(bf16)


def pass_on(order, keep, received, lead=None):
    count, width = keep.shape[0] // 2, keep.shape[1]
    second = pl.BlockSpec((count, width), lambda *_: (1, 0))
    other = second if lead is None else pl.BlockSpec((1, count, width), lambda *_: (lead, 1, 0))
    return over_y(
        order.call(pass_kernel, "pass_on", (keep, received), [second, other], [((count, width), bf16)], 8)[0]
    )


def pass_rows_kernel(*refs):
    out = refs[-1]
    for row in range(out.shape[0]):
        received = refs[2 * row + 1][...].reshape(out.shape[1:])
        out[row] = (refs[2 * row][...].astype(f32) + received.astype(f32)).astype(bf16)


def pass_rows(order, parts, lead=None):
    count, width = parts[0][0].shape[0] // 2, parts[0][0].shape[1]
    second = pl.BlockSpec((count, width), lambda *_: (1, 0))
    other = second if lead is None else pl.BlockSpec((1, count, width), lambda *_: (lead, 1, 0))
    return over_y(
        order.call(
            pass_rows_kernel,
            "pass_on",
            [array for pair in parts for array in pair],
            [second, other] * len(parts),
            [((len(parts), count, width), bf16)],
            12,
        )[0]
    )


def outproj_pass(order, keep, received):
    shape = keep.shape[1:]
    second = pl.BlockSpec((1,) + shape, lambda *_: (1, 0, 0))
    return over_y(order.call(pass_kernel, "pass_on", (keep, received), [second] * 2, [((1,) + shape, bf16)], 8)[0])


def join_kernel(bit, place, mine, received, out):
    count = mine.shape[0]
    which = place[2 + bit]
    out[pl.ds(pl.multiple_of(which * count, 16), count), :] = mine[...]
    out[pl.ds(pl.multiple_of((1 - which) * count, 16), count), :] = received[...]


def join(order, place, bit, mine, received):
    shape = (2 * mine.shape[0],) + mine.shape[1:]
    return order.call(
        functools.partial(join_kernel, bit), "join", (place, mine, received), [smem, vmem, vmem], [(shape, mine.dtype)], 8
    )[0]


def pause_kernel(out):
    out[...] = jnp.zeros_like(out)


def pause(order):
    order.call(pause_kernel, "pause", (), [], [((8, 128), f32)], 4)


def fence(order, *arrays):
    return order.call(
        lambda *_: None,
        "fence",
        arrays,
        [anywhere] * len(arrays),
        [(array.shape, array.dtype) for array in arrays],
        4,
        out_specs=[anywhere] * len(arrays),
        aliases={index: index for index in range(len(arrays))},
    )


def relay_kernel(source, target):
    target[...] = source[0] if len(source.shape) == 3 else source[...]


def relay(order, array, row=None):
    shape = array.shape if row is None else array.shape[1:]
    spec = vmem if row is None else row_of(row, array.shape)
    return order.call(relay_kernel, "relay", (array,), [spec], [(shape, array.dtype)], 8)[0]


def summed(keep, received, from_y):
    shape = keep.shape
    return sum(ref[...].reshape(shape).astype(f32) for ref in (keep, received, from_y))


def block_out_kernel(rows, *refs):
    out = refs[-1]
    for row in range(rows):
        middle, keep, received, from_y = refs[4 * row : 4 * row + 4]
        out[row] = middle[...] + summed(keep, received, from_y)


def block_output(order, middles, feeds, from_y):
    rows = len(from_y)
    count, width = from_y[0].shape
    first = pl.BlockSpec((count, width), lambda *_: (0, 0))
    other = pl.BlockSpec((1, count, width), lambda *_: (1, 0, 0))
    return order.call(
        functools.partial(block_out_kernel, rows),
        "block_output",
        [array for row in range(rows) for array in (middles[row], *feeds[row], from_y[row])],
        [vmem, first, other, vmem] * rows,
        [((rows, count, width), f32, pltpu.HBM)],
        30,
    )[0]


def input_grad_kernel(rows, from_y, inputs, gain, *refs):
    out = refs[-1]
    for row in range(rows):
        dmiddle, keep, received = refs[3 * row : 3 * row + 3]
        dnormed = summed(keep, received, from_y.at[row])
        out[row] = dmiddle[...] + norm_backward(dnormed, inputs[row].astype(f32), gain[...])


def input_gradient(order, dmiddles, inner, from_y, inputs, gain):
    rows, count, width = from_y.shape
    first = pl.BlockSpec((count, width), lambda *_: (0, 0))
    return order.call(
        functools.partial(input_grad_kernel, rows),
        "input_gradient",
        [from_y, inputs, gain] + [array for row in range(rows) for array in (dmiddles[row], *inner[row])],
        [vmem] * 3 + [vmem, first, first] * rows,
        [(from_y.shape, f32, pltpu.HBM)],
        36,
    )[0]


def small_kernel(heads, rows, buckets, place, gain, *refs):
    norms_one, norms_two, out = refs[:rows], refs[rows : 2 * rows], refs[-1]
    bands, fars = refs[2 * rows : 3 * rows], refs[3 * rows : 4 * rows]
    lines = gain.shape[1] // 128
    ones = sum(ref[...] for ref in norms_one) / gain[...]
    twos = sum(ref[...] for ref in norms_two)
    for index, vector in enumerate((ones, twos)):
        for line in range(lines):
            out[index * lines + line : index * lines + line + 1, :] = vector[:, line * 128 : (line + 1) * 128]
    side = REACH
    tiles = {}
    for key_block in range(bands[0].shape[1] // side):
        for query_block in range(bands[0].shape[2] // side):
            tiles.setdefault(key_block - 1 - query_block, []).append((key_block, query_block))
    row_at = lax.broadcasted_iota(jnp.int32, (side, side), 0)
    col_at = lax.broadcasted_iota(jnp.int32, (side, side), 1)
    lane = lax.broadcasted_iota(jnp.int32, (1, 128), 1)
    mine = lane == place[1] + 2 * place[0]
    which = lax.broadcasted_iota(jnp.int32, (buckets, 1), 0)
    for head in range(heads):
        sums = [jnp.zeros((1, side), f32) for _ in range(buckets)]
        for distance, blocks in tiles.items():
            grads = sum(
                band[head, key * side : (key + 1) * side, query * side : (query + 1) * side]
                for band in bands
                for key, query in blocks
            )
            index = bucket_of(row_at - col_at + distance * side, buckets)
            near = abs(distance) < 2
            for bucket in range(buckets):
                after = bucket >= buckets // 2
                if (near or bucket in (buckets // 2 - 1, buckets - 1)) and (distance == 0 or after == (distance > 0)):
                    sums[bucket] += jnp.sum(jnp.where(index == bucket, grads, 0.0), axis=0, keepdims=True)
        far = sum(ref[head : head + 1, :] for ref in fars)
        total = jnp.sum(jnp.concatenate(sums, axis=0), axis=1, keepdims=True)
        total = total + jnp.where(which == buckets // 2 - 1, jnp.sum(far[:, :LANES], axis=1, keepdims=True), 0.0)
        total = total + jnp.where(which == buckets - 1, jnp.sum(far[:, LANES:], axis=1, keepdims=True), 0.0)
        at = 2 * lines + head * buckets
        out[at : at + buckets, :] = jnp.where(mine, total, 0.0)


def small_gradients(order, place, heads, buckets, gain, norms_one, norms_two, bands, fars):
    lines = gain.shape[1] // 128
    rows = len(norms_one)
    return order.call(
        functools.partial(small_kernel, heads, rows, buckets),
        "small_gradients",
        (place, gain, *norms_one, *norms_two, *bands, *fars),
        [smem] + [vmem] * (1 + 4 * rows),
        [((2 * lines + heads * buckets, 128), f32)],
        16,
    )[0]


def add_kernel(*refs):
    refs[-1][...] = sum(ref[...] for ref in refs[:-1])


def add_all(order, arrays):
    return order.call(add_kernel, "small_sum", arrays, [vmem] * len(arrays), [(arrays[0].shape, f32)], 4)[0]


def small_rounds(order, vector):
    count = lax.axis_size("dp").bit_length() - 1
    sends = [over_core, over_y] + [functools.partial(exchange, bit=bit) for bit in range(count)]
    for send in sends:
        moved = send(vector)
        yield None
        vector = add_all(order, [vector, moved])
    yield vector


def per_device(
    block_input,
    out_grad,
    seg_lengths,
    norm1_gain,
    norm2_gain,
    rel_bias,
    w_query,
    w_key,
    w_value,
    w_out,
    w_gate,
    w_up,
    w_down,
):
    rows, count, width = block_input.shape
    length = 4 * count
    here = lax.axis_index("tensor")
    dp_bits = lax.axis_size("dp").bit_length() - 1
    dp_at = lax.axis_index("dp")
    place = jnp.stack([here // 2, here % 2] + [(dp_at >> bit) & 1 for bit in range(dp_bits)]).astype(jnp.int32)
    head_width = w_query.shape[1]
    heads = head_width // DK
    buckets = rel_bias.shape[0]
    gain_one = norm1_gain.astype(f32)[None]
    gain_two = norm2_gain.astype(f32)[None]
    first_head = here * heads
    weight_t = jnp.concatenate([w_query.T, w_key.T, w_value.T], axis=0)
    gate_t, up_t = w_gate.T, w_up.T

    order = Order()
    every_row = range(rows)
    last_row = rows - 1

    band, far = bias_parts(lax.dynamic_slice_in_dim(rel_bias, first_head, heads, 1), length)
    order.after(band, far, weight_t)
    first_y = over_y(block_input[0])
    input_core = over_core(block_input)
    grad_core = over_core(out_grad)
    out_core = over_core(w_out)
    input_y, input_both = [(first_y, None)], [(over_core(first_y), None)]
    grad_y, grad_both = [], []
    bits = (1, 2)
    quarter = w_out.shape[0] // 4
    out_at = (place[2 + bits[0]] + 2 * place[2 + bits[1]]) * quarter
    out_y = over_y(lax.dynamic_slice_in_dim(w_out, out_at, quarter, 0))
    order.after(input_core, grad_core, out_core)
    order.after(first_y)
    for row in range(1, rows):
        input_y.append((over_y(relay(order, block_input, row)), None))
    grad_y.append((over_y(relay(order, out_grad, 0)), None))
    out_y = (out_y, exchange(out_y, bits[0]))

    normed_one, qkvs, logsums, attended, middles = [], [], [], [], []
    normed_keeps, normed_recvs = [], []

    def second_norm(row):
        middle, normed_keep = attention_branch(
            order, attended[row], out_parts, (block_input, row), input_y[row], gain_two
        )
        middles.append(middle)
        normed_keeps.append(normed_keep)
        normed_recvs.append(over_core(normed_keep))

    def heads_arrived(row, other):
        (other,) = fence(order, other)
        attended[row][1], attended[row][3] = other, over_y(other)

    for row in every_row:
        if row == 0:
            out_y = join(order, place, bits[0], *out_y)
            out_y = (out_y, exchange(out_y, bits[1]))
        if row == 1:
            first_other = other
        normed, qkv = project(
            order, [(block_input, row), input_y[row], (input_core, row), input_both[row]], gain_one, weight_t
        )
        if row == 1:
            heads_arrived(0, first_other)
        keep, send, logsum = attention_forward(order, row, place, seg_lengths, qkv, band, far)
        normed_one.append(normed)
        qkvs.append(qkv)
        logsums.append(logsum)
        attended.append([keep, None, over_y(keep), None])
        if row == 0:
            (next_y,) = fence(order, input_y[1][0])
            input_y[1] = (next_y, None)
            input_both.append((over_core(next_y), None))
            out_y = join(order, place, bits[1], *out_y)
            out_parts = [w_out, out_core, out_y, over_core(out_y)]
            (send,) = fence(order, send)
        other = over_core(send)

    (first_grad,) = fence(order, grad_y[0][0])
    grad_y[0] = (first_grad, None)
    grad_both.append((over_core(first_grad), None))
    second_norm(0)
    heads_arrived(1, other)
    for row in range(1, rows):
        grad_y.append((over_y(relay(order, out_grad, row)), None))

    hiddens, dgates, dups, dnormed, feeds = [], [], [], [], []

    def feed(row):
        pieces = [(out_grad, row), grad_y[row], (grad_core, row), grad_both[row]]
        return feed_forward(
            order, normed_keeps[row], normed_recvs[row], (0, 1, 2, 3), pieces, gate_t, up_t, w_down
        )

    def fed(hidden, dgate, dup, dn_keep, ff_keep, sends):
        hiddens.append(hidden)
        dgates.append(dgate)
        dups.append(dup)
        received = over_core(sends)
        dnormed.append([dn_keep, received])
        feeds.append([ff_keep, received])

    fed(*feed(0))
    for row in range(1, rows):
        second_norm(row)
        grad_y[row] = (fence(order, grad_y[row][0])[0], None)
        grad_both.append((over_core(grad_y[row][0]), None))
    feeds_y = []
    dnormed[0].append(pass_on(order, *dnormed[0], lead=0))
    feeds_y.append(pass_on(order, *feeds[0], lead=1))
    lefts = [
        [piece for r in every_row for piece in ((normed_keeps[r], None), (normed_recvs[r], None))],
        [piece for r in every_row for piece in ((out_grad, r), grad_y[r], (grad_core, r), grad_both[r])],
    ]
    earlier = [(hiddens[r], dgates[r], dups[r]) for r in range(last_row)]
    dn_keep, ff_keep, sends, *parts = feed_last(order, place, lefts, earlier, gate_t, up_t, w_down, (0, 1, 0))
    received = over_core(sends)
    dnormed.append([dn_keep, received])
    feeds.append([ff_keep, received])
    down_scatter, gate_scatter = Scatter(0, parts[:2]), Scatter(1, parts[2:4], last=True)

    dmiddles, dbranches, norm2_sums, douts = [], [], [], []
    def back_to_heads(row):
        dmiddle, dbranch, norm2_sum, dout_own, dout_core, dout_y = branch_backward(
            order, row, *dnormed[row], middles[row], out_grad, gain_two, out_parts
        )
        dmiddles.append(dmiddle)
        dbranches.append(dbranch)
        norm2_sums.append(norm2_sum)
        return dout_own, dout_core, over_y(dout_y)

    def spread(dout_own, dout_core, dout_y):
        (dout_y,) = fence(order, dout_y)
        douts.append((dout_own, dout_y, over_core(jnp.stack([dout_core, dout_y[1]]))))

    dqkvs, norm1_sums, inner, band_grads, far_grads = [], [], [], [], []

    def attend_back(row):
        dqkv, dn_keep, dn_send, band_grad, far_grad, norm1_sum = attention_backward(
            order, row, place, seg_lengths, qkvs[row], douts[row], logsums[row], band, far,
            weight_t, normed_one[row],
        )
        band_grads.append(band_grad)
        far_grads.append(far_grad)
        norm1_sums.append(norm1_sum)
        dqkvs.append(dqkv)
        inner.append([dn_keep, over_core(dn_send)])

    going = back_to_heads(0)
    for row in range(1, rows):
        dnormed[row].append(pass_on(order, *dnormed[row], lead=0))
    for row in range(1, rows):
        feeds_y.append(pass_on(order, *feeds[row], lead=1))
    spread(*going)
    attend_back(0)
    up_scatter = Scatter(0, [parts[4], *fence(order, parts[5])])
    order.after(feeds_y[0])
    going = back_to_heads(1)
    order.after(inner[0][1])
    halve(order, place, down_scatter, gate_scatter)
    order.after(feeds_y[1])
    out_keep, out_send = outproj_grad(order, [part for group in attended for part in group], dbranches)
    out_recv = over_core(out_send)
    spread(*going)
    pause(order)
    out_from_y = outproj_pass(order, out_keep, out_recv)
    attend_back(1)
    small = small_gradients(
        order, place, heads, buckets, gain_one, norm1_sums, norm2_sums, band_grads, far_grads
    )
    rounds = small_rounds(order, small)
    next(rounds)
    halve(order, place, up_scatter)
    (attention_parts,) = gradient(
        order,
        "projection_gradient",
        place,
        [[(normed_one[r], None)] for r in every_row],
        [dqkvs],
        [([(0, slice(0, 3 * head_width)), (1, slice(0, head_width))], 0)],
        (out_keep, out_recv, out_from_y),
    )
    attention_scatter = Scatter(0, attention_parts, widths=[head_width] * 4)
    order.after(down_scatter.parts[1], gate_scatter.parts[1])
    next(rounds)
    inner_y = pass_rows(order, inner)
    halve(order, place, up_scatter)
    while up_scatter.bits:
        halve(order, place, up_scatter)
    block_out = block_output(order, middles, feeds, feeds_y)
    halve(order, place, attention_scatter)
    next(rounds)
    while down_scatter.bits:
        halve(order, place, down_scatter, gate_scatter)
    while attention_scatter.bits:
        halve(order, place, attention_scatter)
    next(rounds)
    input_grad = input_gradient(order, dmiddles, inner, inner_y, block_input, gain_one)
    next(rounds)
    up_out, down_out, gate_out = finish(order, up_scatter, down_scatter, gate_scatter)
    small = None
    while small is None:
        small = next(rounds)
    query_out, key_out, value_out, outproj_out = finish_attention(order, attention_scatter)
    lines = width // 128
    bias_out = small[2 * lines :, : lax.axis_size("tensor")].reshape(heads, buckets, -1)
    bias_out = jnp.transpose(bias_out, (1, 2, 0)).reshape(rel_bias.shape)
    return (
        block_out,
        input_grad,
        small[:lines].reshape(width),
        small[lines : 2 * lines].reshape(width),
        bias_out,
        query_out,
        key_out,
        value_out,
        outproj_out,
        gate_out,
        up_out,
        down_out.T,
    )


def solution(mesh):
    in_specs = (
        P("dp", "tensor", None),
        P("dp", "tensor", None),
        P("dp", None),
        P(),
        P(),
        P(),
        P(None, "tensor"),
        P(None, "tensor"),
        P(None, "tensor"),
        P("tensor", None),
        P(None, "tensor"),
        P(None, "tensor"),
        P("tensor", None),
    )
    out_specs = (
        P("dp", "tensor", None),
        P("dp", "tensor", None),
        P(),
        P(),
        P(),
        P("dp", "tensor"),
        P("dp", "tensor"),
        P("dp", "tensor"),
        P("tensor", "dp"),
        P("dp", "tensor"),
        P("dp", "tensor"),
        P("tensor", "dp"),
    )
    return jax.shard_map(
        per_device, mesh=mesh, in_specs=in_specs, out_specs=out_specs, check_vma=False
    )
```
